128 devices in a mesh: dp: 16 (over y_hi, x, core), seq: 8 (over z, y_lo).
Axes of the slice: x: 4, y: 4 (y_hi: 2, y_lo: 2; y = y_hi * 2 + y_lo), z: 4, core: 2. Of those that a mesh axis runs over, the one named last changes fastest.
Arguments:
- residual_in: bfloat16 [16, 1024, 768], P('dp', 'seq'), may hold values from -6 to 6
- cotangent: bfloat16 [16, 1024, 768], P('dp', 'seq'), may hold values from -6 to 6
- segments: int32 [16, 1024], P('dp'), may hold values from 0 to 2, as said below
- first_gain: bfloat16 [768], P('seq'), may hold values from 0.5 to 1.5
- first_shift: bfloat16 [768], P('seq'), may hold values from -1 to 1
- mixer_weight: bfloat16 [768, 2304], P('dp', 'seq'), may hold values from -0.21875 to 0.21875
- mixer_bias: bfloat16 [1536], P('seq'), may hold values from -1 to 1
- merge_weight: bfloat16 [768, 768], P('dp', 'seq'), may hold values from -1.25 to 1.25
- merge_bias: bfloat16 [768], P('seq'), may hold values from -1 to 1
- second_gain: bfloat16 [768], P('seq'), may hold values from 0.5 to 1.5
- second_shift: bfloat16 [768], P('seq'), may hold values from -1 to 1
- expand_weight: bfloat16 [768, 3072], P('dp', 'seq'), may hold values from -0.21875 to 0.21875
- expand_bias: bfloat16 [3072], P('seq'), may hold values from -1 to 1
- shrink_weight: bfloat16 [3072, 768], P('seq', 'dp'), may hold values from -0.109375 to 0.109375
- shrink_bias: bfloat16 [768], P('seq'), may hold values from -1 to 1
Outputs:
- hidden_out: bfloat16 [16, 1024, 768], P('dp', 'seq')
- grad_input: float32 [16, 1024, 768], P('dp', 'seq')
- grad_first_gain: float32 [768], P('seq')
- grad_first_shift: float32 [768], P('seq')
- grad_mixer_weight: float32 [768, 2304], P('dp', 'seq')
- grad_mixer_bias: float32 [1536], P('seq')
- grad_merge_weight: float32 [768, 768], P('dp', 'seq')
- grad_merge_bias: float32 [768], P('seq')
- grad_second_gain: float32 [768], P('seq')
- grad_second_shift: float32 [768], P('seq')
- grad_expand_weight: float32 [768, 3072], P('dp', 'seq')
- grad_expand_bias: float32 [3072], P('seq')
- grad_shrink_weight: float32 [3072, 768], P('seq', 'dp')
- grad_shrink_bias: float32 [768], P('seq')
The draws below stay inside these ranges and needn't reach their ends.
Inputs may be any that keep to these rules, and one draw needn't show every extreme that they name: `segments`: each sequence holds exactly three documents numbered 0, 1, 2 in order; document 1 begins within the first 128 tokens and ends within the last 128 tokens.
All inputs are finite; a program needn't handle non-finite values.
Results may differ from the reference program's by a relative error of at most 0.019.
Values may be sent and summed in bfloat16 or wider, within the bound.
A program may use at most 128 MiB of HBM per device.

```python
import jax
import jax.numpy as jnp
from jax import lax

D = 768
HEADS = 12
HEAD_DIM = 64
FF = 3072
LEN = 1024
TOK_LOCAL = 128
SEQS = 16


def draw_segments(key, part):
    key = jax.random.fold_in(key, 11)
    start_key, end_key = jax.random.split(key)
    opening = jax.random.randint(start_key, (SEQS, 1), 1, TOK_LOCAL)
    closing_step = jax.random.randint(end_key, (SEQS, 1), LEN - TOK_LOCAL + 1, LEN)
    places = jnp.arange(LEN, dtype=jnp.int32)[None, :]
    return (places >= opening).astype(jnp.int32) + (places >= closing_step).astype(jnp.int32)


def steps_of(own_key, extent, cuts, smallest, top_value):
    loudness = 1.0
    for axis_at, blocks in cuts:
        steps = jax.random.uniform(jax.random.fold_in(jax.random.fold_in(own_key, 6), axis_at), (blocks,), jnp.float32, smallest / len(cuts), top_value / len(cuts))
        loudness = loudness * jnp.repeat(jnp.exp(steps), extent[axis_at] // blocks).reshape((-1,) + (1,) * (len(extent) - 1 - axis_at))
    return loudness


def noise(own_key, dims, deviation, reach, cuts=(), held_as=jnp.bfloat16):
    values = jax.random.normal(own_key, dims, jnp.float32) * deviation
    if len(cuts) > 0:
        values = steps_of(own_key, dims, cuts, -0.22, 0.18) * values
    return jnp.clip(values, min=-reach, max=reach).astype(held_as)


def setup_inputs(seed: int = 0) -> dict:
    key_of = jax.random.split(jax.random.key(seed), 16)
    return {
        "residual_in": noise(key_of[0], (SEQS, LEN, D), 1.0, 6.0, ((0, 16), (1, 8))),
        "cotangent": noise(key_of[1], (SEQS, LEN, D), 1.0, 6.0, ((0, 16), (1, 8))),
        "segments": draw_segments(jax.random.fold_in(key_of[15], 71), 0),
        "first_gain": jnp.clip(1.0 + 0.1 * jax.random.normal(key_of[3], (D,), jnp.float32), 0.5, 1.5).astype(jnp.bfloat16),
        "first_shift": noise(key_of[4], (D,), 0.2, 1.0, ((0, 8),)),
        "mixer_weight": noise(key_of[5], (D, 3 * D), D ** -0.5, 0.21875, ((0, 16), (1, 8))),
        "mixer_bias": noise(key_of[6], (2 * D,), 0.2, 1.0, ((0, 8),)),
        "merge_weight": noise(key_of[7], (D, D), (D // 32) ** -0.5, 1.25, ((0, 16), (1, 8))),
        "merge_bias": noise(key_of[8], (D,), 0.2, 1.0, ((0, 8),)),
        "second_gain": jnp.clip(1.0 + 0.1 * jax.random.normal(key_of[9], (D,), jnp.float32), 0.5, 1.5).astype(jnp.bfloat16),
        "second_shift": noise(key_of[10], (D,), 0.2, 1.0, ((0, 8),)),
        "expand_weight": noise(key_of[11], (D, FF), D ** -0.5, 0.21875, ((0, 16), (1, 8))),
        "expand_bias": noise(key_of[12], (FF,), 0.2, 1.0, ((0, 8),)),
        "shrink_weight": noise(key_of[13], (FF, D), FF ** -0.5, 0.109375, ((0, 8), (1, 16))),
        "shrink_bias": noise(key_of[14], (D,), 0.2, 1.0, ((0, 8),)),
    }


EPS = 1e-05
NEG = -1e+30

@jax.custom_vjp
def low(v):
    return lax.optimization_barrier(v.astype(jnp.bfloat16)).astype(jnp.float32)

@jax.custom_vjp
def low_back(v):
    return v

def low_keep(v):
    return (low(v), None)

def low_pass(kept, grad):
    return (grad,)

def back_keep(v):
    return (v, None)

def back_low(kept, grad):
    return (low(grad),)
low.defvjp(low_keep, low_pass)
low_back.defvjp(back_keep, back_low)

def layer_norm(value, gain, shift):
    centre = lax.optimization_barrier(jnp.mean(value, axis=-1, keepdims=True))
    centred = value - centre
    spread = lax.optimization_barrier(jnp.mean(centred * centred, axis=-1, keepdims=True))
    return centred * lax.rsqrt(spread + EPS) * gain + shift

def gelu_tanh(value):
    inner = 0.7978845608028654 * (value + 0.044715 * value * value * value)
    return 0.5 * value * (1.0 + jnp.tanh(inner))

def matmul(left_operand, right_operand):
    return jnp.einsum('xrh,hk->xrk', left_operand, right_operand, precision=lax.Precision.HIGHEST)

def attend(query, keys, values, seg_row):
    length = query.shape[0]
    query_h = query.reshape(length, HEADS, HEAD_DIM)
    keys_h = keys.reshape(length, HEADS, HEAD_DIM)
    values_h = values.reshape(length, HEADS, HEAD_DIM)
    raw = jnp.einsum('qhd,khd->hqk', query_h, keys_h, precision=lax.Precision.HIGHEST) * HEAD_DIM ** (-0.5)
    scores = low_back(raw)
    places = jnp.arange(length)
    allowed = (places[:, None] >= places[None, :]) & (seg_row[:, None] == seg_row[None, :])
    masked = jnp.where(allowed[None], scores, NEG)
    top = lax.optimization_barrier(jnp.max(masked, axis=-1, keepdims=True))
    expo = jnp.exp(masked - top)
    probs = expo / lax.optimization_barrier(jnp.sum(expo, axis=-1, keepdims=True))
    weights = low(probs)
    mixed = jnp.einsum('hqk,khd->qhd', weights, values_h, precision=lax.Precision.HIGHEST)
    return mixed.reshape(length, HEADS * HEAD_DIM)

def reference(residual_in, cotangent, segments, first_gain, first_shift, mixer_weight, mixer_bias, merge_weight, merge_bias, second_gain, second_shift, expand_weight, expand_bias, shrink_weight, shrink_bias):
    params = tuple((p.astype(jnp.float32) for p in (first_gain, first_shift, mixer_weight, mixer_bias, merge_weight, merge_bias, second_gain, second_shift, expand_weight, expand_bias, shrink_weight, shrink_bias)))
    checked = jax.checkpoint(attend)

    def forward(hidden, gain_a, shift_a, w_mix, b_mix, merge_matrix, b_merge, gain_b, shift_b, w_expand, b_expand, w_shrink, b_shrink):
        first = low(layer_norm(hidden, gain_a, shift_a))
        zeros = jnp.zeros((D,), jnp.float32)
        full_bias = jnp.concatenate([b_mix[:D], zeros, b_mix[D:]])
        mixed = low(low_back(matmul(first, w_mix) + full_bias))
        query = mixed[..., :D]
        keys = mixed[..., D:2 * D]
        values = mixed[..., 2 * D:]
        attended = lax.map(lambda block: checked(*block), (query, keys, values, segments))
        attended = low(low_back(attended))
        branch = low_back(matmul(attended, merge_matrix) + b_merge)
        middle = hidden + branch
        second = low(layer_norm(middle, gain_b, shift_b))
        pre = low_back(matmul(second, w_expand) + b_expand)
        active = low(gelu_tanh(pre))
        return middle + matmul(active, w_shrink) + b_shrink
    result, pullback = jax.vjp(forward, residual_in.astype(jnp.float32), *params)
    grads = pullback(cotangent.astype(jnp.float32))
    return (result.astype(jnp.bfloat16), grads[0], grads[1], grads[2], grads[3], grads[4], grads[5], grads[6], grads[7], grads[8], grads[9], grads[10], grads[11], grads[12])
```

```python
import functools
import types

import jax
import jax.numpy as jnp
from jax import lax
from jax.experimental import pallas as pl
from jax.experimental.pallas import tpu as pltpu
from jax.sharding import PartitionSpec as P


D = 768
HD = 64
TOK = 128
SHARD = 384
EPS = 1e-05
NEG = -1e30
MESH = pl.DeviceIdType.MESH
BF = jnp.bfloat16
F32 = jnp.float32
ORDERS = (("x", "y", "z"), ("y", "z", "x"), ("z", "x", "y"))
FIRST_GAIN, FIRST_SHIFT, MIXER_BIAS, MERGE_BIAS, SECOND_GAIN, SECOND_SHIFT, SHRINK_BIAS, EXPAND_BIAS = 0, 1, 2, 4, 5, 6, 7, 8


def place_of():
    dp, seq = lax.axis_index("dp"), lax.axis_index("seq")
    return types.SimpleNamespace(
        x=lax.rem(lax.div(dp, 2), 4),
        yh=lax.div(dp, 8),
        yl=lax.rem(seq, 2),
        z=lax.div(seq, 2),
        c=lax.rem(dp, 2),
    )


def moved(at, **to):
    new = types.SimpleNamespace(**vars(at))
    for name, value in to.items():
        setattr(new, name, value)
    return new


def shifted(at, axis, d):
    d = d % 4
    if axis == "x":
        return moved(at, x=lax.rem(at.x + d, 4))
    if axis == "z":
        return moved(at, z=lax.rem(at.z + d, 4))
    y = lax.rem(at.yh * 2 + at.yl + d, 4)
    return moved(at, yh=lax.div(y, 2), yl=lax.rem(y, 2))


def device(at):
    return (at.yh * 8 + at.x * 2 + at.c, at.z * 2 + at.yl)


def nn(a, b):
    return jnp.dot(a, b, preferred_element_type=F32)


def nt(a, b):
    return lax.dot_general(a, b, (((1,), (1,)), ((), ())), preferred_element_type=F32)


def remote(src, dst, send, recv, to):
    return pltpu.make_async_remote_copy(
        src_ref=src, dst_ref=dst, send_sem=send, recv_sem=recv, device_id=device(to), device_id_type=MESH
    )


def part(ref, at, t, full, lead, core=True):
    every = slice(None)
    where = [every if "z" in full else at.z]
    where += [every, every] if "y" in full else [at.yl, at.yh]
    where += [every if "x" in full else at.x]
    if core:
        where += [at.c]
    return ref.at[tuple(lead) + tuple(where) + (pl.ds(16 * t, 16), every)]


def norm_parts(v):
    centred = v - jnp.mean(v, axis=-1, keepdims=True)
    rstd = lax.rsqrt(jnp.mean(centred * centred, axis=-1, keepdims=True) + EPS)
    return centred * rstd, rstd


def norm_back(dy, gain, normed, rstd):
    dn = dy * gain
    return rstd * (
        dn
        - jnp.mean(dn, axis=-1, keepdims=True)
        - normed * jnp.mean(dn * normed, axis=-1, keepdims=True)
    )


def col_sums(v):
    return jnp.sum(v.astype(F32), axis=0, keepdims=True)


def kernel(
    x_ref, cot_ref, seg_ref, wsh_ref, vec_ref,
    hidden_ref, gin_ref, gmix_ref, gmerge_ref, gexp_ref, gshr_ref, vout_ref,
    w, g, r0, rb1, rb2, rb3, vecs, segs, first_s, mix_s, q_send, kv_send, q_all, kv_all, kvt, lse_s,
    att_send, att_recv, att_s, mid_s, n2_s, sect_s, cott_s, mlp_s, dsec_s, dbr_s, fat_s,
    do_send, do_recv, dkv_s, dkv_sib, dkv_got, dq_send, dq_recv, dkv_send, dkv_recv, dmix_s, dfirst_s,
    vg, vr, vsum, vx,
    ag_ss, ag_rs, sib_ss, sib_rs, vec_ss, vec_rs, one_ss, one_rs, a2a_ss, a2a_rs, kvs_ss, kvs_rs,
    back_ss, back_rs, rs0_ss, rs0_rs, rs_ss, rs_rs, vred_ss, vred_rs, vx_ss, vx_rs, loc,
):
    me = place_of()
    sib = moved(me, c=1 - me.c)
    swap = moved(me, yl=me.c, c=me.yl)
    here = me.yl == me.c
    peers = [shifted(me, a, d) for a in "xyz" for d in (1, 2, 3)] + [sib]
    peers += [moved(shifted(me, "z", d), yl=1 - me.yl) for d in (1, 2, 3)]
    peers += [moved(shifted(me, "z", d), yl=1 - me.yl, c=1 - me.c) for d in range(4)]
    barrier = pltpu.get_barrier_semaphore()
    for p in peers:
        pl.semaphore_signal(barrier, inc=1, device_id=device(p), device_id_type=MESH)
    pl.semaphore_wait(barrier, len(peers))

    pending = []

    def start(copy):
        copy.start()
        pending.append(copy)

    GROUPS = ((0, 1), (1, 2))

    def lead(group):
        first, count = GROUPS[group]
        return (pl.ds(first, count),)

    def ag(group, t, stage, d):
        order = ORDERS[t]
        at = part(w, me, t, order[:stage], lead(group))
        sems = (ag_ss.at[group, t, stage, d - 1], ag_rs.at[group, t, stage, d - 1])
        return remote(at, at, *sems, shifted(me, order[stage], d))

    def ag_wait(group, t, stage, d):
        order = ORDERS[t]
        at = part(w, shifted(me, order[stage], -d), t, order[:stage], lead(group))
        sems = (ag_ss.at[group, t, stage, d - 1], ag_rs.at[group, t, stage, d - 1])
        remote(at, at, *sems, shifted(me, order[stage], d)).wait_recv()

    def hand(group, t, d, mine):
        order = ORDERS[t]
        at = shifted(me if mine else sib, order[2], -d)
        view = part(w, at, t, order[:2], lead(group))
        return remote(view, view, sib_ss.at[group, t, d], sib_rs.at[group, t, d], sib)

    def ag_start(group):
        for d in (1, 3, 2):
            for t in range(3):
                start(ag(group, t, 0, d))

    def ag_next(group, stage):
        for t in range(3):
            for d in (1, 3, 2):
                ag_wait(group, t, stage - 1, d)
            for d in (1, 3, 2):
                start(ag(group, t, stage, d))
            if stage == 2:
                start(hand(group, t, 0, True))

    def ag_finish(group):
        for d in (1, 3, 2):
            for t in range(3):
                ag_wait(group, t, 2, d)
                start(hand(group, t, d, True))
        for d in (0, 1, 3, 2):
            for t in range(3):
                hand(group, t, d, False).wait_recv()

    for a in range(3):
        w[a, me.z, me.yl, me.yh, me.x, me.c] = wsh_ref[a]
    ag_start(0)
    seq = me.z * 2 + me.yl
    vecs[seq] = vec_ref[...]
    seg_own = seg_ref[...].astype(F32)
    segs[0] = seg_own
    start(remote(segs.at[0], segs.at[1], one_ss.at[0], one_rs.at[0], sib))

    def seq_peer(k):
        at = shifted(me, "z", k // 2)
        return moved(at, yl=1 - me.yl) if k % 2 else at

    def seq_from(k):
        at = shifted(me, "z", -(k // 2))
        return moved(at, yl=1 - me.yl) if k % 2 else at

    for k in range(1, 8):
        start(remote(vecs.at[seq], vecs.at[seq], vec_ss.at[k - 1], vec_rs.at[k - 1], seq_peer(k)))
    for k in range(1, 8):
        src = seq_from(k)
        at = vecs.at[src.z * 2 + src.yl]
        remote(at, at, vec_ss.at[k - 1], vec_rs.at[k - 1], seq_peer(k)).wait_recv()

    def whole(row):
        return jnp.concatenate([vecs[s, row : row + 1, 0:96] for s in range(8)], axis=1).astype(F32)

    x_rows = x_ref[...].astype(F32)
    n1, rstd1 = norm_parts(x_rows)
    first = (n1 * whole(FIRST_GAIN) + whole(FIRST_SHIFT)).astype(BF)
    first_s[...] = first
    fat_s[:, 0:TOK] = first.astype(F32).T.astype(BF)
    cott_s[...] = cot_ref[...].astype(F32).T.astype(BF)
    ag_next(0, 1)
    ag_next(0, 2)
    ag_start(1)
    ag_finish(0)
    ag_next(1, 1)

    def unit_bias(u):
        if 8 <= u < 16:
            return jnp.zeros((1, 96), F32)
        j = u if u < 8 else u - 8
        row = MIXER_BIAS + j % 2
        return vecs[j // 2, row : row + 1, 0:96].astype(F32)

    for s in range(8):
        bias = jnp.concatenate([unit_bias(3 * s + k) for k in range(3)], axis=1)
        res = nn(first_s[...], w[0, s // 2, s % 2].reshape(D, SHARD))
        mix_s[:, 288 * s : 288 * s + 288] = (res[:, :288] + bias).astype(BF)
    for h in range(4):
        q = mix_s[:, 192 * h : 192 * h + 192] * jnp.asarray(0.125, BF)
        q_send[h] = jnp.concatenate([q, jnp.zeros((TOK, 64), BF)], axis=1)
        k = mix_s[:, D + 192 * h : D + 192 * h + 192]
        v = mix_s[:, 2 * D + 192 * h : 2 * D + 192 * h + 192]
        kv_send[h] = jnp.concatenate([k, v[:, 128:192], v[:, 0:128]], axis=1)

    def exchange(src_of, dst_of, kind, ss, rs, order=(1, 3, 2, 0)):
        for d in order:
            to = shifted(swap, "z", d)
            src, dst = src_of(to.z), dst_of(me.z)
            if d:
                start(remote(src, dst, ss.at[kind, d], rs.at[kind, d], to))
            else:
                exchange_one(src, dst, kind, ss, rs, to)

    def exchange_one(src, dst, kind, ss, rs, to):
        @pl.when(here)
        def _():
            pltpu.make_async_copy(src, dst, rs.at[kind, 0]).start()

        @pl.when(jnp.logical_not(here))
        def _():
            remote(src, dst, ss.at[kind, 0], rs.at[kind, 0], to).start()

    def exchange_wait(src_of, dst_of, kind, ss, rs, d):
        frm = shifted(me, "z", -d)
        to = shifted(swap, "z", d)
        src, dst = src_of(to.z), dst_of(frm.z)
        if d:
            remote(src, dst, ss.at[kind, d], rs.at[kind, d], to).wait_recv()
        else:

            @pl.when(here)
            def _():
                pltpu.make_async_copy(src, dst, rs.at[kind, 0]).wait()

            @pl.when(jnp.logical_not(here))
            def _():
                remote(src, dst, ss.at[kind, 0], rs.at[kind, 0], to).wait()

    def kv_src(z):
        return kv_send.at[z]

    def kv_dst(z):
        return kv_all.at[z, me.c]

    def kv_there(z):
        return kv_all.at[z, me.yl]

    def q_src(z):
        return q_send.at[z]

    def q_dst(z):
        return q_all.at[z]

    exchange(kv_src, kv_there, 0, a2a_ss, a2a_rs)
    exchange(q_src, q_dst, 1, a2a_ss, a2a_rs)
    kvs = []
    for d in (1, 3, 2, 0):
        exchange_wait(kv_src, kv_dst, 0, a2a_ss, a2a_rs, d)
        z = shifted(me, "z", -d).z
        copy = remote(kv_all.at[z, me.c], kv_all.at[z, me.c], kvs_ss.at[d], kvs_rs.at[d], sib)
        start(copy)
    for d in (1, 3, 2, 0):
        exchange_wait(q_src, q_dst, 1, a2a_ss, a2a_rs, d)
    for d in (1, 3, 2, 0):
        z = shifted(me, "z", -d).z
        at = kv_all.at[z, 1 - me.c]
        remote(at, at, kvs_ss.at[d], kvs_rs.at[d], sib).wait_recv()
    remote(segs.at[0], segs.at[1], one_ss.at[0], one_rs.at[0], sib).wait_recv()
    ag_next(1, 2)

    for b in range(8):
        kvt[:, TOK * b : TOK * b + TOK] = kv_all[b // 2, b % 2].astype(F32).T.astype(BF)
    seg = jnp.where(here, segs[0], segs[1])
    ones = (1, 1)
    begin1 = jnp.sum(jnp.where(seg < 0.5, 1.0, 0.0), axis=(0, 1), keepdims=True).astype(jnp.int32).reshape(ones)
    begin2 = jnp.sum(jnp.where(seg < 1.5, 1.0, 0.0), axis=(0, 1), keepdims=True).astype(jnp.int32).reshape(ones)
    lane = lax.broadcasted_iota(jnp.int32, (TOK, TOK), 1)

    def allowed_of(b):
        n = 256 * (b + 1)
        qpos = 256 * b + TOK * me.c + lax.broadcasted_iota(jnp.int32, (1, TOK), 1)
        low = jnp.where(qpos < begin1, 0, jnp.where(qpos < begin2, begin1, begin2))
        kpos = lax.broadcasted_iota(jnp.int32, (n, TOK), 0)
        return (kpos <= qpos) & (kpos >= low)

    def keys_of(b, h):
        n = 256 * (b + 1)
        at = slice(0, 128) if h < 2 else slice(128, 256)
        return kv_all[0 : b + 1, :, :, at].reshape(n, TOK)

    def values_of(b, h):
        n = 256 * (b + 1)
        at = slice(256, 384) if h < 2 else slice(128, 256)
        return kv_all[0 : b + 1, :, :, at].reshape(n, TOK)

    K_ROWS = (0, 64, 128)
    V_ROWS = (256, 320, 192)

    def half(v, upper):
        keep = lane >= 64 if upper else lane < 64
        return jnp.where(keep, v, jnp.zeros_like(v))

    def query_of(b, h):
        tile = q_all[b, :, 0:128] if h < 2 else q_all[b, :, 128:256]
        return half(tile, h == 1)

    def att_src(z):
        return att_send.at[z]

    def att_dst(z):
        return att_recv.at[z]

    for b in (3, 2, 1, 0):
        n = 256 * (b + 1)
        allowed = allowed_of(b)
        outs = []
        for h in range(3):
            scores = jnp.where(allowed, nt(keys_of(b, h), query_of(b, h)), NEG)
            top = jnp.max(scores, axis=0, keepdims=True)
            expo = jnp.exp(scores - top)
            total = jnp.sum(expo, axis=0, keepdims=True)
            lse_s[b, h : h + 1, :] = top + jnp.log(total)
            weights = (expo * (1.0 / total)).astype(BF)
            outs.append(nn(kvt[V_ROWS[h] : V_ROWS[h] + 64, 0:n], weights))
        outs.append(jnp.zeros((64, TOK), F32))
        both = jnp.concatenate(outs, axis=0)
        att_send[b] = both.T.astype(BF)
    exchange(att_src, att_dst, 0, back_ss, back_rs)
    for d in (1, 3, 2, 0):
        exchange_wait(att_src, att_dst, 0, back_ss, back_rs, d)
    for h in range(4):
        att_s[:, 192 * h : 192 * h + 192] = att_recv[h, :, 0:192]

    def merge_tile(s):
        return w[0, s // 2, s % 2, :, :, :, :, 256:384].reshape(D, TOK)

    branch = jnp.concatenate([nn(att_s[...], merge_tile(s))[:, 32:128] for s in range(8)], axis=1)
    middle = x_ref[...].astype(F32) + branch + whole(MERGE_BIAS)
    mid_s[...] = middle
    n2, rstd2 = norm_parts(middle)
    n2_s[...] = n2
    second = (n2 * whole(SECOND_GAIN) + whole(SECOND_SHIFT)).astype(BF)
    first_s[...] = second
    sect_s[...] = second.astype(F32).T.astype(BF)
    fat_s[:, TOK : 2 * TOK] = att_s[...].astype(F32).T.astype(BF)
    mlp_s[...] = jnp.zeros_like(mlp_s)
    dsec_s[...] = jnp.zeros_like(dsec_s)
    ag_finish(1)

    def rs0(a, z, yl):
        src = g.at[a, z, yl, :, :, 1 - me.c]
        s = z * 2 + yl
        return remote(src, r0.at[a, z, yl], rs0_ss.at[a, s], rs0_rs.at[a, s], sib)

    def units(s, _):
        z, yl = lax.div(s, 2), lax.rem(s, 2)
        rows = vecs[s].astype(F32)
        bias = jnp.concatenate([rows[EXPAND_BIAS + k : EXPAND_BIAS + k + 1] for k in range(3)], axis=1)
        expand = w[1, z, yl].reshape(D, SHARD)
        shrink = w[2, z, yl].reshape(D, SHARD)
        pre = nn(first_s[...], expand) + bias
        square = pre * pre
        tanh = jnp.tanh(0.7978845608028654 * (pre + 0.044715 * square * pre))
        active = (0.5 * pre * (1.0 + tanh)).astype(BF)
        slope = 0.5 * (1.0 + tanh) + 0.5 * pre * (1.0 - tanh * tanh) * (
            0.7978845608028654 * (1.0 + 0.134145 * square)
        )
        d_pre = (nn(cot_ref[...], shrink) * slope).astype(BF)
        mlp_s[...] += nt(active, shrink)
        dsec_s[...] += nt(d_pre, expand)
        sums = col_sums(d_pre)
        for k in range(3):
            vg[s, EXPAND_BIAS + k : EXPAND_BIAS + k + 1, :] = sums[:, TOK * k : TOK * k + TOK]
        blocks = (2, 4, 2, 48, SHARD)
        g[2, z, yl] = nn(cott_s[...], active).astype(BF).reshape(blocks)
        rs0(2, z, yl).start()
        g[1, z, yl] = nn(sect_s[...], d_pre).astype(BF).reshape(blocks)
        rs0(1, z, yl).start()
        return 0

    lax.fori_loop(0, 8, units, 0)
    hidden_ref[...] = (mid_s[...] + mlp_s[...] + whole(SHRINK_BIAS)).astype(BF)

    d_second = dsec_s[...]
    cot = cot_ref[...].astype(F32)
    d_middle = cot + norm_back(d_second, whole(SECOND_GAIN), n2_s[...], rstd2)
    mid_s[...] = d_middle
    d_branch = d_middle.astype(BF)
    dbr_s[...] = d_branch
    g_gain_b = col_sums(d_second * n2_s[...])
    g_shift_b = col_sums(d_second)
    g_b_shrink = col_sums(cot)
    g_b_merge = col_sums(d_branch)
    zeros32 = jnp.zeros((TOK, 32), BF)
    d_att = jnp.zeros((TOK, D), F32)
    for s in range(8):
        d_att += nt(jnp.concatenate([zeros32, dbr_s[:, 96 * s : 96 * s + 96]], axis=1), merge_tile(s))
    d_att = d_att.astype(BF)
    for h in range(4):
        o = d_att[:, 192 * h : 192 * h + 192]
        do_send[h] = jnp.concatenate([o[:, 0:128], jnp.zeros((TOK, 64), BF), o[:, 128:192]], axis=1)

    def do_src(z):
        return do_send.at[z]

    def do_dst(z):
        return do_recv.at[z]

    exchange(do_src, do_dst, 1, back_ss, back_rs)

    def rs0_add(a):
        def step(s, _):
            z, yl = lax.div(s, 2), lax.rem(s, 2)
            rs0(a, z, yl).wait()
            mine = g[a, z, yl, :, :, me.c].astype(F32)
            r0[a, z, yl] = (r0[a, z, yl].astype(F32) + mine).astype(BF)
            return 0

        lax.fori_loop(0, 8, step, 0)

    rbs = (rb1, rb2, rb3)

    def rs_copy(group, t, stage, d):
        order = ORDERS[t][::-1]
        to = shifted(me, order[stage], d)
        src = part(r0, to, t, order[stage + 1 :], lead(group), core=False)
        at = rbs[stage][t].at[(d - 1,) + lead(group)]
        return remote(src, at, rs_ss.at[group, t, stage, d - 1], rs_rs.at[group, t, stage, d - 1], to)

    def rs_start(group, stage):
        for d in (1, 3, 2):
            for t in range(3):
                start(rs_copy(group, t, stage, d))

    def rs_sum(group, t, stage):
        order = ORDERS[t][::-1]
        for d in (1, 3, 2):
            rs_copy(group, t, stage, d).wait_recv()
        at = part(r0, me, t, order[stage + 1 :], lead(group), core=False)
        first, count = GROUPS[group]
        got = rbs[stage][t]
        total = at[...].astype(F32)
        for d in range(3):
            total += got[d, first : first + count].astype(F32)
        return at, total

    def rs_next(group, stage):
        for t in range(3):
            at, total = rs_sum(group, t, stage - 1)
            at[...] = total.astype(BF)
            for d in (1, 3, 2):
                start(rs_copy(group, t, stage, d))

    def rs_finish(group, store):
        for t in range(3):
            _, total = rs_sum(group, t, 2)
            store(t, total)

    rs0_add(2)
    rs0_add(1)
    rs_start(1, 0)

    for d in (1, 3, 2, 0):
        exchange_wait(do_src, do_dst, 1, back_ss, back_rs, d)
    dkv_s[...] = jnp.zeros_like(dkv_s)

    def sib_copy(b):
        return remote(dkv_sib.at[b], dkv_got.at[b], kvs_ss.at[4 + b], kvs_rs.at[4 + b], sib)

    for b in (3, 2, 1, 0):
        n = 256 * (b + 1)
        allowed = allowed_of(b)
        dqs, dss, pbs, dos, qs = [], [], [], [], []
        for h in range(3):
            q = query_of(b, h)
            do = half(do_recv[b, :, 0:128] if h < 2 else do_recv[b, :, 128:256], h > 0)
            scores = jnp.where(allowed, nt(keys_of(b, h), q), NEG)
            probs = jnp.exp(scores - lse_s[b, h : h + 1, :])
            dw = nt(values_of(b, h), do)
            centre = jnp.sum(probs * dw, axis=0, keepdims=True)
            ds = (probs * (dw - centre)).astype(BF)
            dqs.append(nn(kvt[K_ROWS[h] : K_ROWS[h] + 64, 0:n], ds))
            dss.append(ds)
            pbs.append(probs.astype(BF))
            dos.append(do)
            qs.append(q)
        dqs.append(jnp.zeros((64, TOK), F32))
        dq_send[b] = (jnp.concatenate(dqs, axis=0) * 0.125).T.astype(BF)

        def pair(l0, l1, r0_, r1_):
            return nn(jnp.concatenate([l0, l1], axis=1), jnp.concatenate([r0_, r1_], axis=0))

        dkv_s[0:n, 0:128] += pair(dss[0], dss[1], qs[0], qs[1])
        dkv_s[0:n, 128:256] += pair(dss[2], pbs[2], qs[2], dos[2])
        dkv_s[0:n, 256:384] += pair(pbs[0], pbs[1], dos[0], dos[1])
        other = pl.multiple_of(256 * b + TOK * (1 - me.c), TOK)
        dkv_sib[b] = dkv_s[pl.ds(other, TOK), :].astype(BF)
        start(sib_copy(b))

    def dq_src(z):
        return dq_send.at[z]

    def dq_dst(z):
        return dq_recv.at[z]

    def dkv_src(z):
        return dkv_send.at[z]

    def dkv_dst(z):
        return dkv_recv.at[z]

    exchange(dq_src, dq_dst, 2, back_ss, back_rs)
    for b in (3, 2, 1, 0):
        sib_copy(b).wait_recv()
        own = pl.multiple_of(256 * b + TOK * me.c, TOK)
        dkv_send[b] = (dkv_s[pl.ds(own, TOK), :] + dkv_got[b].astype(F32)).astype(BF)
    exchange(dkv_src, dkv_dst, 3, back_ss, back_rs)
    rs_next(1, 1)
    for d in (1, 3, 2, 0):
        exchange_wait(dq_src, dq_dst, 2, back_ss, back_rs, d)
    for d in (1, 3, 2, 0):
        exchange_wait(dkv_src, dkv_dst, 3, back_ss, back_rs, d)

    for h in range(4):
        got = dkv_recv[h]
        dmix_s[:, 192 * h : 192 * h + 192] = dq_recv[h, :, 0:192]
        dmix_s[:, D + 192 * h : D + 192 * h + 192] = got[:, 0:192]
        dmix_s[:, 2 * D + 192 * h : 2 * D + 192 * h + 192] = jnp.concatenate(
            [got[:, 256:384], got[:, 192:256]], axis=1
        )
    zeros96, zeros288 = jnp.zeros((TOK, 96), BF), jnp.zeros((TOK, 288), BF)
    d_first = jnp.zeros((TOK, D), F32)
    for s in range(8):
        z, yl = s // 2, s % 2
        left = jnp.concatenate([dmix_s[:, 288 * s : 288 * s + 288], zeros96], axis=1)
        right = jnp.concatenate([zeros288, dbr_s[:, 96 * s : 96 * s + 96]], axis=1)
        grad = nn(fat_s[...], jnp.concatenate([left, right], axis=0))
        g[0, z, yl] = grad.astype(BF).reshape(2, 4, 2, 48, SHARD)
        start(rs0(0, z, yl))
        d_first += nt(left, w[0, z, yl].reshape(D, SHARD))
    d_x = norm_back(d_first, whole(FIRST_GAIN), n1, rstd1)
    gin_ref[...] = mid_s[...] + d_x
    g_gain_a = col_sums(d_first * n1)
    g_shift_a = col_sums(d_first)
    sums = col_sums(dmix_s[...])
    biases = jnp.concatenate([sums[:, 0:D], sums[:, 2 * D : 3 * D]], axis=1)

    rows = [(FIRST_GAIN, g_gain_a), (FIRST_SHIFT, g_shift_a), (MERGE_BIAS, g_b_merge), (SECOND_GAIN, g_gain_b)]
    rows += [(SECOND_SHIFT, g_shift_b), (SHRINK_BIAS, g_b_shrink)]
    for s in range(8):
        for row, value in rows:
            vg[s, row : row + 1, 0:96] = value[:, 96 * s : 96 * s + 96]
        for k in range(2):
            at = 192 * s + 96 * k
            vg[s, MIXER_BIAS + k : MIXER_BIAS + k + 1, 0:96] = biases[:, at : at + 96]

    def vred(k):
        to = seq_peer(k)
        return remote(vg.at[to.z * 2 + to.yl], vr.at[k - 1], vred_ss.at[k - 1], vred_rs.at[k - 1], to)

    for k in range(1, 8):
        start(vred(k))
    for s in range(8):
        pass
    rs0_add_a(rs0, g, r0, me)
    rs_start(0, 0)
    for k in range(1, 8):
        vred(k).wait_recv()
    total = vg[seq]
    for k in range(7):
        total += vr[k]
    vsum[0] = total
    vcopy = remote(vsum.at[0], vsum.at[1], vx_ss.at[0], vx_rs.at[0], sib)
    start(vcopy)

    def store_es(t, total):
        gexp_ref[16 * t : 16 * t + 16, :] = total[0]
        gshr_ref[16 * t : 16 * t + 16, :] = total[1]

    def store_a(t, total):
        gmix_ref[16 * t : 16 * t + 16, :] = total[0, :, 0:288]
        gmerge_ref[16 * t : 16 * t + 16, :] = total[0, :, 288:384]

    rs_next(1, 2)
    vcopy.wait_recv()
    vx[me.x] = vsum[0] + vsum[1]

    def vx_copy(d, back=False):
        at = vx.at[shifted(me, "x", -d).x] if back else vx.at[me.x]
        return remote(at, at, vx_ss.at[d], vx_rs.at[d], shifted(me, "x", d))

    for d in (1, 2, 3):
        start(vx_copy(d))
    rs_next(0, 1)
    for d in (1, 2, 3):
        vx_copy(d, True).wait_recv()
    vsum[2] = vx[0] + vx[1] + vx[2] + vx[3]
    ycopy = remote(vsum.at[2], vsum.at[3], vx_ss.at[4], vx_rs.at[4], shifted(me, "y", 2))
    start(ycopy)
    rs_finish(1, store_es)
    rs_next(0, 2)
    ycopy.wait_recv()
    vout_ref[...] = vsum[2] + vsum[3]
    rs_finish(0, store_a)
    for copy in pending:
        copy.wait_send()


def rs0_add_a(rs0, g, r0, me):
    def step(s, _):
        z, yl = lax.div(s, 2), lax.rem(s, 2)
        rs0(0, z, yl).wait_recv()
        mine = g[0, z, yl, :, :, me.c].astype(F32)
        r0[0, z, yl] = (r0[0, z, yl].astype(F32) + mine).astype(BF)
        return 0

    lax.fori_loop(0, 8, step, 0)


def scratches():
    v, dma = pltpu.VMEM, pltpu.SemaphoreType.DMA
    third = (16, SHARD)
    return [
        v((3, 4, 2, 2, 4, 2, 48, SHARD), BF),
        v((3, 4, 2, 2, 4, 2, 48, SHARD), BF),
        v((3, 4, 2, 2, 4, 48, SHARD), BF),
        [v((3, 3, 2, 2, 4) + third, BF), v((3, 3, 4, 2, 2) + third, BF), v((3, 3, 4, 4) + third, BF)],
        [v((3, 3, 4) + third, BF), v((3, 3, 2, 2) + third, BF), v((3, 3, 4) + third, BF)],
        [v((3, 3) + third, BF) for _ in range(3)],
        v((8, 16, TOK), BF),
        v((2, 8, TOK), F32),
        v((TOK, D), BF),
        v((TOK, 3 * D), BF),
        v((4, TOK, 256), BF),
        v((4, TOK, SHARD), BF),
        v((4, TOK, 256), BF),
        v((4, 2, TOK, SHARD), BF),
        v((SHARD, 8 * TOK), BF),
        v((4, 8, TOK), F32),
        v((4, TOK, 256), BF),
        v((4, TOK, 256), BF),
        v((TOK, D), BF),
        v((TOK, D), F32),
        v((TOK, D), F32),
        v((D, TOK), BF),
        v((D, TOK), BF),
        v((TOK, D), F32),
        v((TOK, D), F32),
        v((TOK, D), BF),
        v((D, 2 * TOK), BF),
        v((4, TOK, 256), BF),
        v((4, TOK, 256), BF),
        v((8 * TOK, SHARD), F32),
        v((4, TOK, SHARD), BF),
        v((4, TOK, SHARD), BF),
        v((4, TOK, 256), BF),
        v((4, TOK, 256), BF),
        v((4, TOK, SHARD), BF),
        v((4, TOK, SHARD), BF),
        v((TOK, 3 * D), BF),
        v((TOK, D), F32),
        v((8, 16, TOK), F32),
        v((7, 16, TOK), F32),
        v((4, 16, TOK), F32),
        v((4, 16, TOK), F32),
        dma((2, 3, 3, 3)), dma((2, 3, 3, 3)),
        dma((2, 3, 4)), dma((2, 3, 4)),
        dma((7,)), dma((7,)),
        dma((1,)), dma((1,)),
        dma((2, 4)), dma((2, 4)),
        dma((8,)), dma((8,)),
        dma((4, 4)), dma((4, 4)),
        dma((3, 8)), dma((3, 8)),
        dma((2, 3, 3, 3)), dma((2, 3, 3, 3)),
        dma((7,)), dma((7,)),
        dma((5,)), dma((5,)),
        dma((1,)),
    ]


def body(
    residual_in, cotangent, segments, first_gain, first_shift, mixer_weight, mixer_bias, merge_weight, merge_bias,
    second_gain, second_shift, expand_weight, expand_bias, shrink_weight, shrink_bias,
):
    weights = jnp.stack([jnp.concatenate([mixer_weight, merge_weight], axis=1), expand_weight, shrink_weight.T])
    small = [first_gain, first_shift, mixer_bias[:96], mixer_bias[96:], merge_bias, second_gain, second_shift, shrink_bias]
    vec = jnp.concatenate(
        [jnp.pad(jnp.stack(small), ((0, 0), (0, 32))), expand_bias.reshape(3, TOK), jnp.zeros((5, TOK), BF)], axis=0
    )
    vmem = pl.BlockSpec(memory_space=pltpu.VMEM)
    shapes = [((TOK, D), BF), ((TOK, D), F32), ((48, 288), F32), ((48, 96), F32), ((48, SHARD), F32), ((48, SHARD), F32)]
    shapes += [((16, TOK), F32)]
    hidden, gin, gmix, gmerge, gexp, gshr, vout = pl.pallas_call(
        kernel,
        out_shape=[jax.ShapeDtypeStruct(*s) for s in shapes],
        in_specs=[vmem] * 5,
        out_specs=[vmem] * 7,
        scratch_shapes=scratches(),
        compiler_params=pltpu.CompilerParams(
            collective_id=0, has_side_effects=True, vmem_limit_bytes=62 * 1024 * 1024
        ),
    )(residual_in[0], cotangent[0], segments.reshape(8, TOK), weights, vec)
    return (
        hidden[None], gin[None], vout[0, :96], vout[1, :96], gmix, vout[2:4, :96].reshape(192), gmerge, vout[4, :96],
        vout[5, :96], vout[6, :96], gexp, vout[8:11].reshape(SHARD), gshr.T, vout[7, :96],
    )


def solution(mesh):
    vector, matrix = P("seq"), P("dp", "seq")
    tokens = P("dp", "seq", None)
    return jax.shard_map(
        body,
        mesh=mesh,
        in_specs=(
            tokens, tokens, P("dp", None), vector, vector, matrix, vector, matrix, vector, vector, vector, matrix, vector,
            P("seq", "dp"), vector,
        ),
        out_specs=(
            tokens, tokens, vector, vector, matrix, vector, matrix, vector, vector, vector, matrix, vector,
            P("seq", "dp"), vector,
        ),
        check_vma=False,
    )
```

```python
import functools
import types

import jax
import jax.numpy as jnp
from jax import lax
from jax.experimental import pallas as pl
from jax.experimental.pallas import tpu as pltpu
from jax.sharding import PartitionSpec as P


D = 768
HD = 64
TOK = 128
SHARD = 384
WIDE = 896
MERGE = 768
EPS = 1e-05
NEG = -1e30
MESH = pl.DeviceIdType.MESH
BF = jnp.bfloat16
F32 = jnp.float32
ORDERS = (("x", "y", "z"), ("y", "z", "x"), ("z", "x", "y"))
FIRST_GAIN, FIRST_SHIFT, MIXER_BIAS, MERGE_BIAS, SECOND_GAIN, SECOND_SHIFT, SHRINK_BIAS, EXPAND_BIAS = 0, 1, 2, 4, 5, 6, 7, 8


def place_of():
    dp, seq = lax.axis_index("dp"), lax.axis_index("seq")
    return types.SimpleNamespace(
        x=lax.rem(lax.div(dp, 2), 4),
        yh=lax.div(dp, 8),
        yl=lax.rem(seq, 2),
        z=lax.div(seq, 2),
        c=lax.rem(dp, 2),
    )


def moved(at, **to):
    new = types.SimpleNamespace(**vars(at))
    for name, value in to.items():
        setattr(new, name, value)
    return new


def shifted(at, axis, d):
    d = d % 4
    if axis == "x":
        return moved(at, x=lax.rem(at.x + d, 4))
    if axis == "z":
        return moved(at, z=lax.rem(at.z + d, 4))
    y = lax.rem(at.yh * 2 + at.yl + d, 4)
    return moved(at, yh=lax.div(y, 2), yl=lax.rem(y, 2))


def device(at):
    return (at.yh * 8 + at.x * 2 + at.c, at.z * 2 + at.yl)


def nn(a, b):
    return jnp.dot(a, b, preferred_element_type=F32)


def nt(a, b):
    return lax.dot_general(a, b, (((1,), (1,)), ((), ())), preferred_element_type=F32)


def remote(src, dst, send, recv, to):
    return pltpu.make_async_remote_copy(
        src_ref=src, dst_ref=dst, send_sem=send, recv_sem=recv, device_id=device(to), device_id_type=MESH
    )


def part(ref, at, t, full, core=True):
    every = slice(None)
    where = [every if "z" in full else at.z]
    where += [every, every] if "y" in full else [at.yl, at.yh]
    where += [every if "x" in full else at.x]
    if core:
        where += [at.c]
    return ref.at[tuple(where) + (pl.ds(16 * t, 16), every)]


def norm_parts(v):
    centred = v - jnp.mean(v, axis=-1, keepdims=True)
    rstd = lax.rsqrt(jnp.mean(centred * centred, axis=-1, keepdims=True) + EPS)
    return centred * rstd, rstd


def norm_back(dy, gain, normed, rstd):
    dn = dy * gain
    return rstd * (
        dn
        - jnp.mean(dn, axis=-1, keepdims=True)
        - normed * jnp.mean(dn * normed, axis=-1, keepdims=True)
    )


def col_sums(v):
    return jnp.sum(v.astype(F32), axis=0, keepdims=True)


def turned(v):
    return v.astype(F32).T.astype(BF)


def lanes(*pieces):
    return jnp.concatenate(pieces, axis=1)


def tile(k):
    return pl.ds(pl.multiple_of(k * TOK, TOK), TOK)


IN = (
    "x_in", "cot_in", "seg_in", "mixer_in", "merge_in", "expand_in", "shrink_in", "fgain_in", "fshift_in", "mixb_in",
    "mergeb_in", "sgain_in", "sshift_in", "expandb_in", "shrinkb_in",
)
OUT = ("hidden", "gin", "gmix", "gmerge", "gexp", "gshr", "vout")


def kernel(names, *refs):
    r = types.SimpleNamespace(**dict(zip(names, refs, strict=True)))
    me = place_of()
    sib = moved(me, c=1 - me.c)
    swap = moved(me, yl=me.c, c=me.yl)
    here = me.yl == me.c
    seq = me.z * 2 + me.yl
    ypos = me.yh * 2 + me.yl
    pending = []

    def post(copy):
        copy.start()
        pending.append(copy.wait_send)

    def post_unless(alone, src, dst, send, recv, to):
        @pl.when(alone)
        def _():
            pltpu.make_async_copy(src, dst, recv).start()

        @pl.when(jnp.logical_not(alone))
        def _():
            remote(src, dst, send, recv, to).start()

        def finish():
            @pl.when(jnp.logical_not(alone))
            def _():
                remote(src, dst, send, recv, to).wait_send()

        pending.append(finish)

    def arrived(at, send, recv):
        remote(at, at, send, recv, sib).wait_recv()

    zero32 = jnp.zeros((48, 32), BF)
    for i in range(3):
        r.units[i] = lanes(r.mixer_in[:, 96 * i : 96 * i + 96], zero32)
    own = (me.z, me.yl, me.yh, me.x, me.c)
    r.w[own] = lanes(r.expand_in[...], r.shrink_in[...], r.merge_in[...], zero32)
    mixb = r.mixb_in[...].astype(F32).reshape(1, 192)
    small = [(FIRST_GAIN, r.fgain_in), (FIRST_SHIFT, r.fshift_in), (MERGE_BIAS, r.mergeb_in)]
    small += [(SECOND_GAIN, r.sgain_in), (SECOND_SHIFT, r.sshift_in), (SHRINK_BIAS, r.shrinkb_in)]
    for row, ref in small:
        r.vecs[seq, row : row + 1, 0:96] = ref[...].astype(F32).reshape(1, 96)
    expb = r.expandb_in[...].astype(F32).reshape(1, SHARD)
    for k in range(2):
        r.vecs[seq, MIXER_BIAS + k : MIXER_BIAS + k + 1, 0:96] = mixb[:, 96 * k : 96 * k + 96]
    for k in range(3):
        r.vecs[seq, EXPAND_BIAS + k : EXPAND_BIAS + k + 1, :] = expb[:, TOK * k : TOK * k + TOK]
    r.segs[0] = r.seg_in[...].astype(F32)

    peers = [shifted(shifted(me, "z", dz), "y", dy) for dz in range(4) for dy in range(4) if dz or dy]
    peers += [shifted(me, "x", d) for d in (1, 2, 3)] + [sib, shifted(sib, "y", 2)]
    peers += [moved(shifted(me, "z", d), yl=1 - me.yl, c=1 - me.c) for d in range(4)]
    barrier = pltpu.get_barrier_semaphore()
    for p in peers:
        pl.semaphore_signal(barrier, inc=1, device_id=device(p), device_id_type=MESH)
    pl.semaphore_wait(barrier, len(peers))

    def send_block(kind, b, src, dst):
        to = moved(swap, z=b)
        post_unless(here & (me.z == b), src, dst, r.ex_ss.at[kind, b], r.ex_rs.at[kind, me.z], to)

    def take_block(kind, z, dst):
        arrived(dst, r.ex_ss.at[kind, z], r.ex_rs.at[kind, z])

    X, ATT, DO, DF = range(4)
    for b in range(4):
        send_block(X, b, r.x_in, r.xall.at[me.z])
    for i in range(3):
        u = 3 * seq + i
        for dy in range(4):
            y = lax.rem(ypos + dy, 4)
            to = moved(me, z=lax.div(lax.rem(u, 8), 2), yh=lax.div(y, 2), yl=lax.rem(y, 2))
            half = lax.rem(u, 2)
            kind = lax.div(u, 8)
            dst = r.wm.at[half, me.yh, me.x, me.c, :, tile(kind)]
            sems = (r.wm1_ss.at[i, dy], r.wm1_rs.at[half, me.yh, kind])
            if dy:
                post(remote(r.units.at[i], dst, *sems, to))
            else:
                post_unless(to.z == me.z, r.units.at[i], dst, *sems, to)

    def seq_peer(k):
        at = shifted(me, "z", k // 2)
        return moved(at, yl=1 - me.yl) if k % 2 else at

    def seq_from(k):
        at = shifted(me, "z", -(k // 2))
        return moved(at, yl=1 - me.yl) if k % 2 else at

    for k in range(1, 8):
        post(remote(r.vecs.at[seq], r.vecs.at[seq], r.vec_ss.at[k - 1], r.vec_rs.at[k - 1], seq_peer(k)))
    post(remote(r.segs.at[0], r.segs.at[1], r.one_ss.at[0], r.one_rs.at[0], sib))

    def ag(t, stage, d):
        order = ORDERS[t]
        at = part(r.w, me, t, order[:stage])
        return remote(
            at, at, r.ag_ss.at[t, stage, d - 1], r.ag_rs.at[t, stage, d - 1], shifted(me, order[stage], d)
        )

    def ag_wait(t, stage, d):
        order = ORDERS[t]
        at = part(r.w, shifted(me, order[stage], -d), t, order[:stage])
        arrived(at, r.ag_ss.at[t, stage, d - 1], r.ag_rs.at[t, stage, d - 1])

    def hand(t, d, mine):
        order = ORDERS[t]
        at = shifted(me if mine else sib, order[2], -d)
        view = part(r.w, at, t, order[:2])
        return remote(view, view, r.hand_ss.at[t, d], r.hand_rs.at[t, d], sib)

    def ag_start():
        for d in (1, 3, 2):
            for t in range(3):
                post(ag(t, 0, d))

    def ag_next(stage):
        for t in range(3):
            for d in (1, 3, 2):
                ag_wait(t, stage - 1, d)
            for d in (1, 3, 2):
                post(ag(t, stage, d))
            if stage == 2:
                post(hand(t, 0, True))

    def ag_finish():
        for d in (1, 3, 2):
            for t in range(3):
                ag_wait(t, 2, d)
                post(hand(t, d, True))
        for d in (0, 1, 3, 2):
            for t in range(3):
                hand(t, d, False).wait_recv()

    ag_start()
    for half in range(2):
        for yh in range(2):
            for kind in range(3):
                at = r.wm.at[half, yh, me.x, me.c, :, pl.ds(TOK * kind, TOK)]
                arrived(at, r.wm1_ss.at[0, 0], r.wm1_rs.at[half, yh, kind])

    def wm_view(d, core):
        return r.wm.at[:, :, lax.rem(me.x + 4 - d, 4), core]

    for d in (1, 3, 2):
        post(
            remote(
                wm_view(0, me.c), wm_view(0, me.c), r.wm2_ss.at[d], r.wm2_rs.at[d], shifted(me, "x", d)
            )
        )
    post(remote(wm_view(0, me.c), wm_view(0, me.c), r.wms_ss.at[0], r.wms_rs.at[0], sib))
    for k in range(1, 8):
        src = seq_from(k)
        arrived(r.vecs.at[src.z * 2 + src.yl], r.vec_ss.at[k - 1], r.vec_rs.at[k - 1])

    def whole(row):
        return jnp.concatenate([r.vecs[s, row : row + 1, 0:96] for s in range(8)], axis=1)

    r.cott[...] = turned(r.cot_in[...])
    n1, rstd1 = norm_parts(r.x_in[...].astype(F32))
    r.n1[...] = n1
    gain1, shift1 = whole(FIRST_GAIN), whole(FIRST_SHIFT)
    for b in range(4):
        take_block(X, b, r.xall.at[b])
        normed, _ = norm_parts(r.xall[b].astype(F32))
        r.n1all[b] = normed
        first = normed * gain1 + shift1
        r.fall[b] = first.astype(BF)
        r.fallt[:, TOK * b : TOK * b + TOK] = first.astype(BF).astype(F32).T.astype(BF)
    ag_next(1)
    for d in (1, 3, 2):
        arrived(wm_view(d, me.c), r.wm2_ss.at[d], r.wm2_rs.at[d])
        post(remote(wm_view(d, me.c), wm_view(d, me.c), r.wms_ss.at[d], r.wms_rs.at[d], sib))
    ag_next(2)
    for d in (0, 1, 3, 2):
        arrived(wm_view(d, 1 - me.c), r.wms_ss.at[d], r.wms_rs.at[d])

    def mixer(half, first, count):
        at = slice(TOK * first, TOK * (first + count))
        return r.wm[half, :, :, :, :, at].reshape(D, TOK * count)

    first = r.fall[...].reshape(4 * TOK, D)

    def mixer_bias(at, half):
        row = MIXER_BIAS + half
        return r.vecs[at, row : row + 1, 0:96]

    kv0, kv1 = nn(first, mixer(0, 1, 2)), nn(first, mixer(1, 1, 2))
    keys = lanes(kv0[:, 0:96], kv1[:, 0:96]).astype(BF)
    vbias = lanes(mixer_bias(4 + me.z, 0), mixer_bias(4 + me.z, 1))
    values = (lanes(kv0[:, 128:224], kv1[:, 128:224]) + vbias).astype(BF)
    packed = lanes(keys, values[:, 128:192], values[:, 0:128])
    for b in range(4):
        r.kv_all[b, me.c] = packed[TOK * b : TOK * b + TOK]
    at = r.kv_all.at[:, me.c]
    post(remote(at, at, r.kvs_ss.at[4], r.kvs_rs.at[4], sib))
    qbias = lanes(mixer_bias(me.z, 0), mixer_bias(me.z, 1))
    q = lanes(nn(first, mixer(0, 0, 1))[:, 0:96], nn(first, mixer(1, 0, 1))[:, 0:96])
    q = (q + qbias).astype(BF) * jnp.asarray(0.125, BF)
    q = lanes(q, jnp.zeros((4 * TOK, 64), BF))
    for b in range(4):
        r.q_all[b] = q[TOK * b : TOK * b + TOK]
        r.kvt[:, tile(2 * b + me.c)] = turned(packed[TOK * b : TOK * b + TOK])
    arrived(r.segs.at[1], r.one_ss.at[0], r.one_rs.at[0])
    arrived(r.kv_all.at[:, 1 - me.c], r.kvs_ss.at[4], r.kvs_rs.at[4])
    for b in range(4):
        r.kvt[:, tile(2 * b + 1 - me.c)] = turned(r.kv_all[b, 1 - me.c])

    seg = jnp.where(here, r.segs[0], r.segs[1])

    def starts(bound):
        return jnp.sum(jnp.where(seg < bound, 1.0, 0.0), axis=(0, 1), keepdims=True).astype(jnp.int32)

    begin1, begin2 = starts(0.5), starts(1.5)
    lane = lax.broadcasted_iota(jnp.int32, (TOK, TOK), 1)

    def allowed_of(b):
        n = 256 * (b + 1)
        qpos = 256 * b + TOK * me.c + lax.broadcasted_iota(jnp.int32, (1, TOK), 1)
        low = jnp.where(qpos < begin1, 0, jnp.where(qpos < begin2, begin1, begin2))
        kpos = lax.broadcasted_iota(jnp.int32, (n, TOK), 0)
        return (kpos <= qpos) & (kpos >= low)

    def keys_of(b, h):
        at = slice(0, 128) if h < 2 else slice(128, 256)
        return r.kv_all[0 : b + 1, :, :, at].reshape(256 * (b + 1), TOK)

    def values_of(b, h):
        at = slice(256, 384) if h < 2 else slice(128, 256)
        return r.kv_all[0 : b + 1, :, :, at].reshape(256 * (b + 1), TOK)

    K_ROWS = (0, 64, 128)
    V_ROWS = (256, 320, 192)

    def one_head(v, upper):
        keep = lane >= 64 if upper else lane < 64
        return jnp.where(keep, v, jnp.zeros_like(v))

    def query_of(b, h):
        return one_head(r.q_all[b, :, 0:128] if h < 2 else r.q_all[b, :, 128:256], h == 1)

    for b in (3, 2, 1, 0):
        n = 256 * (b + 1)
        allowed = allowed_of(b)
        outs = []
        for h in range(3):
            scores = jnp.where(allowed, nt(keys_of(b, h), query_of(b, h)), NEG)
            top = jnp.max(scores, axis=0, keepdims=True)
            expo = jnp.exp(scores - top)
            total = jnp.sum(expo, axis=0, keepdims=True)
            r.lse[b, h : h + 1, :] = top + jnp.log(total)
            weights = (expo * (1.0 / total)).astype(BF)
            outs.append(nn(r.kvt[V_ROWS[h] : V_ROWS[h] + 64, 0:n], weights))
        outs.append(jnp.zeros((64, TOK), F32))
        r.att_send[b] = jnp.concatenate(outs, axis=0).T.astype(BF)
        send_block(ATT, b, r.att_send.at[b], r.att_recv.at[me.z])
    for b in range(4):
        take_block(ATT, b, r.att_recv.at[b])
        r.att[:, 192 * b : 192 * b + 192] = r.att_recv[b, :, 0:192]
    ag_finish()

    def merge_tile(s):
        return r.w[s // 2, s % 2, :, :, :, :, MERGE:WIDE].reshape(D, TOK)

    branch = lanes(*[nn(r.att[...], merge_tile(s))[:, 0:96] for s in range(8)])
    middle = r.x_in[...].astype(F32) + branch + whole(MERGE_BIAS)
    r.mid[...] = middle
    n2, rstd2 = norm_parts(middle)
    r.n2[...] = n2
    second = (n2 * whole(SECOND_GAIN) + whole(SECOND_SHIFT)).astype(BF)
    r.second[...] = second
    r.secondt[...] = turned(second)
    r.attt[...] = turned(r.att[...])
    r.mlp[...] = jnp.zeros((TOK, D), F32)
    r.dsec[...] = jnp.zeros((TOK, D), F32)

    def rs0(z, yl):
        src = r.g.at[z, yl, :, :, 1 - me.c, :, pl.ds(0, MERGE)]
        s = z * 2 + yl
        return remote(src, r.r0.at[z, yl, :, :, :, pl.ds(0, MERGE)], r.rs0_ss.at[s], r.rs0_rs.at[s], sib)

    def rs0_merge():
        src = r.g.at[:, :, :, :, 1 - me.c, :, pl.ds(MERGE, TOK)]
        dst = r.r0.at[:, :, :, :, :, pl.ds(MERGE, TOK)]
        return remote(src, dst, r.rs0_ss.at[8], r.rs0_rs.at[8], sib)

    def units(s, _):
        z, yl = lax.div(s, 2), lax.rem(s, 2)
        rows = r.vecs[s]
        bias = lanes(*[rows[EXPAND_BIAS + k : EXPAND_BIAS + k + 1] for k in range(3)])
        expand = r.w[z, yl, :, :, :, :, 0:SHARD].reshape(D, SHARD)
        shrink = r.w[z, yl, :, :, :, :, SHARD:MERGE].reshape(D, SHARD)
        pre = nn(r.second[...], expand) + bias
        square = pre * pre
        tanh = jnp.tanh(0.7978845608028654 * (pre + 0.044715 * square * pre))
        active = (0.5 * pre * (1.0 + tanh)).astype(BF)
        slope = 0.5 * (1.0 + tanh) + 0.5 * pre * (1.0 - tanh * tanh) * (
            0.7978845608028654 * (1.0 + 0.134145 * square)
        )
        d_pre = (nn(r.cot_in[...], shrink) * slope).astype(BF)
        r.mlp[...] += nt(active, shrink)
        r.dsec[...] += nt(d_pre, expand)
        sums = col_sums(d_pre)
        for k in range(3):
            r.vg[s, EXPAND_BIAS + k : EXPAND_BIAS + k + 1, :] = sums[:, TOK * k : TOK * k + TOK]
        blocks = (2, 4, 2, 48, SHARD)
        r.g[z, yl, :, :, :, :, 0:SHARD] = nn(r.secondt[...], d_pre).astype(BF).reshape(blocks)
        r.g[z, yl, :, :, :, :, SHARD:MERGE] = nn(r.cott[...], active).astype(BF).reshape(blocks)
        rs0(z, yl).start()
        return 0

    lax.fori_loop(0, 8, units, 0)
    r.hidden[...] = (r.mid[...] + r.mlp[...] + whole(SHRINK_BIAS)).astype(BF)

    d_second = r.dsec[...]
    cot = r.cot_in[...].astype(F32)
    d_middle = cot + norm_back(d_second, whole(SECOND_GAIN), r.n2[...], rstd2)
    r.mid[...] = d_middle
    d_branch = d_middle.astype(BF)
    r.dbr[...] = d_branch
    g_gain_b = col_sums(d_second * r.n2[...])
    g_shift_b = col_sums(d_second)
    g_b_shrink = col_sums(cot)
    g_b_merge = col_sums(d_branch)
    zeros = jnp.zeros((TOK, 32), BF)

    def branch_part(s):
        return lanes(r.dbr[:, 96 * s : 96 * s + 96], zeros)

    d_att = jnp.zeros((TOK, D), F32)
    for s in range(8):
        d_att += nt(branch_part(s), merge_tile(s))
    d_att = d_att.astype(BF)
    for b in range(4):
        o = d_att[:, 192 * b : 192 * b + 192]
        r.do_send[b] = lanes(o[:, 0:128], jnp.zeros((TOK, 64), BF), o[:, 128:192])
        send_block(DO, b, r.do_send.at[b], r.do_recv.at[me.z])

    for s in range(8):
        r.g[s // 2, s % 2, :, :, :, :, MERGE:WIDE] = (
            nn(r.attt[...], branch_part(s)).astype(BF).reshape(2, 4, 2, 48, TOK)
        )
    rs0_merge().start()

    def rs_copy(t, stage, d):
        order = ORDERS[t][::-1]
        to = shifted(me, order[stage], d)
        src = part(r.r0, to, t, order[stage + 1 :], core=False)
        at = (r.rb1, r.rb2, r.rb3)[stage][t].at[d - 1]
        return remote(src, at, r.rs_ss.at[t, stage, d - 1], r.rs_rs.at[t, stage, d - 1], to)

    def rs_start():
        for d in (1, 3, 2):
            for t in range(3):
                post(rs_copy(t, 0, d))

    def rs_sum(t, stage):
        order = ORDERS[t][::-1]
        for d in (1, 3, 2):
            rs_copy(t, stage, d).wait_recv()
        at = part(r.r0, me, t, order[stage + 1 :], core=False)
        got = (r.rb1, r.rb2, r.rb3)[stage][t]
        total = at[...].astype(F32)
        for d in range(3):
            total += got[d].astype(F32)
        return at, total

    def rs_next(stage):
        for t in range(3):
            at, total = rs_sum(t, stage - 1)
            at[...] = total.astype(BF)
            for d in (1, 3, 2):
                post(rs_copy(t, stage, d))

    rs0_merge().wait()

    def add(s, _):
        z, yl = lax.div(s, 2), lax.rem(s, 2)
        rs0(z, yl).wait()
        mine = r.g[z, yl, :, :, me.c].astype(F32)
        r.r0[z, yl] = (r.r0[z, yl].astype(F32) + mine).astype(BF)
        return 0

    lax.fori_loop(0, 8, add, 0)
    rs_start()

    rows = [(MERGE_BIAS, g_b_merge), (SECOND_GAIN, g_gain_b), (SECOND_SHIFT, g_shift_b), (SHRINK_BIAS, g_b_shrink)]
    for s in range(8):
        for row, value in rows:
            r.vg[s, row : row + 1, 0:96] = value[:, 96 * s : 96 * s + 96]
        r.vg[s, MIXER_BIAS : MIXER_BIAS + 2, :] = jnp.zeros((2, TOK), F32)

    r.dkv[...] = jnp.zeros((8 * TOK, SHARD), F32)
    for b in range(4):
        take_block(DO, b, r.do_recv.at[b])

    def sib_copy(b):
        return remote(r.dkv_sib.at[b], r.dkv_got.at[b], r.kvs_ss.at[b], r.kvs_rs.at[b], sib)

    def pair(l0, l1, r0, r1):
        return nn(jnp.concatenate([l0, l1], axis=1), jnp.concatenate([r0, r1], axis=0))

    gain_sum, shift_sum = [], []

    def finish_block(b):
        sib_copy(b).wait_recv()
        own = pl.multiple_of(256 * b + TOK * me.c, TOK)
        dkv = (r.dkv[pl.ds(own, TOK), :] + r.dkv_got[b].astype(F32)).astype(BF)
        dq = r.dq[b]
        dv = lanes(dkv[:, 256:384], dkv[:, 192:256])
        d_first = jnp.zeros((TOK, D), F32)
        for half in range(2):
            at = slice(96 * half, 96 * half + 96)
            padded = lanes(dq[:, at], zeros, dkv[:, at], zeros, dv[:, at], zeros)
            r.dpad[half, TOK * b : TOK * b + TOK, :] = padded
            d_first += nt(padded, mixer(half, 0, 3))
        r.df_send[b] = d_first.astype(BF)
        send_block(DF, b, r.df_send.at[b], r.df_recv.at[me.z])
        gain_sum.append(col_sums(d_first * r.n1all[b]))
        shift_sum.append(col_sums(d_first))

    for b in (3, 2, 1, 0):
        n = 256 * (b + 1)
        allowed = allowed_of(b)
        dqs, dss, pbs, dos, qs = [], [], [], [], []
        for h in range(3):
            q = query_of(b, h)
            do = one_head(r.do_recv[b, :, 0:128] if h < 2 else r.do_recv[b, :, 128:256], h > 0)
            scores = jnp.where(allowed, nt(keys_of(b, h), q), NEG)
            probs = jnp.exp(scores - r.lse[b, h : h + 1, :])
            dw = nt(values_of(b, h), do)
            centre = jnp.sum(probs * dw, axis=0, keepdims=True)
            ds = (probs * (dw - centre)).astype(BF)
            dqs.append(nn(r.kvt[K_ROWS[h] : K_ROWS[h] + 64, 0:n], ds))
            dss.append(ds)
            pbs.append(probs.astype(BF))
            dos.append(do)
            qs.append(q)
        dqs.append(jnp.zeros((64, TOK), F32))
        r.dq[b] = (jnp.concatenate(dqs, axis=0) * 0.125).T.astype(BF)
        r.dkv[0:n, 0:128] += pair(dss[0], dss[1], qs[0], qs[1])
        r.dkv[0:n, 128:256] += pair(dss[2], pbs[2], qs[2], dos[2])
        r.dkv[0:n, 256:384] += pair(pbs[0], pbs[1], dos[0], dos[1])
        other = pl.multiple_of(256 * b + TOK * (1 - me.c), TOK)
        r.dkv_sib[b] = r.dkv[pl.ds(other, TOK), :].astype(BF)
        post(sib_copy(b))
        if b < 3:
            finish_block(b + 1)
    finish_block(0)

    for half in range(2):
        grad = nn(r.fallt[...], r.dpad[half]).astype(BF)
        r.gm[half] = grad.reshape(2, 4, 2, 48, SHARD)
    gm_sib = remote(r.gm.at[:, :, :, 1 - me.c], r.rm0, r.rm0_ss.at[0], r.rm0_rs.at[0], sib)
    post(gm_sib)
    for half in range(2):
        sums = col_sums(r.dpad[half])
        row = MIXER_BIAS + half
        r.vg[me.z, row : row + 1, 0:96] = sums[:, 0:96]
        r.vg[4 + me.z, row : row + 1, 0:96] = sums[:, 256:352]
    gain_a, shift_a = sum(gain_sum), sum(shift_sum)
    for s in range(8):
        r.vg[s, FIRST_GAIN : FIRST_GAIN + 1, 0:96] = gain_a[:, 96 * s : 96 * s + 96]
        r.vg[s, FIRST_SHIFT : FIRST_SHIFT + 1, 0:96] = shift_a[:, 96 * s : 96 * s + 96]

    def vred(k):
        to = seq_peer(k)
        return remote(r.vg.at[to.z * 2 + to.yl], r.vr.at[k - 1], r.vred_ss.at[k - 1], r.vred_rs.at[k - 1], to)

    for k in range(1, 8):
        post(vred(k))
    gm_sib.wait_recv()
    r.rm0[...] = (r.rm0[...].astype(F32) + r.gm[:, :, :, me.c].astype(F32)).astype(BF)

    def rmx_copy(d):
        to = shifted(me, "x", d)
        return remote(r.rm0.at[:, :, to.x], r.rmx.at[d - 1], r.rmx_ss.at[d - 1], r.rmx_rs.at[d - 1], to)

    for d in (1, 3, 2):
        post(rmx_copy(d))
    rs_next(1)
    for k in range(1, 8):
        vred(k).wait_recv()
    total = r.vg[seq]
    for k in range(7):
        total += r.vr[k]
    r.vx[me.x] = total

    def vx_copy(d, back=False):
        at = r.vx.at[shifted(me, "x", -d).x] if back else r.vx.at[me.x]
        return remote(at, at, r.vx_ss.at[d], r.vx_rs.at[d], shifted(me, "x", d))

    for d in (1, 2, 3):
        post(vx_copy(d))
    for d in (1, 3, 2):
        rmx_copy(d).wait_recv()
    summed = r.rm0[:, :, me.x].astype(F32)
    for d in range(3):
        summed += r.rmx[d].astype(F32)
    r.rmy[...] = summed.astype(BF)
    for half in range(2):
        for yh in range(2):
            for kind in range(3):
                u = 8 * kind + 2 * me.z + half
                owner = lax.div(u, 3)
                to = moved(me, yh=yh, z=lax.div(owner, 2), yl=lax.rem(owner, 2))
                slot = (lax.rem(u, 3), ypos)
                alone = (me.yh == yh) & (owner == seq)
                post_unless(
                    alone,
                    r.rmy.at[half, yh, :, pl.ds(TOK * kind, TOK)],
                    r.rmf.at[slot],
                    r.rmf_ss.at[half, yh, kind],
                    r.rmf_rs.at[slot],
                    to,
                )
    for d in (1, 2, 3):
        vx_copy(d, True).wait_recv()
    ours = me.yh * 2 + me.c
    r.vy[ours] = r.vx[0] + r.vx[1] + r.vx[2] + r.vx[3]
    pairs = ((sib, 0), (shifted(me, "y", 2), 1), (shifted(sib, "y", 2), 2))

    def vy_copy(k, back=False):
        to = pairs[k][0]
        at = r.vy.at[to.yh * 2 + to.c] if back else r.vy.at[ours]
        return remote(at, at, r.vy_ss.at[k], r.vy_rs.at[k], to)

    for k in range(3):
        post(vy_copy(k))
    rs_next(2)

    d_first = jnp.zeros((TOK, D), F32)
    for b in range(4):
        take_block(DF, b, r.df_recv.at[b])
        d_first += r.df_recv[b].astype(F32)
    r.gin[...] = r.mid[...] + norm_back(d_first, gain1, r.n1[...], rstd1)

    for t in range(3):
        _, total = rs_sum(t, 2)
        at = slice(16 * t, 16 * t + 16)
        r.gexp[at, :] = total[:, 0:SHARD]
        r.gshr[at, :] = total[:, SHARD:MERGE]
        r.gmerge[at, :] = total[:, MERGE : MERGE + 96]
    for k in range(3):
        vy_copy(k, True).wait_recv()
    r.vout[...] = r.vy[0] + r.vy[1] + r.vy[2] + r.vy[3]
    for i in range(3):
        total = jnp.zeros((48, TOK), F32)
        for y in range(4):
            arrived(r.rmf.at[i, y], r.rmf_ss.at[0, 0, 0], r.rmf_rs.at[i, y])
            total += r.rmf[i, y].astype(F32)
        r.gmix[:, 96 * i : 96 * i + 96] = total[:, 0:96]
    for finish in pending:
        finish()


def scratches():
    v, dma = pltpu.VMEM, pltpu.SemaphoreType.DMA
    third, blocks = (16, WIDE), (2, 4, 2, 48)
    s = {
        "w": v((4, 2) + blocks + (WIDE,), BF),
        "g": v((4, 2) + blocks + (WIDE,), BF),
        "r0": v((4, 2, 2, 4, 48, WIDE), BF),
        "rb1": [v((3, 2, 2, 4) + third, BF), v((3, 4, 2, 2) + third, BF), v((3, 4, 4) + third, BF)],
        "rb2": [v((3, 4) + third, BF), v((3, 2, 2) + third, BF), v((3, 4) + third, BF)],
        "rb3": [v((3,) + third, BF) for _ in range(3)],
        "units": v((3, 48, TOK), BF),
        "wm": v((2,) + blocks + (SHARD,), BF),
        "gm": v((2,) + blocks + (SHARD,), BF),
        "rm0": v((2, 2, 4, 48, SHARD), BF),
        "rmx": v((3, 2, 2, 48, SHARD), BF),
        "rmy": v((2, 2, 48, SHARD), BF),
        "rmf": v((3, 4, 48, TOK), BF),
        "vecs": v((8, 16, TOK), F32),
        "segs": v((2, 8, TOK), F32),
        "xall": v((4, TOK, D), BF),
        "n1all": v((4, TOK, D), F32),
        "fall": v((4, TOK, D), BF),
        "fallt": v((D, 4 * TOK), BF),
        "q_all": v((4, TOK, 256), BF),
        "kv_all": v((4, 2, TOK, SHARD), BF),
        "kvt": v((SHARD, 8 * TOK), BF),
        "lse": v((4, 8, TOK), F32),
        "dkv": v((8 * TOK, SHARD), F32),
        "dkv_sib": v((4, TOK, SHARD), BF),
        "dkv_got": v((4, TOK, SHARD), BF),
        "dq": v((4, TOK, 256), BF),
        "dpad": v((2, 4 * TOK, SHARD), BF),
        "df_send": v((4, TOK, D), BF),
        "df_recv": v((4, TOK, D), BF),
    }
    for name in ("att_send", "att_recv", "do_send", "do_recv"):
        s[name] = v((4, TOK, 256), BF)
    for name in ("mid", "n1", "n2", "mlp", "dsec"):
        s[name] = v((TOK, D), F32)
    for name in ("att", "second", "dbr"):
        s[name] = v((TOK, D), BF)
    for name in ("cott", "secondt", "attt"):
        s[name] = v((D, TOK), BF)
    for name, count in (("vg", 8), ("vr", 7), ("vx", 4), ("vy", 4)):
        s[name] = v((count, 16, TOK), F32)
    sems = {
        "ag": (3, 3, 3), "hand": (3, 4), "ex": (4, 4), "wm1": (3, 4), "wm2": (4,), "wms": (4,), "vec": (7,), "one": (1,),
        "kvs": (5,), "rs0": (9,), "rs": (3, 3, 3), "rm0": (1,), "rmx": (3,), "rmf": (2, 2, 3), "vred": (7,), "vx": (4,),
        "vy": (3,),
    }
    for name, shape in sems.items():
        s[name + "_ss"] = dma(shape)
        s[name + "_rs"] = dma(shape)
    s["wm1_rs"] = dma((2, 2, 3))
    s["rmf_rs"] = dma((3, 4))
    return s


def finish(hidden, gin, gmix, gmerge, gexp, gshr, vout, *outs):
    for ref, out in zip((hidden, gin, gmix, gmerge, gexp, gshr), outs[:6], strict=True):
        out[...] = ref[...]
    v = vout[...]
    rows = (FIRST_GAIN, FIRST_SHIFT, MERGE_BIAS, SECOND_GAIN, SECOND_SHIFT, SHRINK_BIAS)
    for row, out in zip(rows, outs[6:12], strict=True):
        out[...] = v[row : row + 1, 0:96].reshape(96)
    outs[12][...] = lanes(v[MIXER_BIAS : MIXER_BIAS + 1, 0:96], v[MIXER_BIAS + 1 : MIXER_BIAS + 2, 0:96]).reshape(192)
    outs[13][...] = lanes(*[v[EXPAND_BIAS + k : EXPAND_BIAS + k + 1] for k in range(3)]).reshape(SHARD)


def body(
    residual_in, cotangent, segments, first_gain, first_shift, mixer_weight, mixer_bias, merge_weight, merge_bias,
    second_gain, second_shift, expand_weight, expand_bias, shrink_weight, shrink_bias,
):
    vmem = pl.BlockSpec(memory_space=pltpu.VMEM)
    scratch = scratches()
    shapes = [((TOK, D), BF), ((TOK, D), F32), ((48, 288), F32), ((48, 96), F32), ((48, SHARD), F32), ((48, SHARD), F32)]
    held = [jax.ShapeDtypeStruct(*s) for s in shapes]
    parts = pl.pallas_call(
        functools.partial(kernel, IN + OUT + tuple(scratch)),
        out_shape=held + [jax.ShapeDtypeStruct((16, TOK), F32)],
        in_specs=[vmem] * len(IN),
        out_specs=[vmem] * len(OUT),
        scratch_shapes=list(scratch.values()),
        compiler_params=pltpu.CompilerParams(
            collective_id=0, has_side_effects=True, vmem_limit_bytes=62 * 1024 * 1024
        ),
    )(
        residual_in[0], cotangent[0], segments.reshape(8, TOK), mixer_weight, merge_weight, expand_weight,
        shrink_weight.T, first_gain, first_shift, mixer_bias, merge_bias, second_gain, second_shift, expand_bias,
        shrink_bias,
    )
    vectors = [jax.ShapeDtypeStruct((n,), F32) for n in (96, 96, 96, 96, 96, 96, 192, SHARD)]
    hidden, gin, gmix, gmerge, gexp, gshr, fg, fs, mb, sg, ss, sb, xb, eb = pl.pallas_call(
        finish, out_shape=held + vectors, in_specs=[vmem] * 7, out_specs=[vmem] * 14
    )(*parts)
    return hidden[None], gin[None], fg, fs, gmix, xb, gmerge, mb, sg, ss, gexp, eb, gshr.T, sb


def solution(mesh):
    vector, matrix = P("seq"), P("dp", "seq")
    tokens = P("dp", "seq", None)
    return jax.shard_map(
        body,
        mesh=mesh,
        in_specs=(
            tokens, tokens, P("dp", None), vector, vector, matrix, vector, matrix, vector, vector, vector, matrix, vector,
            P("seq", "dp"), vector,
        ),
        out_specs=(
            tokens, tokens, vector, vector, matrix, vector, matrix, vector, vector, vector, matrix, vector,
            P("seq", "dp"), vector,
        ),
        check_vma=False,
    )
```

```python
import functools
import types

import jax
import jax.numpy as jnp
from jax import lax
from jax.experimental import pallas as pl
from jax.experimental.pallas import tpu as pltpu
from jax.sharding import PartitionSpec as P


D = 768
HD = 64
TOK = 128
SHARD = 384
WIDE = 768
EPS = 1e-05
NEG = -1e30
MESH = pl.DeviceIdType.MESH
BF = jnp.bfloat16
F32 = jnp.float32
SENDS, RECVS = 45, 46
FIRST_GAIN, FIRST_SHIFT, MIXER_BIAS, MERGE_BIAS, SECOND_GAIN, SECOND_SHIFT, SHRINK_BIAS, EXPAND_BIAS = 0, 1, 2, 4, 5, 6, 7, 8


def place_of():
    dp, seq = lax.axis_index("dp"), lax.axis_index("seq")
    return types.SimpleNamespace(
        x=lax.rem(lax.div(dp, 2), 4),
        yh=lax.div(dp, 8),
        yl=lax.rem(seq, 2),
        z=lax.div(seq, 2),
        c=lax.rem(dp, 2),
    )


def moved(at, **to):
    new = types.SimpleNamespace(**vars(at))
    for name, value in to.items():
        setattr(new, name, value)
    return new


def shifted(at, axis, d):
    d = d % 4
    if axis == "x":
        return moved(at, x=lax.rem(at.x + d, 4))
    if axis == "z":
        return moved(at, z=lax.rem(at.z + d, 4))
    y = lax.rem(at.yh * 2 + at.yl + d, 4)
    return moved(at, yh=lax.div(y, 2), yl=lax.rem(y, 2))


def device(at):
    return (at.yh * 8 + at.x * 2 + at.c, at.z * 2 + at.yl)


def nn(a, b):
    return jnp.dot(a, b, preferred_element_type=F32)


def nt(a, b):
    return lax.dot_general(a, b, (((1,), (1,)), ((), ())), preferred_element_type=F32)


def remote(src, dst, send, recv, to):
    return pltpu.make_async_remote_copy(
        src_ref=src, dst_ref=dst, send_sem=send, recv_sem=recv, device_id=device(to), device_id_type=MESH
    )


def norm_parts(v):
    centred = v - jnp.mean(v, axis=-1, keepdims=True)
    rstd = lax.rsqrt(jnp.mean(centred * centred, axis=-1, keepdims=True) + EPS)
    return centred * rstd, rstd


def norm_back(dy, gain, normed, rstd):
    dn = dy * gain
    return rstd * (
        dn
        - jnp.mean(dn, axis=-1, keepdims=True)
        - normed * jnp.mean(dn * normed, axis=-1, keepdims=True)
    )


def col_sums(v):
    return jnp.sum(v.astype(F32), axis=0, keepdims=True)


def turned(v):
    return v.astype(F32).T.astype(BF)


def lanes(*pieces):
    return jnp.concatenate(pieces, axis=1)


def tile(k):
    return pl.ds(pl.multiple_of(k * TOK, TOK), TOK)


IN = (
    "x_in", "cot_in", "seg_in", "mixer_in", "merge_in", "expand_in", "shrink_in", "fgain_in", "fshift_in", "mixb_in",
    "mergeb_in", "sgain_in", "sshift_in", "expandb_in", "shrinkb_in",
)
OUT = ("hidden", "gin", "gmix", "gmerge", "gexp", "gshr", "vout")


def kernel(names, *refs):
    r = types.SimpleNamespace(**dict(zip(names, refs, strict=True)))
    me = place_of()
    sib = moved(me, c=1 - me.c)
    swap = moved(me, yl=me.c, c=me.yl)
    here = me.yl == me.c
    seq = me.z * 2 + me.yl
    ypos = me.yh * 2 + me.yl
    pending = []
    sends, recvs = {}, {}

    def send_of(*key):
        return r.send.at[sends.setdefault(key, len(sends))]

    def recv_of(*key):
        return r.recv.at[recvs.setdefault(key, len(recvs))]

    def copy_to(to, src, dst, *key, recv=None):
        return remote(src, dst, send_of(*key), recv_of(*(recv or key)), to)

    def arrived(size, *key):
        remote(size, size, r.send.at[0], recv_of(*key), sib).wait_recv()

    def wait_sent(size, *key):
        remote(size, size, send_of(*key), r.recv.at[0], sib).wait_send()

    def sent(size, *key):
        pending.append(lambda: wait_sent(size, *key))

    def sent_unless(alone, size, *key):
        def finish():
            @pl.when(jnp.logical_not(alone))
            def _():
                wait_sent(size, *key)

        pending.append(finish)

    def start_unless(alone, to, src, dst, *key, recv=None):
        @pl.when(alone)
        def _():
            pltpu.make_async_copy(src, dst, recv_of(*(recv or key))).start()

        @pl.when(jnp.logical_not(alone))
        def _():
            copy_to(to, src, dst, *key, recv=recv).start()

    zero32 = jnp.zeros((48, 32), BF)
    for i in range(3):
        r.units[i] = lanes(r.mixer_in[:, 96 * i : 96 * i + 96], zero32)
    own = (me.z, me.yl, me.yh, me.x, me.c)
    r.wz[own[1:]] = lanes(r.expand_in[...], r.shrink_in[...])
    r.m_w[own] = lanes(r.merge_in[...], zero32)
    mixb = r.mixb_in[...].astype(F32).reshape(1, 192)
    small = [(FIRST_GAIN, r.fgain_in), (FIRST_SHIFT, r.fshift_in), (MERGE_BIAS, r.mergeb_in)]
    small += [(SECOND_GAIN, r.sgain_in), (SECOND_SHIFT, r.sshift_in), (SHRINK_BIAS, r.shrinkb_in)]
    for row, ref in small:
        r.vecs[seq, row : row + 1, 0:96] = ref[...].astype(F32).reshape(1, 96)
    expb = r.expandb_in[...].astype(F32).reshape(1, SHARD)
    for k in range(2):
        r.vecs[seq, MIXER_BIAS + k : MIXER_BIAS + k + 1, 0:96] = mixb[:, 96 * k : 96 * k + 96]
    for k in range(3):
        r.vecs[seq, EXPAND_BIAS + k : EXPAND_BIAS + k + 1, :] = expb[:, TOK * k : TOK * k + TOK]
    r.segs[0] = r.seg_in[...].astype(F32)

    peers = [shifted(shifted(me, "z", dz), "y", dy) for dz in range(4) for dy in range(4) if dz or dy]
    peers += [shifted(me, "x", d) for d in (1, 2, 3)] + [sib, shifted(sib, "y", 2)]
    peers += [moved(shifted(me, "z", d), yl=1 - me.yl, c=1 - me.c) for d in range(4)]
    peers += [shifted(shifted(at, "x", d), "y", dy) for d in (1, 2, 3) for at, dy in ((sib, 0), (me, 2), (sib, 2))]
    barrier = pltpu.get_barrier_semaphore()
    for p in peers:
        pl.semaphore_signal(barrier, inc=1, device_id=device(p), device_id_type=MESH)
    pl.semaphore_wait(barrier, len(peers))

    def send_block(b, src):
        start_unless(here & (me.z == b), moved(swap, z=b), src, r.df_recv.at[me.z], "block")

    def take_blocks():
        arrived(r.df_recv, "block")

        def finish():
            @pl.when(here)
            def _():
                wait_sent(r.df_recv.at[0:3], "block")

            @pl.when(jnp.logical_not(here))
            def _():
                wait_sent(r.df_recv, "block")

        pending.append(finish)

    def send_own(name):
        at = getattr(r, name).at[me.z]
        for d in (1, 3, 2):
            copy_to(shifted(me, "z", d), at, at, name).start()

    def send_along(name, src_of, order=(1, 3, 2)):
        for d in order:
            to = shifted(me, "z", d)
            copy_to(to, src_of(to.z), getattr(r, name).at[me.z], name).start()

    def take_along(name):
        arrived(getattr(r, name).at[0:3], name)
        sent(getattr(r, name).at[0:3], name)

    def send_back(src, dst, key):
        start_unless(here, swap, src, dst, key)
        sent_unless(here, src, key)

    for i in range(3):
        u = 3 * seq + i
        group = lax.div(lax.rem(u, 8), 2)
        dst = r.wm.at[lax.rem(u, 2), me.yh, me.x, me.c, :, tile(lax.div(u, 8))]
        for dy in range(4):
            y = lax.rem(ypos + dy, 4)
            to = moved(me, z=group, yh=lax.div(y, 2), yl=lax.rem(y, 2))
            if dy:
                copy_to(to, r.units.at[i], dst, "unit").start()
            else:
                start_unless(group == me.z, to, r.units.at[i], dst, "unit", i, recv=("unit",))
        sent_unless(group == me.z, r.units.at[i], "unit", i)
    sent(r.rmf.at[:, 0:3], "unit")

    send_back(r.x_in, r.xall.at[me.z], "x")

    @pl.when(here)
    def _():
        arrived(r.xall.at[0], "x")
        send_own("xall")

    def seq_peer(k):
        at = shifted(me, "z", k // 2)
        return moved(at, yl=1 - me.yl) if k % 2 else at

    for k in range(1, 8):
        copy_to(seq_peer(k), r.vecs.at[seq], r.vecs.at[seq], "vec").start()
    sent(r.vr, "vec")

    def plane(ref, d):
        return ref.at[(slice(None),) * (len(ref.shape) - 4) + (lax.rem(me.x + 4 - d, 4), me.c)]

    def plane_start(ref, key):
        at = plane(ref, 0)
        for d in (1, 3, 2):
            copy_to(shifted(me, "x", d), at, at, key, recv=(key, d)).start()
        copy_to(sib, at, at, key, "hand").start()
        every = (slice(None),) * (len(ref.shape) - 4)
        sent(ref.at[every + (slice(0, 3), me.c)], key)
        sent(ref.at[every + (slice(0, 4), me.c)], key, "hand")

    def plane_hand(ref, key):
        for d in (1, 3, 2):
            at = plane(ref, d)
            arrived(at, key, d)
            copy_to(sib, at, at, key, "hand").start()

    def plane_finish(ref, key):
        every = (slice(None),) * (len(ref.shape) - 4)
        arrived(ref.at[every + (slice(0, 4), 1 - me.c)], key, "hand")

    def column(d):
        at = shifted(me, "y", -d)
        return r.wz.at[at.yl, at.yh, :, me.c]

    def column_start():
        for d in (1, 3, 2):
            copy_to(shifted(me, "y", d), column(0), column(0), "column", recv=("column", d)).start()
        copy_to(sib, column(0), column(0), "column", "hand").start()
        sent(r.wz.at[0, :, 0:3], "column")
        sent(r.wz.at[:, :, :, me.c], "column", "hand")

    def column_hand():
        for d in (1, 3, 2):
            arrived(column(d), "column", d)
            copy_to(sib, column(d), column(d), "column", "hand").start()

    def column_finish():
        arrived(r.wz.at[:, :, :, 1 - me.c], "column", "hand")

    copy_to(sib, r.segs.at[0], r.segs.at[1], "seg").start()
    sent(r.segs.at[0], "seg")
    own = r.wz.at[me.yl, me.yh, me.x, me.c]
    for d in (1, 3, 2):
        copy_to(shifted(me, "x", d), own, own, "hidden").start()
    sent(r.gy, "hidden")
    around = [(dz, dy) for dz in (1, 3, 0, 2) for dy in (0, 1, 3, 2) if dz or dy]
    at = r.m_w.at[me.z, me.yl, me.yh, me.x, me.c]
    for dz, dy in around:
        copy_to(shifted(shifted(me, "z", dz), "y", dy), at, at, "merge").start()
    sent(r.m_y, "merge")
    send_back(r.cot_in, r.call.at[me.z], "cot")
    arrived(r.wm.at[:, :, me.x, me.c], "unit")

    plane_start(r.wm, "mixer")
    @pl.when(jnp.logical_not(here))
    def _():
        arrived(r.xall.at[0], "x")
        send_own("xall")

    arrived(r.gy, "hidden")
    column_start()
    arrived(r.vr, "vec")

    def whole(row):
        return jnp.concatenate([r.vecs[s, row : row + 1, 0:96] for s in range(8)], axis=1)


    n1, rstd1 = norm_parts(r.x_in[...].astype(F32))
    r.n1[...] = n1
    gain1, shift1 = whole(FIRST_GAIN), whole(FIRST_SHIFT)
    plane_hand(r.wm, "mixer")
    take_along("xall")
    arrived(r.call.at[0], "cot")
    send_own("call")
    for b in range(4):
        normed, _ = norm_parts(r.xall[b].astype(F32))
        r.n1all[b] = normed
        first = normed * gain1 + shift1
        r.fall[b] = first.astype(BF)
        r.fallt[:, :, :, TOK * b : TOK * b + TOK] = turned(first.astype(BF)).reshape(8, 2, 48, TOK)
    plane_finish(r.wm, "mixer")

    at = r.fallt.at[:, 1 - me.c]
    copy_to(sib, at, r.fallt_sib, "first").start()
    sent(r.fallt_sib, "first")
    def mixer(half, first, count):
        at = slice(TOK * first, TOK * (first + count))
        return r.wm[half, :, :, :, :, at].reshape(D, TOK * count)

    first = r.fall[...].reshape(4 * TOK, D)

    def mixer_bias(at, half):
        row = MIXER_BIAS + half
        return r.vecs[at, row : row + 1, 0:96]

    kv0, kv1 = nn(first, mixer(0, 1, 2)), nn(first, mixer(1, 1, 2))
    keys = lanes(kv0[:, 0:96], kv1[:, 0:96]).astype(BF)
    vbias = lanes(mixer_bias(4 + me.z, 0), mixer_bias(4 + me.z, 1))
    values = (lanes(kv0[:, 128:224], kv1[:, 128:224]) + vbias).astype(BF)
    packed = lanes(keys, values[:, 128:192], values[:, 0:128])
    for b in range(4):
        r.kv_all[b, me.c] = packed[TOK * b : TOK * b + TOK]
    at = r.kv_all.at[:, me.c]
    copy_to(sib, at, at, "kv").start()
    sent(at, "kv")
    arrived(r.m_y, "merge")
    plane_start(r.m_w, "merge x")
    qbias = lanes(mixer_bias(me.z, 0), mixer_bias(me.z, 1))
    q = lanes(nn(first, mixer(0, 0, 1))[:, 0:96], nn(first, mixer(1, 0, 1))[:, 0:96])
    q = (q + qbias).astype(BF) * jnp.asarray(0.125, BF)
    q = lanes(q, jnp.zeros((4 * TOK, 64), BF))
    for b in range(4):
        r.q_all[b] = q[TOK * b : TOK * b + TOK]
        r.kvt[:, tile(2 * b + me.c)] = turned(packed[TOK * b : TOK * b + TOK])
    arrived(r.segs.at[1], "seg")
    arrived(r.kv_all.at[:, 1 - me.c], "kv")
    for b in range(4):
        r.kvt[:, tile(2 * b + 1 - me.c)] = turned(r.kv_all[b, 1 - me.c])

    seg = jnp.where(here, r.segs[0], r.segs[1])

    def starts(bound):
        return jnp.sum(jnp.where(seg < bound, 1.0, 0.0), axis=(0, 1), keepdims=True).astype(jnp.int32)

    begin1, begin2 = starts(0.5), starts(1.5)
    lane = lax.broadcasted_iota(jnp.int32, (TOK, TOK), 1)

    def allowed_of(b):
        n = 256 * (b + 1)
        qpos = 256 * b + TOK * me.c + lax.broadcasted_iota(jnp.int32, (1, TOK), 1)
        low = jnp.where(qpos < begin1, 0, jnp.where(qpos < begin2, begin1, begin2))
        kpos = lax.broadcasted_iota(jnp.int32, (n, TOK), 0)
        return (kpos <= qpos) & (kpos >= low)

    def keys_of(b, h):
        at = slice(0, 128) if h < 2 else slice(128, 256)
        return r.kv_all[0 : b + 1, :, :, at].reshape(256 * (b + 1), TOK)

    def values_of(b, h):
        at = slice(256, 384) if h < 2 else slice(128, 256)
        return r.kv_all[0 : b + 1, :, :, at].reshape(256 * (b + 1), TOK)

    K_ROWS = (0, 64, 128)
    V_ROWS = (256, 320, 192)

    def one_head(v, upper):
        keep = lane >= 64 if upper else lane < 64
        return jnp.where(keep, v, jnp.zeros_like(v))

    def query_of(b, h):
        return one_head(r.q_all[b, :, 0:128] if h < 2 else r.q_all[b, :, 128:256], h == 1)

    spare = []
    for b in (3, 2, 1, 0):
        n = 256 * (b + 1)
        allowed = allowed_of(b)
        outs = []
        for h in range(3):
            scores = jnp.where(allowed, nt(keys_of(b, h), query_of(b, h)), NEG)
            top = jnp.max(scores, axis=0, keepdims=True)
            expo = jnp.exp(scores - top)
            total = jnp.sum(expo, axis=0, keepdims=True)
            r.lse[b, h : h + 1, :] = top + jnp.log(total)
            weights = (expo * (1.0 / total)).astype(BF)
            outs.append(nn(r.kvt[V_ROWS[h] : V_ROWS[h] + 64, 0:n], weights))
        r.att_all[me.z, b] = jnp.concatenate(outs[0:2], axis=0).T.astype(BF)
        spare.append(outs[2])
        ready = [b]
        if b % 2 == 0:
            r.att_all[me.z, 4 + b // 2] = jnp.concatenate([spare[-1], spare[-2]], axis=0).T.astype(BF)
            ready.append(4 + b // 2)
        for k in ready:
            for d in (1, 3, 2):
                at = r.att_all.at[me.z, k]
                copy_to(shifted(me, "z", d), at, at, "att", recv=("att", b // 2)).start()
        if b == 1:
            column_hand()
        if b == 0:
            plane_hand(r.m_w, "merge x")
    sent(r.att_all.at[0:3], "att")
    take_along("call")
    for b in range(4):
        r.cott[:, TOK * b : TOK * b + TOK] = turned(r.call[b])
    plane_finish(r.m_w, "merge x")
    for s in range(8):
        r.mc[:, 96 * s : 96 * s + 96] = r.m_w[s // 2, s % 2].reshape(D, TOK)[:, 0:96]

    gain2, shift2 = whole(SECOND_GAIN), whole(SECOND_SHIFT)
    for pair in (1, 0):
        arrived(r.att_all.at[0:3, 0:3], "att", pair)
        for b in (2 * pair + 1, 2 * pair):
            at = slice(64 * (b % 2), 64 * (b % 2) + 64)
            r.att[b] = lanes(*[v for g in range(4) for v in (r.att_all[g, b], r.att_all[g, 4 + pair, :, at])])
        rows = slice(2 * pair, 2 * pair + 2)
        branch = nn(r.att[rows].reshape(2 * TOK, D), r.mc[...])
        middle = r.xall[rows].reshape(2 * TOK, D).astype(F32) + branch + whole(MERGE_BIAS)
        r.mid[rows] = middle.reshape(2, TOK, D)
        n2, _ = norm_parts(middle)
        r.second[rows] = (n2 * gain2 + shift2).astype(BF).reshape(2, TOK, D)
    column_finish()

    def hidden(first):
        return lanes(*[r.wz[yl, :, :, :, :, first : first + SHARD].reshape(D, SHARD) for yl in range(2)])

    bias = lanes(*[r.vecs[2 * me.z + yl, EXPAND_BIAS + k : EXPAND_BIAS + k + 1] for yl in range(2) for k in range(3)])
    for step in range(2):
        blocks = [shifted(me, "z", d).z for d in ((2, 1), (3, 0))[step]]

        def rows_of(ref, blocks=blocks):
            return jnp.concatenate([ref[b] for b in blocks], axis=0)

        pre = nn(rows_of(r.second), hidden(0)) + bias
        square = pre * pre
        tanh = jnp.tanh(0.7978845608028654 * (pre + 0.044715 * square * pre))
        active = (0.5 * pre * (1.0 + tanh)).astype(BF)
        slope = 0.5 * (1.0 + tanh) + 0.5 * pre * (1.0 - tanh * tanh) * (
            0.7978845608028654 * (1.0 + 0.134145 * square)
        )
        d_pre = (nn(rows_of(r.call), hidden(SHARD)) * slope).astype(BF)
        d_second = nt(d_pre, hidden(0)).astype(BF)
        for i, b in enumerate(blocks):
            at = slice(TOK * i, TOK * i + TOK)
            r.active[b] = active[at]
            r.dpre[b] = d_pre[at]
            (r.dsec_send if (step, i) != (1, 1) else r.dsec)[b] = d_second[at]
        send_along("dsec", lambda z: r.dsec_send.at[z], ((2, 1), (3,))[step])

    sums = col_sums(r.dpre[...].reshape(4 * TOK, WIDE))
    r.vg[...] = jnp.zeros((8, 16, TOK), F32)
    for yl in range(2):
        for k in range(3):
            at = TOK * (3 * yl + k)
            r.vg[2 * me.z + yl, EXPAND_BIAS + k : EXPAND_BIAS + k + 1, :] = sums[:, at : at + TOK]
    for b in range(4):
        r.secondt[:, TOK * b : TOK * b + TOK] = turned(r.second[b])
    shape = (2, 4, 2, 48, SHARD)
    for first, left, right in ((0, r.secondt, r.dpre), (SHARD, r.cott, r.active)):
        grad = nn(left[...], right[...].reshape(4 * TOK, WIDE)).astype(BF)
        for yl in range(2):
            r.gz[yl, :, :, :, :, first : first + SHARD] = grad[:, SHARD * yl : SHARD * yl + SHARD].reshape(shape)
    copy_to(sib, r.gz.at[:, :, :, 1 - me.c], r.gz0, "hidden", "pair").start()
    sent(r.gz0, "hidden", "pair")
    result = nt(r.active[...].reshape(4 * TOK, WIDE), hidden(SHARD)).astype(BF)
    for b in range(4):
        r.res_send[b] = result[TOK * b : TOK * b + TOK]
    r.attt[...] = turned(r.att[me.z])

    def pair_sum(ref, own, key):
        arrived(ref, key, "pair")
        every = (slice(None),) * (len(ref.shape) - 2)
        ref[...] = (ref[...].astype(F32) + own[every + (me.c,)].astype(F32)).astype(BF)

    def plane_send(ref, got, key):
        every = (slice(None),) * (len(ref.shape) - 3)
        for d in (1, 3, 2):
            to = shifted(me, "x", d)
            copy_to(to, ref.at[every + (to.x,)], got.at[d - 1], key, "sum").start()
        sent(got, key, "sum")

    def plane_total(ref, got, key):
        arrived(got, key, "sum")
        total = ref[(slice(None),) * (len(ref.shape) - 3) + (me.x,)].astype(F32)
        for d in range(3):
            total += got[d].astype(F32)
        return total.astype(BF)

    pair_sum(r.gz0, r.gz, "hidden")
    for d in (1, 3, 2):
        to = shifted(me, "y", d)
        copy_to(to, r.gz0.at[to.yl, to.yh], r.gzy.at[d - 1], "hidden y").start()
    sent(r.gzy, "hidden y")
    take_along("dsec")

    d_second = sum(r.dsec[b].astype(F32) for b in range(4))
    cot = r.call[me.z].astype(F32)
    n2, rstd2 = norm_parts(r.mid[me.z])
    d_middle = cot + norm_back(d_second, gain2, n2, rstd2)
    d_branch = d_middle.astype(BF)
    r.dbr[...] = d_branch
    zeros = jnp.zeros((TOK, 32), BF)
    d_att = nt(d_branch, r.mc[...]).astype(BF)
    for b in range(4):
        o = d_att[:, 192 * b : 192 * b + 192]
        r.do_send[b] = lanes(o[:, 0:128], jnp.zeros((TOK, 64), BF), o[:, 128:192])
    send_along("do_recv", lambda z: r.do_send.at[z])
    send_along("res_recv", lambda z: r.res_send.at[z])
    r.res_recv[me.z] = r.res_send[me.z]
    r.do_recv[me.z] = r.do_send[me.z]

    r.dmid[...] = d_middle
    send_back(r.dmid, r.dmid_recv, "dmid")

    for s in range(8):
        right = lanes(r.dbr[:, 96 * s : 96 * s + 96], zeros)
        r.m_g[s // 2, s % 2] = nn(r.attt[...], right).astype(BF).reshape(2, 4, 2, 48, TOK)
    copy_to(sib, r.m_g.at[:, :, :, :, 1 - me.c], r.m_r0, "merge", "pair").start()
    sent(r.m_r0, "merge", "pair")

    g_gain_b = col_sums(d_second * n2)
    g_shift_b = col_sums(d_second)
    g_b_shrink = col_sums(cot)
    g_b_merge = col_sums(d_branch)
    rows = [(MERGE_BIAS, g_b_merge), (SECOND_GAIN, g_gain_b), (SECOND_SHIFT, g_shift_b), (SHRINK_BIAS, g_b_shrink)]
    for s in range(8):
        for row, value in rows:
            r.vg[s, row : row + 1, 0:96] = value[:, 96 * s : 96 * s + 96]

    pair_sum(r.m_r0, r.m_g, "merge")
    plane_send(r.m_r0, r.m_x, "merge")

    r.dkv[...] = jnp.zeros((8 * TOK, SHARD), F32)
    take_along("do_recv")
    sent(r.dkv_got, "dkv")

    def pair(l0, l1, r0, r1):
        return nn(jnp.concatenate([l0, l1], axis=1), jnp.concatenate([r0, r1], axis=0))

    gain_sum, shift_sum = [], []

    def finish_block(b):
        arrived(r.dkv_got.at[b], "dkv", b)
        own = pl.multiple_of(256 * b + TOK * me.c, TOK)
        dkv = (r.dkv[pl.ds(own, TOK), :] + r.dkv_got[b].astype(F32)).astype(BF)
        dq = r.dq[b]
        dv = lanes(dkv[:, 256:384], dkv[:, 192:256])
        for half in range(2):
            at = slice(96 * half, 96 * half + 96)
            r.dpad[half, b] = lanes(dq[:, at], zeros, dkv[:, at], zeros, dv[:, at], zeros)
        at = r.dpad.at[:, b]
        copy_to(sib, at, r.dpad_sib.at[:, b], "dpad").start()
        d_first = nt(r.dpad[0, b], mixer(0, 0, 3)) + nt(r.dpad[1, b], mixer(1, 0, 3))
        r.df_send[b] = d_first.astype(BF)
        if b:
            send_block(b, r.df_send.at[b])
        gain_sum.append(col_sums(d_first * r.n1all[b]))
        shift_sum.append(col_sums(d_first))

    for b in (3, 2, 1, 0):
        n = 256 * (b + 1)
        allowed = allowed_of(b)
        dqs, dss, pbs, dos, qs = [], [], [], [], []
        for h in range(3):
            q = query_of(b, h)
            do = one_head(r.do_recv[b, :, 0:128] if h < 2 else r.do_recv[b, :, 128:256], h > 0)
            scores = jnp.where(allowed, nt(keys_of(b, h), q), NEG)
            probs = jnp.exp(scores - r.lse[b, h : h + 1, :])
            dw = nt(values_of(b, h), do)
            centre = jnp.sum(probs * dw, axis=0, keepdims=True)
            ds = (probs * (dw - centre)).astype(BF)
            dqs.append(nn(r.kvt[K_ROWS[h] : K_ROWS[h] + 64, 0:n], ds))
            dss.append(ds)
            pbs.append(probs.astype(BF))
            dos.append(do)
            qs.append(q)
        dqs.append(jnp.zeros((64, TOK), F32))
        r.dq[b] = (jnp.concatenate(dqs, axis=0) * 0.125).T.astype(BF)
        r.dkv[0:n, 0:128] += pair(dss[0], dss[1], qs[0], qs[1])
        r.dkv[0:n, 128:256] += pair(dss[2], pbs[2], qs[2], dos[2])
        r.dkv[0:n, 256:384] += pair(pbs[0], pbs[1], dos[0], dos[1])
        other = pl.multiple_of(256 * b + TOK * (1 - me.c), TOK)
        r.dkv_sib[b] = r.dkv[pl.ds(other, TOK), :].astype(BF)
        copy_to(sib, r.dkv_sib.at[b], r.dkv_got.at[b], "dkv", recv=("dkv", b)).start()
        if b == 1:
            arrived(r.gzy, "hidden y")
            total = r.gz0[me.yl, me.yh].astype(F32)
            for d in range(3):
                total += r.gzy[d].astype(F32)
            r.gzx[...] = total.astype(BF)
            for d in (1, 3, 2):
                to = shifted(me, "x", d)
                copy_to(to, r.gzx.at[to.x], r.gy.at[d - 1], "hidden x").start()
            sent(r.gy, "hidden x")
        if b < 3:
            finish_block(b + 1)
    finish_block(0)
    arrived(r.fallt_sib, "first")
    for half in range(2):
        sums = col_sums(r.dpad[half].reshape(4 * TOK, SHARD))
        row = MIXER_BIAS + half
        r.vg[me.z, row : row + 1, 0:96] = sums[:, 0:96]
        r.vg[4 + me.z, row : row + 1, 0:96] = sums[:, 256:352]
    gain_a, shift_a = sum(gain_sum), sum(shift_sum)
    for s in range(8):
        r.vg[s, FIRST_GAIN : FIRST_GAIN + 1, 0:96] = gain_a[:, 96 * s : 96 * s + 96]
        r.vg[s, FIRST_SHIFT : FIRST_SHIFT + 1, 0:96] = shift_a[:, 96 * s : 96 * s + 96]

    for k in range(1, 8):
        to = seq_peer(k)
        copy_to(to, r.vg.at[to.z * 2 + to.yl], r.vr.at[k - 1], "rows").start()
    sent(r.vr, "rows")
    send_block(0, r.df_send.at[0])

    arrived(r.dpad_sib, "dpad")
    sent(r.dpad, "dpad")
    left = jnp.concatenate([r.fallt[:, me.c].reshape(D // 2, 4 * TOK), r.fallt_sib[...].reshape(D // 2, 4 * TOK)], axis=1)
    for half in range(2):
        right = [ref[half].reshape(4 * TOK, SHARD) for ref in (r.dpad, r.dpad_sib)]
        r.rm0[half] = nn(left, jnp.concatenate(right, axis=0)).astype(BF).reshape(2, 4, 48, SHARD)
    plane_send(r.rm0, r.rmx, "mixer")
    r.m_t[...] = plane_total(r.m_r0, r.m_x, "merge")
    for i, (dz, dy) in enumerate(around):
        to = shifted(shifted(me, "z", dz), "y", dy)
        copy_to(to, r.m_t.at[to.z, to.yl, to.yh], r.m_y.at[i], "merge all").start()
    sent(r.m_y, "merge all")
    take_along("res_recv")
    result = r.mid[me.z] + whole(SHRINK_BIAS)
    for b in range(4):
        result += r.res_recv[b].astype(F32)
    r.hid[...] = result.astype(BF)
    send_back(r.hid, r.hid_recv, "hid")
    arrived(r.vr, "rows")
    total = r.vg[seq]
    for k in range(7):
        total += r.vr[k]
    ours = me.yh * 8 + me.x * 2 + me.c
    r.vx[ours] = total
    others = [(at, dx, dy) for at in (me, sib) for dx in range(4) for dy in (0, 2) if dx or dy or at is sib]
    for at, dx, dy in others:
        copy_to(shifted(shifted(at, "x", dx), "y", dy), r.vx.at[ours], r.vx.at[ours], "rows all").start()
    sent(r.vx.at[0:15], "rows all")
    r.rmy[...] = plane_total(r.rm0, r.rmx, "mixer")
    for dyh in range(2):
        yh = lax.rem(me.yh + dyh, 2)
        for half in range(2):
            for kind in range(3):
                u = 8 * kind + 2 * me.z + half
                owner = lax.div(u, 3)
                to = moved(me, yh=yh, z=lax.div(owner, 2), yl=lax.rem(owner, 2))
                src = r.rmy.at[half, yh, :, pl.ds(TOK * kind, TOK)]
                dst = r.rmf.at[lax.rem(u, 3), ypos]
                if dyh:
                    copy_to(to, src, dst, "piece").start()
                else:
                    start_unless(owner == seq, to, src, dst, "piece", half, kind, recv=("piece",))
                    sent_unless(owner == seq, r.units.at[0], "piece", half, kind)
    sent(r.rmf.at[:, 0:2], "piece")
    d_first = jnp.zeros((TOK, D), F32)
    take_blocks()
    for b in range(4):
        d_first += r.df_recv[b].astype(F32)
    arrived(r.dmid_recv, "dmid")
    r.gin[...] = r.dmid_recv[...] + norm_back(d_first, gain1, r.n1[...], rstd1)

    arrived(r.hid_recv, "hid")
    r.hidden[...] = r.hid_recv[...]
    arrived(r.gy, "hidden x")
    total = r.gzx[me.x].astype(F32)
    for d in range(3):
        total += r.gy[d].astype(F32)
    r.gexp[...] = total[:, 0:SHARD]
    r.gshr[...] = total[:, SHARD:WIDE]
    arrived(r.m_y, "merge all")
    total = r.m_t[me.z, me.yl, me.yh].astype(F32)
    for i in range(15):
        total += r.m_y[i].astype(F32)
    r.gmerge[...] = total[:, 0:96]
    arrived(r.vx.at[0:15], "rows all")
    total = r.vx[0]
    for k in range(1, 16):
        total += r.vx[k]
    r.vout[...] = total
    arrived(r.rmf, "piece")
    for i in range(3):
        total = jnp.zeros((48, TOK), F32)
        for y in range(4):
            total += r.rmf[i, y].astype(F32)
        r.gmix[:, 96 * i : 96 * i + 96] = total[:, 0:96]
    for finish in pending:
        finish()
    if (len(sends), len(recvs)) != (SENDS, RECVS):
        raise ValueError((len(sends), len(recvs)))


def scratches():
    v, dma = pltpu.VMEM, pltpu.SemaphoreType.DMA
    blocks = (2, 4, 2, 48)
    s = dict(
        m_w=v((4, 2) + blocks + (TOK,), BF),
        m_g=v((4, 2) + blocks + (TOK,), BF),
        m_r0=v((4, 2, 2, 4, 48, TOK), BF),
        m_x=v((3, 4, 2, 2, 48, TOK), BF),
        m_t=v((4, 2, 2, 48, TOK), BF),
        m_y=v((15, 48, TOK), BF),
        mc=v((D, D), BF),
        wz=v((2,) + blocks + (WIDE,), BF),
        gz=v((2,) + blocks + (WIDE,), BF),
        gz0=v((2, 2, 4, 48, WIDE), BF),
        gzx=v((4, 48, WIDE), BF),
        gzy=v((3, 4, 48, WIDE), BF),
        gy=v((3, 48, WIDE), BF),
        units=v((3, 48, TOK), BF),
        wm=v((2,) + blocks + (SHARD,), BF),
        rm0=v((2, 2, 4, 48, SHARD), BF),
        rmx=v((3, 2, 2, 48, SHARD), BF),
        rmy=v((2, 2, 48, SHARD), BF),
        rmf=v((3, 4, 48, TOK), BF),
        vecs=v((8, 16, TOK), F32),
        segs=v((2, 8, TOK), F32),
        fallt=v((8, 2, 48, 4 * TOK), BF),
        fallt_sib=v((8, 48, 4 * TOK), BF),
        cott=v((D, 4 * TOK), BF),
        secondt=v((D, 4 * TOK), BF),
        attt=v((D, TOK), BF),
        q_all=v((4, TOK, 256), BF),
        kv_all=v((4, 2, TOK, SHARD), BF),
        kvt=v((SHARD, 8 * TOK), BF),
        lse=v((4, 8, TOK), F32),
        att_all=v((4, 6, TOK, TOK), BF),
        dkv=v((8 * TOK, SHARD), F32),
        dkv_sib=v((4, TOK, SHARD), BF),
        dkv_got=v((4, TOK, SHARD), BF),
        dq=v((4, TOK, 256), BF),
        dpad=v((2, 4, TOK, SHARD), BF),
        dpad_sib=v((2, 4, TOK, SHARD), BF),
        do_send=v((4, TOK, 256), BF),
        do_recv=v((4, TOK, 256), BF),
        n1all=v((4, TOK, D), F32),
        mid=v((4, TOK, D), F32),
    )
    for name in ("xall", "call", "fall", "att", "second", "dsec_send", "dsec", "res_send", "res_recv", "df_send", "df_recv"):
        s[name] = v((4, TOK, D), BF)
    for name in ("active", "dpre"):
        s[name] = v((4, TOK, WIDE), BF)
    for name in ("n1", "dmid", "dmid_recv"):
        s[name] = v((TOK, D), F32)
    for name in ("dbr", "hid", "hid_recv"):
        s[name] = v((TOK, D), BF)
    for name, count in (("vg", 8), ("vr", 7), ("vx", 16)):
        s[name] = v((count, 16, TOK), F32)
    s["send"], s["recv"] = dma((SENDS,)), dma((RECVS,))
    return s


def finish(hidden, gin, gmix, gmerge, gexp, gshr, vout, *outs):
    for ref, out in zip((hidden, gin, gmix, gmerge, gexp, gshr), outs[:6], strict=True):
        out[...] = ref[...]
    v = vout[...]
    rows = (FIRST_GAIN, FIRST_SHIFT, MERGE_BIAS, SECOND_GAIN, SECOND_SHIFT, SHRINK_BIAS)
    for row, out in zip(rows, outs[6:12], strict=True):
        out[...] = v[row : row + 1, 0:96].reshape(96)
    outs[12][...] = lanes(v[MIXER_BIAS : MIXER_BIAS + 1, 0:96], v[MIXER_BIAS + 1 : MIXER_BIAS + 2, 0:96]).reshape(192)
    outs[13][...] = lanes(*[v[EXPAND_BIAS + k : EXPAND_BIAS + k + 1] for k in range(3)]).reshape(SHARD)


def body(
    residual_in, cotangent, segments, first_gain, first_shift, mixer_weight, mixer_bias, merge_weight, merge_bias,
    second_gain, second_shift, expand_weight, expand_bias, shrink_weight, shrink_bias,
):
    vmem = pl.BlockSpec(memory_space=pltpu.VMEM)
    scratch = scratches()
    shapes = [((TOK, D), BF), ((TOK, D), F32), ((48, 288), F32), ((48, 96), F32), ((48, SHARD), F32), ((48, SHARD), F32)]
    held = [jax.ShapeDtypeStruct(*s) for s in shapes]
    parts = pl.pallas_call(
        functools.partial(kernel, IN + OUT + tuple(scratch)),
        out_shape=held + [jax.ShapeDtypeStruct((16, TOK), F32)],
        in_specs=[vmem] * len(IN),
        out_specs=[vmem] * len(OUT),
        scratch_shapes=list(scratch.values()),
        compiler_params=pltpu.CompilerParams(
            collective_id=0, has_side_effects=True, vmem_limit_bytes=62 * 1024 * 1024
        ),
    )(
        residual_in[0], cotangent[0], segments.reshape(8, TOK), mixer_weight, merge_weight, expand_weight,
        shrink_weight.T, first_gain, first_shift, mixer_bias, merge_bias, second_gain, second_shift, expand_bias,
        shrink_bias,
    )
    vectors = [jax.ShapeDtypeStruct((n,), F32) for n in (96, 96, 96, 96, 96, 96, 192, SHARD)]
    hidden, gin, gmix, gmerge, gexp, gshr, fg, fs, mb, sg, ss, sb, xb, eb = pl.pallas_call(
        finish, out_shape=held + vectors, in_specs=[vmem] * 7, out_specs=[vmem] * 14
    )(*parts)
    return hidden[None], gin[None], fg, fs, gmix, xb, gmerge, mb, sg, ss, gexp, eb, gshr.T, sb


def solution(mesh):
    vector, matrix = P("seq"), P("dp", "seq")
    tokens = P("dp", "seq", None)
    return jax.shard_map(
        body,
        mesh=mesh,
        in_specs=(
            tokens, tokens, P("dp", None), vector, vector, matrix, vector, matrix, vector, vector, vector, matrix, vector,
            P("seq", "dp"), vector,
        ),
        out_specs=(
            tokens, tokens, vector, vector, matrix, vector, matrix, vector, vector, vector, matrix, vector,
            P("seq", "dp"), vector,
        ),
        check_vma=False,
    )
```

```python
import functools
import types

import jax
import jax.numpy as jnp
from jax import lax
from jax.experimental import pallas as pl
from jax.experimental.pallas import tpu as pltpu
from jax.sharding import PartitionSpec as P


D = 768
HD = 64
TOK = 128
SHARD = 384
WIDE = 768
EPS = 1e-05
NEG = -1e30
MESH = pl.DeviceIdType.MESH
BF = jnp.bfloat16
F32 = jnp.float32
SENDS, RECVS = 47, 49
FIRST_GAIN, FIRST_SHIFT, MIXER_BIAS, MERGE_BIAS, SECOND_GAIN, SECOND_SHIFT, SHRINK_BIAS, EXPAND_BIAS = 0, 1, 2, 4, 5, 6, 7, 8


def place_of():
    dp, seq = lax.axis_index("dp"), lax.axis_index("seq")
    return types.SimpleNamespace(
        x=lax.rem(lax.div(dp, 2), 4),
        yh=lax.div(dp, 8),
        yl=lax.rem(seq, 2),
        z=lax.div(seq, 2),
        c=lax.rem(dp, 2),
    )


def moved(at, **to):
    new = types.SimpleNamespace(**vars(at))
    for name, value in to.items():
        setattr(new, name, value)
    return new


def shifted(at, axis, d):
    d = d % 4
    if axis == "x":
        return moved(at, x=lax.rem(at.x + d, 4))
    if axis == "z":
        return moved(at, z=lax.rem(at.z + d, 4))
    y = lax.rem(at.yh * 2 + at.yl + d, 4)
    return moved(at, yh=lax.div(y, 2), yl=lax.rem(y, 2))


def device(at):
    return (at.yh * 8 + at.x * 2 + at.c, at.z * 2 + at.yl)


def nn(a, b):
    return jnp.dot(a, b, preferred_element_type=F32)


def nt(a, b):
    return lax.dot_general(a, b, (((1,), (1,)), ((), ())), preferred_element_type=F32)


def remote(src, dst, send, recv, to):
    return pltpu.make_async_remote_copy(
        src_ref=src, dst_ref=dst, send_sem=send, recv_sem=recv, device_id=device(to), device_id_type=MESH
    )


def norm_parts(v):
    centred = v - jnp.mean(v, axis=-1, keepdims=True)
    rstd = lax.rsqrt(jnp.mean(centred * centred, axis=-1, keepdims=True) + EPS)
    return centred * rstd, rstd


def norm_back(dy, gain, normed, rstd):
    dn = dy * gain
    return rstd * (
        dn
        - jnp.mean(dn, axis=-1, keepdims=True)
        - normed * jnp.mean(dn * normed, axis=-1, keepdims=True)
    )


def col_sums(v):
    return jnp.sum(v.astype(F32), axis=0, keepdims=True)


def turned(v):
    return v.astype(F32).T.astype(BF)


def lanes(*pieces):
    return jnp.concatenate(pieces, axis=1)


def tile(k):
    return pl.ds(pl.multiple_of(k * TOK, TOK), TOK)


IN = (
    "x_in", "cot_in", "seg_in", "mixer_in", "merge_in", "expand_in", "shrink_in", "fgain_in", "fshift_in", "mixb_in",
    "mergeb_in", "sgain_in", "sshift_in", "expandb_in", "shrinkb_in",
)
OUT = ("hidden", "gin", "gmix", "gmerge", "gexp", "gshr", "vout")


def kernel(names, *refs):
    r = types.SimpleNamespace(**dict(zip(names, refs, strict=True)))
    me = place_of()
    sib = moved(me, c=1 - me.c)
    swap = moved(me, yl=me.c, c=me.yl)
    here = me.yl == me.c
    seq = me.z * 2 + me.yl
    ypos = me.yh * 2 + me.yl
    pending = []
    sends, recvs = {}, {}

    def send_of(*key):
        return r.send.at[sends.setdefault(key, len(sends))]

    def recv_of(*key):
        return r.recv.at[recvs.setdefault(key, len(recvs))]

    def copy_to(to, src, dst, *key, recv=None):
        return remote(src, dst, send_of(*key), recv_of(*(recv or key)), to)

    def arrived(size, *key):
        remote(size, size, r.send.at[0], recv_of(*key), sib).wait_recv()

    def wait_sent(size, *key):
        remote(size, size, send_of(*key), r.recv.at[0], sib).wait_send()

    def sent(size, *key):
        pending.append(lambda: wait_sent(size, *key))

    def sent_unless(alone, size, *key):
        def finish():
            @pl.when(jnp.logical_not(alone))
            def _():
                wait_sent(size, *key)

        pending.append(finish)

    def start_unless(alone, to, src, dst, *key, recv=None):
        @pl.when(alone)
        def _():
            pltpu.make_async_copy(src, dst, recv_of(*(recv or key))).start()

        @pl.when(jnp.logical_not(alone))
        def _():
            copy_to(to, src, dst, *key, recv=recv).start()

    zero32 = jnp.zeros((48, 32), BF)
    for i in range(3):
        r.units[i] = lanes(r.mixer_in[:, 96 * i : 96 * i + 96], zero32)
    own = (me.z, me.yl, me.yh, me.x, me.c)
    r.wz[own[1:]] = lanes(r.expand_in[...], r.shrink_in[...])
    r.m_w[own[0:3]] = lanes(r.merge_in[...], zero32)
    mixb = r.mixb_in[...].astype(F32).reshape(1, 192)
    small = [(FIRST_GAIN, r.fgain_in), (FIRST_SHIFT, r.fshift_in), (MERGE_BIAS, r.mergeb_in)]
    small += [(SECOND_GAIN, r.sgain_in), (SECOND_SHIFT, r.sshift_in), (SHRINK_BIAS, r.shrinkb_in)]
    for row, ref in small:
        r.vecs[seq, row : row + 1, 0:96] = ref[...].astype(F32).reshape(1, 96)
    expb = r.expandb_in[...].astype(F32).reshape(1, SHARD)
    for k in range(2):
        r.vecs[seq, MIXER_BIAS + k : MIXER_BIAS + k + 1, 0:96] = mixb[:, 96 * k : 96 * k + 96]
    for k in range(3):
        r.vecs[seq, EXPAND_BIAS + k : EXPAND_BIAS + k + 1, :] = expb[:, TOK * k : TOK * k + TOK]
    r.segs[0] = r.seg_in[...].astype(F32)

    peers = [shifted(shifted(me, "z", dz), "y", dy) for dz in range(4) for dy in range(4) if dz or dy]
    peers += [shifted(me, "x", d) for d in (1, 2, 3)] + [sib, shifted(sib, "y", 2)]
    peers += [moved(shifted(me, "z", d), yl=1 - me.yl, c=1 - me.c) for d in range(4)]
    peers += [shifted(shifted(at, "x", d), "y", dy) for d in (1, 2, 3) for at, dy in ((sib, 0), (me, 2), (sib, 2))]
    barrier = pltpu.get_barrier_semaphore()
    for p in peers:
        pl.semaphore_signal(barrier, inc=1, device_id=device(p), device_id_type=MESH)
    pl.semaphore_wait(barrier, len(peers))

    def send_own(name):
        at = getattr(r, name).at[me.z]
        for d in (1, 3, 2):
            copy_to(shifted(me, "z", d), at, at, name).start()

    def send_along(name, src_of, order=(1, 3, 2)):
        for d in order:
            to = shifted(me, "z", d)
            copy_to(to, src_of(to.z), getattr(r, name).at[me.z], name).start()

    def take_along(name):
        arrived(getattr(r, name).at[0:3], name)
        sent(getattr(r, name).at[0:3], name)

    def send_back(src, dst, key):
        start_unless(here, swap, src, dst, key)
        sent_unless(here, src, key)

    for i in range(3):
        u = 3 * seq + i
        group = lax.div(lax.rem(u, 8), 2)
        dst = r.wm.at[lax.rem(u, 2), me.yh, me.x, me.c, :, tile(lax.div(u, 8))]
        for dy in range(4):
            y = lax.rem(ypos + dy, 4)
            to = moved(me, z=group, yh=lax.div(y, 2), yl=lax.rem(y, 2))
            if dy:
                copy_to(to, r.units.at[i], dst, "unit").start()
            else:
                start_unless(group == me.z, to, r.units.at[i], dst, "unit", i, recv=("unit",))
        sent_unless(group == me.z, r.units.at[i], "unit", i)
    sent(r.rmf.at[:, 0:3], "unit")

    send_back(r.x_in, r.xall.at[me.z], "x")

    @pl.when(here)
    def _():
        arrived(r.xall.at[0], "x")
        send_own("xall")

    def seq_peer(k):
        at = shifted(me, "z", k // 2)
        return moved(at, yl=1 - me.yl) if k % 2 else at

    for k in range(1, 8):
        copy_to(seq_peer(k), r.vecs.at[seq], r.vecs.at[seq], "vec").start()
    sent(r.vr, "vec")

    def plane(ref, d):
        return ref.at[(slice(None),) * (len(ref.shape) - 4) + (lax.rem(me.x + 4 - d, 4), me.c)]

    def plane_start(ref, key):
        at = plane(ref, 0)
        for d in (1, 3, 2):
            copy_to(shifted(me, "x", d), at, at, key, recv=(key, d)).start()
        copy_to(sib, at, at, key, "hand").start()
        every = (slice(None),) * (len(ref.shape) - 4)
        sent(ref.at[every + (slice(0, 3), me.c)], key)
        sent(ref.at[every + (slice(0, 4), me.c)], key, "hand")

    def plane_hand(ref, key):
        for d in (1, 3, 2):
            at = plane(ref, d)
            arrived(at, key, d)
            copy_to(sib, at, at, key, "hand").start()

    def plane_finish(ref, key):
        every = (slice(None),) * (len(ref.shape) - 4)
        arrived(ref.at[every + (slice(0, 4), 1 - me.c)], key, "hand")

    def column(d):
        at = shifted(me, "y", -d)
        return r.wz.at[at.yl, at.yh, :, me.c]

    def column_start():
        for d in (1, 3, 2):
            copy_to(shifted(me, "y", d), column(0), column(0), "column", recv=("column", d)).start()
        copy_to(sib, column(0), column(0), "column", "hand").start()
        sent(r.wz.at[0, :, 0:3], "column")
        sent(r.wz.at[:, :, :, me.c], "column", "hand")

    def column_hand():
        for d in (1, 3, 2):
            arrived(column(d), "column", d)
            copy_to(sib, column(d), column(d), "column", "hand").start()

    def column_finish():
        arrived(r.wz.at[:, :, :, 1 - me.c], "column", "hand")

    copy_to(sib, r.segs.at[0], r.segs.at[1], "seg").start()
    sent(r.segs.at[0], "seg")
    own = r.wz.at[me.yl, me.yh, me.x, me.c]
    for d in (1, 3, 2):
        copy_to(shifted(me, "x", d), own, own, "hidden").start()
    sent(r.gy, "hidden")
    around = [(dz, dy) for dz in (1, 3, 0, 2) for dy in (0, 1, 3, 2) if dz or dy]
    at = r.m_w.at[me.z, me.yl, me.yh]
    for dz, dy in around:
        copy_to(shifted(shifted(me, "z", dz), "y", dy), at, at, "merge").start()
    sent(r.m_y, "merge")
    send_back(r.cot_in, r.call.at[me.z], "cot")
    arrived(r.wm.at[:, :, me.x, me.c], "unit")

    plane_start(r.wm, "mixer")
    @pl.when(jnp.logical_not(here))
    def _():
        arrived(r.xall.at[0], "x")
        send_own("xall")

    arrived(r.gy, "hidden")
    column_start()
    arrived(r.vr, "vec")

    def whole(row):
        return jnp.concatenate([r.vecs[s, row : row + 1, 0:96] for s in range(8)], axis=1)


    gain1, shift1 = whole(FIRST_GAIN), whole(FIRST_SHIFT)
    plane_hand(r.wm, "mixer")
    arrived(r.m_y, "merge")
    for yh in range(2):
        pieces = [r.m_w[s // 2, s % 2, yh, :, 0:96] for s in range(8)]
        r.mc[yh, me.x, me.c] = lanes(*pieces)
    plane_start(r.mc, "merge x")
    take_along("xall")
    arrived(r.call.at[0], "cot")
    send_own("call")
    for b in range(4):
        normed, rstd = norm_parts(r.xall[b].astype(F32))
        r.n1all[b] = normed
        r.rstd1[b] = jnp.broadcast_to(rstd, (TOK, TOK))
        first = normed * gain1 + shift1
        r.fall[b] = first.astype(BF)
        r.fallt[:, :, :, TOK * b : TOK * b + TOK] = turned(first.astype(BF)).reshape(8, 2, 48, TOK)
    plane_finish(r.wm, "mixer")

    at = r.fallt.at[:, 1 - me.c]
    copy_to(sib, at, r.fallt_sib, "first").start()
    sent(r.fallt_sib, "first")
    def mixer(half, first, count):
        at = slice(TOK * first, TOK * (first + count))
        return r.wm[half, :, :, :, :, at].reshape(D, TOK * count)

    first = r.fall[...].reshape(4 * TOK, D)

    def mixer_bias(at, half):
        row = MIXER_BIAS + half
        return r.vecs[at, row : row + 1, 0:96]

    kv0, kv1 = nn(first, mixer(0, 1, 2)), nn(first, mixer(1, 1, 2))
    keys = lanes(kv0[:, 0:96], kv1[:, 0:96]).astype(BF)
    vbias = lanes(mixer_bias(4 + me.z, 0), mixer_bias(4 + me.z, 1))
    values = (lanes(kv0[:, 128:224], kv1[:, 128:224]) + vbias).astype(BF)
    packed = lanes(keys, values[:, 128:192], values[:, 0:128])
    for b in range(4):
        r.kv_all[b, me.c] = packed[TOK * b : TOK * b + TOK]
    at = r.kv_all.at[:, me.c]
    copy_to(sib, at, at, "kv").start()
    sent(at, "kv")
    qbias = lanes(mixer_bias(me.z, 0), mixer_bias(me.z, 1))
    q = lanes(nn(first, mixer(0, 0, 1))[:, 0:96], nn(first, mixer(1, 0, 1))[:, 0:96])
    q = (q + qbias).astype(BF) * jnp.asarray(0.125, BF)
    q = lanes(q, jnp.zeros((4 * TOK, 64), BF))
    for b in range(4):
        r.q_all[b] = q[TOK * b : TOK * b + TOK]
        r.kvt[:, tile(2 * b + me.c)] = turned(packed[TOK * b : TOK * b + TOK])
    arrived(r.segs.at[1], "seg")
    arrived(r.kv_all.at[:, 1 - me.c], "kv")
    for b in range(4):
        r.kvt[:, tile(2 * b + 1 - me.c)] = turned(r.kv_all[b, 1 - me.c])

    seg = jnp.where(here, r.segs[0], r.segs[1])

    def starts(bound):
        return jnp.sum(jnp.where(seg < bound, 1.0, 0.0), axis=(0, 1), keepdims=True).astype(jnp.int32)

    begin1, begin2 = starts(0.5), starts(1.5)
    lane = lax.broadcasted_iota(jnp.int32, (TOK, TOK), 1)

    def allowed_of(b):
        n = 256 * (b + 1)
        qpos = 256 * b + TOK * me.c + lax.broadcasted_iota(jnp.int32, (1, TOK), 1)
        low = jnp.where(qpos < begin1, 0, jnp.where(qpos < begin2, begin1, begin2))
        kpos = lax.broadcasted_iota(jnp.int32, (n, TOK), 0)
        return (kpos <= qpos) & (kpos >= low)

    def keys_of(b, h):
        at = slice(0, 128) if h < 2 else slice(128, 256)
        return r.kv_all[0 : b + 1, :, :, at].reshape(256 * (b + 1), TOK)

    def values_of(b, h):
        at = slice(256, 384) if h < 2 else slice(128, 256)
        return r.kv_all[0 : b + 1, :, :, at].reshape(256 * (b + 1), TOK)

    K_ROWS = (0, 64, 128)
    V_ROWS = (256, 320, 192)

    def one_head(v, upper):
        keep = lane >= 64 if upper else lane < 64
        return jnp.where(keep, v, jnp.zeros_like(v))

    def query_of(b, h):
        return one_head(r.q_all[b, :, 0:128] if h < 2 else r.q_all[b, :, 128:256], h == 1)

    spare = []
    for b in (3, 2, 1, 0):
        n = 256 * (b + 1)
        allowed = allowed_of(b)
        outs = []
        for h in range(3):
            scores = jnp.where(allowed, nt(keys_of(b, h), query_of(b, h)), NEG)
            top = jnp.max(scores, axis=0, keepdims=True)
            expo = jnp.exp(scores - top)
            total = jnp.sum(expo, axis=0, keepdims=True)
            r.lse[b, h : h + 1, :] = top + jnp.log(total)
            weights = (expo * (1.0 / total)).astype(BF)
            outs.append(nn(r.kvt[V_ROWS[h] : V_ROWS[h] + 64, 0:n], weights))
        r.att_all[me.z, b] = jnp.concatenate(outs[0:2], axis=0).T.astype(BF)
        spare.append(outs[2])
        ready = [b]
        if b % 2 == 0:
            r.att_all[me.z, 4 + b // 2] = jnp.concatenate([spare[-1], spare[-2]], axis=0).T.astype(BF)
            ready.append(4 + b // 2)
        for k in ready:
            for d in (1, 3, 2):
                at = r.att_all.at[me.z, k]
                copy_to(shifted(me, "z", d), at, at, "att", recv=("att", b // 2)).start()
        if b == 1:
            column_hand()
        if b == 0:
            plane_hand(r.mc, "merge x")
    sent(r.att_all.at[0:3], "att")
    take_along("call")
    for b in range(4):
        r.cott[:, TOK * b : TOK * b + TOK] = turned(r.call[b])
    plane_finish(r.mc, "merge x")
    merge = r.mc[...].reshape(D, D)

    column_finish()
    gain2, shift2, b_merge = whole(SECOND_GAIN), whole(SECOND_SHIFT), whole(MERGE_BIAS)

    def hidden(first):
        return lanes(*[r.wz[yl, :, :, :, :, first : first + SHARD].reshape(D, SHARD) for yl in range(2)])

    bias = lanes(*[r.vecs[2 * me.z + yl, EXPAND_BIAS + k : EXPAND_BIAS + k + 1] for yl in range(2) for k in range(3)])
    sums2 = []
    for pair in (1, 0):
        arrived(r.att_all.at[0:3, 0:3], "att", pair)
        rows = slice(2 * pair, 2 * pair + 2)
        for b in (2 * pair, 2 * pair + 1):
            at = slice(64 * (b % 2), 64 * (b % 2) + 64)
            r.att[b] = lanes(*[v for g in range(4) for v in (r.att_all[g, b], r.att_all[g, 4 + pair, :, at])])
        branch = nn(r.att[rows].reshape(2 * TOK, D), merge)
        middle = r.xall[rows].reshape(2 * TOK, D).astype(F32) + branch + b_merge
        r.mid[rows] = middle.reshape(2, TOK, D)
        n2, rstd2 = norm_parts(middle)
        second = (n2 * gain2 + shift2).astype(BF)
        r.second[rows] = second.reshape(2, TOK, D)
        pre = nn(second, hidden(0)) + bias
        square = pre * pre
        tanh = jnp.tanh(0.7978845608028654 * (pre + 0.044715 * square * pre))
        r.active[rows] = (0.5 * pre * (1.0 + tanh)).astype(BF).reshape(2, TOK, WIDE)
        slope = 0.5 * (1.0 + tanh) + 0.5 * pre * (1.0 - tanh * tanh) * (
            0.7978845608028654 * (1.0 + 0.134145 * square)
        )
        cot = r.call[rows]
        d_pre = (nn(cot.reshape(2 * TOK, D), hidden(SHARD)) * slope).astype(BF)
        r.dpre[rows] = d_pre.reshape(2, TOK, WIDE)
        d_second = nt(d_pre, hidden(0))
        sums2.append((col_sums(d_second * n2), col_sums(d_second)))
        d_middle = norm_back(d_second, gain2, n2, rstd2)
        d_branch = []
        for i in range(2):
            own = jnp.where(me.z == 2 * pair + i, cot[i].astype(F32), 0.0) + d_middle[TOK * i : TOK * i + TOK]
            r.dmid[2 * pair + i] = own
            d_branch.append(own.astype(BF))
            r.dbr[2 * pair + i] = d_branch[-1]
        d_att = nt(jnp.concatenate(d_branch, axis=0), merge).astype(BF)
        low, high = d_att[0:TOK], d_att[TOK : 2 * TOK]
        for z in range(4):
            at = 192 * z
            r.do_send[pair, z, 0] = low[:, at : at + 128]
            r.do_send[pair, z, 1] = high[:, at : at + 128]
            r.do_send[pair, z, 2] = lanes(low[:, at + 128 : at + 192], high[:, at + 128 : at + 192])
        for d in (1, 3, 2):
            to = shifted(me, "z", d)
            copy_to(to, r.do_send.at[pair, to.z], r.do_recv.at[pair, me.z], "do", recv=("do", pair)).start()
        r.do_recv[pair, me.z] = r.do_send[pair, me.z]
    sent(r.do_send.at[:, 0:3], "do")

    zeros = jnp.zeros((TOK, 32), BF)

    for b in range(4):
        r.attt[:, TOK * b : TOK * b + TOK] = turned(r.att[b])
    grad = nn(r.attt[...], r.dbr[...].reshape(4 * TOK, D)).astype(BF)
    r.m_g[...] = grad.reshape(2, 4, 2, 48, D)
    copy_to(sib, r.m_g.at[:, :, 1 - me.c], r.m_r0, "merge", "pair").start()
    sent(r.m_r0, "merge", "pair")

    sums = col_sums(r.dpre[...].reshape(4 * TOK, WIDE))
    r.vg[...] = jnp.zeros((8, 16, TOK), F32)
    for yl in range(2):
        for k in range(3):
            at = TOK * (3 * yl + k)
            r.vg[2 * me.z + yl, EXPAND_BIAS + k : EXPAND_BIAS + k + 1, :] = sums[:, at : at + TOK]
    for b in range(4):
        r.secondt[:, TOK * b : TOK * b + TOK] = turned(r.second[b])
    halves = ((r.g_e, r.g_e0), (r.g_s, r.g_s0))

    def hidden_gradient(k, left, right):
        ref, pair0 = halves[k]
        grad = nn(left[...], right[...].reshape(4 * TOK, WIDE)).astype(BF)
        for yl in range(2):
            ref[yl] = grad[:, SHARD * yl : SHARD * yl + SHARD].reshape(2, 4, 2, 48, SHARD)
        copy_to(sib, ref.at[:, :, :, 1 - me.c], pair0, "hidden", k, "pair").start()
        sent(pair0, "hidden", k, "pair")

    hidden_gradient(0, r.secondt, r.dpre)

    hidden_gradient(1, r.cott, r.active)
    result = nt(r.active[...].reshape(4 * TOK, WIDE), hidden(SHARD)).astype(BF)
    for b in range(4):
        r.res_send[b] = result[TOK * b : TOK * b + TOK]
    send_along("res_recv", lambda z: r.res_send.at[z])
    r.res_recv[me.z] = r.res_send[me.z]

    def pair_sum(ref, own, key):
        arrived(ref, *key, "pair")
        every = (slice(None),) * (len(ref.shape) - 2)
        ref[...] = (ref[...].astype(F32) + own[every + (me.c,)].astype(F32)).astype(BF)

    def plane_send(ref, got, key):
        every = (slice(None),) * (len(ref.shape) - 3)
        for d in (1, 3, 2):
            to = shifted(me, "x", d)
            copy_to(to, ref.at[every + (to.x,)], got.at[d - 1], key, "sum").start()
        sent(got, key, "sum")

    def plane_total(ref, got, key):
        arrived(got, key, "sum")
        total = ref[(slice(None),) * (len(ref.shape) - 3) + (me.x,)].astype(F32)
        for d in range(3):
            total += got[d].astype(F32)
        return total.astype(BF)

    def expand_sum():
        pair_sum(r.g_e0, r.g_e, ("hidden", 0))
        for d in (1, 3, 2):
            to = shifted(me, "y", d)
            copy_to(to, r.g_e0.at[to.yl, to.yh], r.g_ey.at[d - 1], "expand y").start()
        sent(r.g_ey, "expand y")

    def shrink_sum():
        pair_sum(r.g_s0, r.g_s, ("hidden", 1))
        plane_send(r.g_s0, r.g_sx, "shrink")

    pair_sum(r.m_r0, r.m_g, ("merge",))
    plane_send(r.m_r0, r.m_x, "merge")
    expand_sum()
    r.dkv[...] = jnp.zeros((8 * TOK, SHARD), F32)
    sent(r.dkv_got, "dkv")

    def take_pair(p):
        arrived(r.do_recv.at[p, 0:3], "do", p)
        total = r.do_recv[p, 0].astype(F32)
        for z in range(1, 4):
            total += r.do_recv[p, z].astype(F32)
        r.do_all[2 * p, :, 0:TOK] = total[0].astype(BF)
        r.do_all[2 * p, :, TOK : 2 * TOK] = lanes(total[2, :, 64:128], total[2, :, 0:64]).astype(BF)
        r.do_all[2 * p + 1, :, 0:TOK] = total[1].astype(BF)
        r.do_all[2 * p + 1, :, TOK : 2 * TOK] = total[2].astype(BF)

    def pair(l0, l1, r0, r1):
        return nn(jnp.concatenate([l0, l1], axis=1), jnp.concatenate([r0, r1], axis=0))

    gain_sum, shift_sum = [], []

    def finish_block(b):
        arrived(r.dkv_got.at[b], "dkv", b)
        own = pl.multiple_of(256 * b + TOK * me.c, TOK)
        dkv = (r.dkv[pl.ds(own, TOK), :] + r.dkv_got[b].astype(F32)).astype(BF)
        dq = r.dq[b]
        dv = lanes(dkv[:, 256:384], dkv[:, 192:256])
        for half in range(2):
            at = slice(96 * half, 96 * half + 96)
            r.dpad[half, b] = lanes(dq[:, at], zeros, dkv[:, at], zeros, dv[:, at], zeros)
        at = r.dpad.at[:, b]
        copy_to(sib, at, r.dpad_sib.at[:, b], "dpad").start()

    def first_back(p):
        rows = slice(2 * p, 2 * p + 2)
        d_first = nt(r.dpad[0, rows].reshape(2 * TOK, SHARD), mixer(0, 0, 3))
        d_first += nt(r.dpad[1, rows].reshape(2 * TOK, SHARD), mixer(1, 0, 3))
        for i in range(2):
            b = 2 * p + i
            part, normed = d_first[TOK * i : TOK * i + TOK], r.n1all[b]
            gain_sum.append(col_sums(part * normed))
            shift_sum.append(col_sums(part))
            r.df_send[b] = (r.dmid[b] + norm_back(part, gain1, normed, r.rstd1[b][:, 0:1])).astype(BF)

    for b in (3, 2, 1, 0):
        if b % 2:
            take_pair(b // 2)
        n = 256 * (b + 1)
        allowed = allowed_of(b)
        dqs, dss, pbs, dos, qs = [], [], [], [], []
        for h in range(3):
            q = query_of(b, h)
            do = one_head(r.do_all[b, :, 0:128] if h < 2 else r.do_all[b, :, 128:256], h > 0)
            scores = jnp.where(allowed, nt(keys_of(b, h), q), NEG)
            probs = jnp.exp(scores - r.lse[b, h : h + 1, :])
            dw = nt(values_of(b, h), do)
            centre = jnp.sum(probs * dw, axis=0, keepdims=True)
            ds = (probs * (dw - centre)).astype(BF)
            dqs.append(nn(r.kvt[K_ROWS[h] : K_ROWS[h] + 64, 0:n], ds))
            dss.append(ds)
            pbs.append(probs.astype(BF))
            dos.append(do)
            qs.append(q)
        dqs.append(jnp.zeros((64, TOK), F32))
        r.dq[b] = (jnp.concatenate(dqs, axis=0) * 0.125).T.astype(BF)
        r.dkv[0:n, 0:128] += pair(dss[0], dss[1], qs[0], qs[1])
        r.dkv[0:n, 128:256] += pair(dss[2], pbs[2], qs[2], dos[2])
        r.dkv[0:n, 256:384] += pair(pbs[0], pbs[1], dos[0], dos[1])
        other = pl.multiple_of(256 * b + TOK * (1 - me.c), TOK)
        r.dkv_sib[b] = r.dkv[pl.ds(other, TOK), :].astype(BF)
        copy_to(sib, r.dkv_sib.at[b], r.dkv_got.at[b], "dkv", recv=("dkv", b)).start()
        if b == 3:
            shrink_sum()
        if b == 2:
            finish_block(3)
        if b == 0:
            finish_block(1)
        if b % 2 == 0:
            finish_block(b)
            first_back(b // 2)
    total = plane_total(r.m_r0, r.m_x, "merge")
    for s in range(8):
        for yh in range(2):
            r.m_t[s // 2, s % 2, yh] = lanes(total[yh, :, 96 * s : 96 * s + 96], zero32)
    for i, (dz, dy) in enumerate(around):
        to = shifted(shifted(me, "z", dz), "y", dy)
        copy_to(to, r.m_t.at[to.z, to.yl, to.yh], r.m_y.at[i], "merge all").start()
    sent(r.m_y, "merge all")
    arrived(r.g_ey, "expand y")
    total = r.g_e0[me.yl, me.yh].astype(F32)
    for d in range(3):
        total += r.g_ey[d].astype(F32)
    r.g_ex[...] = total.astype(BF)
    for d in (1, 3, 2):
        to = shifted(me, "x", d)
        copy_to(to, r.g_ex.at[to.x], r.e_got.at[d - 1], "expand x").start()
    sent(r.e_got, "expand x")
    g_gain_b, g_shift_b = sums2[0][0] + sums2[1][0], sums2[0][1] + sums2[1][1]
    g_b_shrink = col_sums(r.call[me.z])
    g_b_merge = col_sums(r.dbr[...].reshape(4 * TOK, D))
    rows = [(MERGE_BIAS, g_b_merge), (SECOND_GAIN, g_gain_b), (SECOND_SHIFT, g_shift_b), (SHRINK_BIAS, g_b_shrink)]
    for s in range(8):
        for row, value in rows:
            r.vg[s, row : row + 1, 0:96] = value[:, 96 * s : 96 * s + 96]

    arrived(r.fallt_sib, "first")
    for half in range(2):
        sums = col_sums(r.dpad[half].reshape(4 * TOK, SHARD))
        row = MIXER_BIAS + half
        r.vg[me.z, row : row + 1, 0:96] = sums[:, 0:96]
        r.vg[4 + me.z, row : row + 1, 0:96] = sums[:, 256:352]
    gain_a, shift_a = sum(gain_sum), sum(shift_sum)
    for s in range(8):
        r.vg[s, FIRST_GAIN : FIRST_GAIN + 1, 0:96] = gain_a[:, 96 * s : 96 * s + 96]
        r.vg[s, FIRST_SHIFT : FIRST_SHIFT + 1, 0:96] = shift_a[:, 96 * s : 96 * s + 96]

    for k in range(1, 8):
        to = seq_peer(k)
        copy_to(to, r.vg.at[to.z * 2 + to.yl], r.vr.at[k - 1], "rows").start()
    sent(r.vr, "rows")
    send_along("df_recv", lambda z: r.df_send.at[z])
    r.df_recv[me.z] = r.df_send[me.z]

    arrived(r.dpad_sib, "dpad")
    sent(r.dpad, "dpad")
    left = jnp.concatenate([r.fallt[:, me.c].reshape(D // 2, 4 * TOK), r.fallt_sib[...].reshape(D // 2, 4 * TOK)], axis=1)
    for half in range(2):
        right = [ref[half].reshape(4 * TOK, SHARD) for ref in (r.dpad, r.dpad_sib)]
        r.rm0[half] = nn(left, jnp.concatenate(right, axis=0)).astype(BF).reshape(2, 4, 48, SHARD)
    plane_send(r.rm0, r.rmx, "mixer")
    take_along("res_recv")
    result = r.mid[me.z] + whole(SHRINK_BIAS)
    for b in range(4):
        result += r.res_recv[b].astype(F32)
    r.hid[...] = result.astype(BF)
    send_back(r.hid, r.hid_recv, "hid")
    arrived(r.vr, "rows")
    total = r.vg[seq]
    for k in range(7):
        total += r.vr[k]
    ours = me.yh * 8 + me.x * 2 + me.c
    r.vx[ours] = total
    others = [(at, dx, dy) for at in (me, sib) for dx in range(4) for dy in (0, 2) if dx or dy or at is sib]
    for at, dx, dy in others:
        copy_to(shifted(shifted(at, "x", dx), "y", dy), r.vx.at[ours], r.vx.at[ours], "rows all").start()
    sent(r.vx.at[0:15], "rows all")
    r.g_sy[...] = plane_total(r.g_s0, r.g_sx, "shrink")
    for d in (1, 3, 2):
        to = shifted(me, "y", d)
        copy_to(to, r.g_sy.at[to.yl, to.yh], r.s_got.at[d - 1], "shrink y").start()
    sent(r.s_got, "shrink y")
    r.rmy[...] = plane_total(r.rm0, r.rmx, "mixer")
    for dyh in range(2):
        yh = lax.rem(me.yh + dyh, 2)
        for half in range(2):
            for kind in range(3):
                u = 8 * kind + 2 * me.z + half
                owner = lax.div(u, 3)
                to = moved(me, yh=yh, z=lax.div(owner, 2), yl=lax.rem(owner, 2))
                src = r.rmy.at[half, yh, :, pl.ds(TOK * kind, TOK)]
                dst = r.rmf.at[lax.rem(u, 3), ypos]
                if dyh:
                    copy_to(to, src, dst, "piece").start()
                else:
                    start_unless(owner == seq, to, src, dst, "piece", half, kind, recv=("piece",))
                    sent_unless(owner == seq, r.units.at[0], "piece", half, kind)
    sent(r.rmf.at[:, 0:2], "piece")
    take_along("df_recv")
    r.gin_send[...] = sum(r.df_recv[b].astype(F32) for b in range(4)).astype(BF)
    send_back(r.gin_send, r.gin_recv, "gin")

    arrived(r.hid_recv, "hid")
    r.hidden[...] = r.hid_recv[...]
    arrived(r.e_got, "expand x")
    r.gexp[...] = r.g_ex[me.x].astype(F32) + sum(r.e_got[d].astype(F32) for d in range(3))
    arrived(r.s_got, "shrink y")
    r.gshr[...] = r.g_sy[me.yl, me.yh].astype(F32) + sum(r.s_got[d].astype(F32) for d in range(3))
    arrived(r.m_y, "merge all")
    total = r.m_t[me.z, me.yl, me.yh].astype(F32)
    for i in range(15):
        total += r.m_y[i].astype(F32)
    r.gmerge[...] = total[:, 0:96]
    arrived(r.gin_recv, "gin")
    r.gin[...] = r.gin_recv[...].astype(F32)
    arrived(r.vx.at[0:15], "rows all")
    total = r.vx[0]
    for k in range(1, 16):
        total += r.vx[k]
    r.vout[...] = total
    arrived(r.rmf, "piece")
    for i in range(3):
        total = jnp.zeros((48, TOK), F32)
        for y in range(4):
            total += r.rmf[i, y].astype(F32)
        r.gmix[:, 96 * i : 96 * i + 96] = total[:, 0:96]
    for finish in pending:
        finish()
    if (len(sends), len(recvs)) != (SENDS, RECVS):
        raise ValueError((len(sends), len(recvs)))


def scratches():
    v, dma = pltpu.VMEM, pltpu.SemaphoreType.DMA
    blocks = (2, 4, 2, 48)
    s = dict(
        m_w=v((4, 2, 2, 48, TOK), BF),
        m_g=v(blocks + (D,), BF),
        m_r0=v((2, 4, 48, D), BF),
        m_x=v((3, 2, 48, D), BF),
        m_t=v((4, 2, 2, 48, TOK), BF),
        m_y=v((15, 48, TOK), BF),
        mc=v(blocks + (D,), BF),
        wz=v((2,) + blocks + (WIDE,), BF),
        g_e=v((2,) + blocks + (SHARD,), BF),
        g_s=v((2,) + blocks + (SHARD,), BF),
        g_e0=v((2, 2, 4, 48, SHARD), BF),
        g_s0=v((2, 2, 4, 48, SHARD), BF),
        g_ey=v((3, 4, 48, SHARD), BF),
        g_ex=v((4, 48, SHARD), BF),
        g_sx=v((3, 2, 2, 48, SHARD), BF),
        g_sy=v((2, 2, 48, SHARD), BF),
        e_got=v((3, 48, SHARD), BF),
        s_got=v((3, 48, SHARD), BF),
        gy=v((3, 48, WIDE), BF),
        units=v((3, 48, TOK), BF),
        wm=v((2,) + blocks + (SHARD,), BF),
        rm0=v((2, 2, 4, 48, SHARD), BF),
        rmx=v((3, 2, 2, 48, SHARD), BF),
        rmy=v((2, 2, 48, SHARD), BF),
        rmf=v((3, 4, 48, TOK), BF),
        vecs=v((8, 16, TOK), F32),
        segs=v((2, 8, TOK), F32),
        fallt=v((8, 2, 48, 4 * TOK), BF),
        fallt_sib=v((8, 48, 4 * TOK), BF),
        cott=v((D, 4 * TOK), BF),
        secondt=v((D, 4 * TOK), BF),
        attt=v((D, 4 * TOK), BF),
        rstd1=v((4, TOK, TOK), F32),
        dmid=v((4, TOK, D), F32),
        q_all=v((4, TOK, 256), BF),
        kv_all=v((4, 2, TOK, SHARD), BF),
        kvt=v((SHARD, 8 * TOK), BF),
        lse=v((4, 8, TOK), F32),
        att_all=v((4, 6, TOK, TOK), BF),
        dkv=v((8 * TOK, SHARD), F32),
        dkv_sib=v((4, TOK, SHARD), BF),
        dkv_got=v((4, TOK, SHARD), BF),
        dq=v((4, TOK, 256), BF),
        dpad=v((2, 4, TOK, SHARD), BF),
        dpad_sib=v((2, 4, TOK, SHARD), BF),
        do_send=v((2, 4, 3, TOK, TOK), BF),
        do_recv=v((2, 4, 3, TOK, TOK), BF),
        do_all=v((4, TOK, 256), BF),
        n1all=v((4, TOK, D), F32),
        mid=v((4, TOK, D), F32),
    )
    for name in ("xall", "call", "fall", "att", "second", "dbr", "res_send", "res_recv", "df_send", "df_recv"):
        s[name] = v((4, TOK, D), BF)
    for name in ("active", "dpre"):
        s[name] = v((4, TOK, WIDE), BF)
    for name in ("hid", "hid_recv", "gin_send", "gin_recv"):
        s[name] = v((TOK, D), BF)
    for name, count in (("vg", 8), ("vr", 7), ("vx", 16)):
        s[name] = v((count, 16, TOK), F32)
    s["send"], s["recv"] = dma((SENDS,)), dma((RECVS,))
    return s


def finish(hidden, gin, gmix, gmerge, gexp, gshr, vout, *outs):
    for ref, out in zip((hidden, gin, gmix, gmerge, gexp, gshr), outs[:6], strict=True):
        out[...] = ref[...]
    v = vout[...]
    rows = (FIRST_GAIN, FIRST_SHIFT, MERGE_BIAS, SECOND_GAIN, SECOND_SHIFT, SHRINK_BIAS)
    for row, out in zip(rows, outs[6:12], strict=True):
        out[...] = v[row : row + 1, 0:96].reshape(96)
    outs[12][...] = lanes(v[MIXER_BIAS : MIXER_BIAS + 1, 0:96], v[MIXER_BIAS + 1 : MIXER_BIAS + 2, 0:96]).reshape(192)
    outs[13][...] = lanes(*[v[EXPAND_BIAS + k : EXPAND_BIAS + k + 1] for k in range(3)]).reshape(SHARD)


def body(
    residual_in, cotangent, segments, first_gain, first_shift, mixer_weight, mixer_bias, merge_weight, merge_bias,
    second_gain, second_shift, expand_weight, expand_bias, shrink_weight, shrink_bias,
):
    vmem = pl.BlockSpec(memory_space=pltpu.VMEM)
    scratch = scratches()
    shapes = [((TOK, D), BF), ((TOK, D), F32), ((48, 288), F32), ((48, 96), F32), ((48, SHARD), F32), ((48, SHARD), F32)]
    held = [jax.ShapeDtypeStruct(*s) for s in shapes]
    parts = pl.pallas_call(
        functools.partial(kernel, IN + OUT + tuple(scratch)),
        out_shape=held + [jax.ShapeDtypeStruct((16, TOK), F32)],
        in_specs=[vmem] * len(IN),
        out_specs=[vmem] * len(OUT),
        scratch_shapes=list(scratch.values()),
        compiler_params=pltpu.CompilerParams(
            collective_id=0, has_side_effects=True, vmem_limit_bytes=62 * 1024 * 1024
        ),
    )(
        residual_in[0], cotangent[0], segments.reshape(8, TOK), mixer_weight, merge_weight, expand_weight,
        shrink_weight.T, first_gain, first_shift, mixer_bias, merge_bias, second_gain, second_shift, expand_bias,
        shrink_bias,
    )
    vectors = [jax.ShapeDtypeStruct((n,), F32) for n in (96, 96, 96, 96, 96, 96, 192, SHARD)]
    hidden, gin, gmix, gmerge, gexp, gshr, fg, fs, mb, sg, ss, sb, xb, eb = pl.pallas_call(
        finish, out_shape=held + vectors, in_specs=[vmem] * 7, out_specs=[vmem] * 14
    )(*parts)
    return hidden[None], gin[None], fg, fs, gmix, xb, gmerge, mb, sg, ss, gexp, eb, gshr.T, sb


def solution(mesh):
    vector, matrix = P("seq"), P("dp", "seq")
    tokens = P("dp", "seq", None)
    return jax.shard_map(
        body,
        mesh=mesh,
        in_specs=(
            tokens, tokens, P("dp", None), vector, vector, matrix, vector, matrix, vector, vector, vector, matrix, vector,
            P("seq", "dp"), vector,
        ),
        out_specs=(
            tokens, tokens, vector, vector, matrix, vector, matrix, vector, vector, vector, matrix, vector,
            P("seq", "dp"), vector,
        ),
        check_vma=False,
    )
```

```python
import functools
import types

import jax
import jax.numpy as jnp
from jax import lax
from jax.experimental import pallas as pl
from jax.experimental.pallas import tpu as pltpu
from jax.sharding import PartitionSpec as P


D = 768
HD = 64
TOK = 128
SHARD = 384
HEADS3 = 640
WIDE = 768
EPS = 1e-05
NEG = -1e30
MESH = pl.DeviceIdType.MESH
BF = jnp.bfloat16
F32 = jnp.float32
SENDS, RECVS = 48, 50
FIRST_GAIN, FIRST_SHIFT, MIXER_BIAS, MERGE_BIAS, SECOND_GAIN, SECOND_SHIFT, SHRINK_BIAS, EXPAND_BIAS = 0, 1, 2, 4, 5, 6, 7, 8


def place_of():
    dp, seq = lax.axis_index("dp"), lax.axis_index("seq")
    return types.SimpleNamespace(
        x=lax.rem(lax.div(dp, 2), 4),
        yh=lax.div(dp, 8),
        yl=lax.rem(seq, 2),
        z=lax.div(seq, 2),
        c=lax.rem(dp, 2),
    )


def moved(at, **to):
    new = types.SimpleNamespace(**vars(at))
    for name, value in to.items():
        setattr(new, name, value)
    return new


def shifted(at, axis, d):
    d = d % 4
    if axis == "x":
        return moved(at, x=lax.rem(at.x + d, 4))
    if axis == "z":
        return moved(at, z=lax.rem(at.z + d, 4))
    y = lax.rem(at.yh * 2 + at.yl + d, 4)
    return moved(at, yh=lax.div(y, 2), yl=lax.rem(y, 2))


def device(at):
    return (at.yh * 8 + at.x * 2 + at.c, at.z * 2 + at.yl)


def nn(a, b):
    return jnp.dot(a, b, preferred_element_type=F32)


def nt(a, b):
    return lax.dot_general(a, b, (((1,), (1,)), ((), ())), preferred_element_type=F32)


def remote(src, dst, send, recv, to):
    return pltpu.make_async_remote_copy(
        src_ref=src, dst_ref=dst, send_sem=send, recv_sem=recv, device_id=device(to), device_id_type=MESH
    )


def norm_parts(v):
    centred = v - jnp.mean(v, axis=-1, keepdims=True)
    rstd = lax.rsqrt(jnp.mean(centred * centred, axis=-1, keepdims=True) + EPS)
    return centred * rstd, rstd


def norm_back(dy, gain, normed, rstd):
    dn = dy * gain
    return rstd * (
        dn
        - jnp.mean(dn, axis=-1, keepdims=True)
        - normed * jnp.mean(dn * normed, axis=-1, keepdims=True)
    )


def col_sums(v):
    return jnp.sum(v.astype(F32), axis=0, keepdims=True)


def turned(v):
    return v.astype(F32).T.astype(BF)


def lanes(*pieces):
    return jnp.concatenate(pieces, axis=1)


def tile(k):
    return pl.ds(pl.multiple_of(k * TOK, TOK), TOK)


IN = (
    "x_in", "cot_in", "seg_in", "mixer_in", "merge_in", "expand_in", "shrink_in", "fgain_in", "fshift_in", "mixb_in",
    "mergeb_in", "sgain_in", "sshift_in", "expandb_in", "shrinkb_in",
)
OUT = ("hidden", "gin", "gmix", "gmerge", "gexp", "gshr", "vout")


def kernel(names, *refs):
    r = types.SimpleNamespace(**dict(zip(names, refs, strict=True)))
    me = place_of()
    sib = moved(me, c=1 - me.c)
    swap = moved(me, yl=me.c, c=me.yl)
    here = me.yl == me.c
    seq = me.z * 2 + me.yl
    ypos = me.yh * 2 + me.yl
    pending = []
    sends, recvs = {}, {}

    def send_of(*key):
        return r.send.at[sends.setdefault(key, len(sends))]

    def recv_of(*key):
        return r.recv.at[recvs.setdefault(key, len(recvs))]

    def copy_to(to, src, dst, *key, recv=None):
        return remote(src, dst, send_of(*key), recv_of(*(recv or key)), to)

    def arrived(size, *key):
        remote(size, size, r.send.at[0], recv_of(*key), sib).wait_recv()

    def wait_sent(size, *key):
        remote(size, size, send_of(*key), r.recv.at[0], sib).wait_send()

    def sent(size, *key):
        pending.append(lambda: wait_sent(size, *key))

    def sent_unless(alone, size, *key):
        def finish():
            @pl.when(jnp.logical_not(alone))
            def _():
                wait_sent(size, *key)

        pending.append(finish)

    def start_unless(alone, to, src, dst, *key, recv=None):
        @pl.when(alone)
        def _():
            pltpu.make_async_copy(src, dst, recv_of(*(recv or key))).start()

        @pl.when(jnp.logical_not(alone))
        def _():
            copy_to(to, src, dst, *key, recv=recv).start()

    zero32 = jnp.zeros((48, 32), BF)
    for i in range(3):
        r.units[i] = lanes(r.mixer_in[:, 96 * i : 96 * i + 96], zero32)
    own = (me.z, me.yl, me.yh, me.x, me.c)
    r.wz[own[1:]] = lanes(r.expand_in[...], r.shrink_in[...])
    r.m_w[own[0:3]] = lanes(r.merge_in[...], zero32)
    mixb = r.mixb_in[...].astype(F32).reshape(1, 192)
    small = [(FIRST_GAIN, r.fgain_in), (FIRST_SHIFT, r.fshift_in), (MERGE_BIAS, r.mergeb_in)]
    small += [(SECOND_GAIN, r.sgain_in), (SECOND_SHIFT, r.sshift_in), (SHRINK_BIAS, r.shrinkb_in)]
    for row, ref in small:
        r.vecs[seq, row : row + 1, 0:96] = ref[...].astype(F32).reshape(1, 96)
    expb = r.expandb_in[...].astype(F32).reshape(1, SHARD)
    for k in range(2):
        r.vecs[seq, MIXER_BIAS + k : MIXER_BIAS + k + 1, 0:96] = mixb[:, 96 * k : 96 * k + 96]
    for k in range(3):
        r.vecs[seq, EXPAND_BIAS + k : EXPAND_BIAS + k + 1, :] = expb[:, TOK * k : TOK * k + TOK]
    r.segs[0] = r.seg_in[...].astype(F32)

    peers = [shifted(shifted(me, "z", dz), "y", dy) for dz in range(4) for dy in range(4) if dz or dy]
    peers += [shifted(me, "x", d) for d in (1, 2, 3)] + [sib, shifted(sib, "y", 2)]
    peers += [moved(shifted(me, "z", d), yl=1 - me.yl, c=1 - me.c) for d in range(4)]
    peers += [shifted(shifted(at, "x", d), "y", dy) for d in (1, 2, 3) for at, dy in ((sib, 0), (me, 2), (sib, 2))]
    barrier = pltpu.get_barrier_semaphore()
    for p in peers:
        pl.semaphore_signal(barrier, inc=1, device_id=device(p), device_id_type=MESH)
    pl.semaphore_wait(barrier, len(peers))

    def send_own(name):
        at = getattr(r, name).at[me.z]
        for d in (1, 3, 2):
            copy_to(shifted(me, "z", d), at, at, name).start()

    def send_along(name, src_of, order=(1, 3, 2)):
        for d in order:
            to = shifted(me, "z", d)
            copy_to(to, src_of(to.z), getattr(r, name).at[me.z], name).start()

    def take_along(name):
        arrived(getattr(r, name).at[0:3], name)
        sent(getattr(r, name).at[0:3], name)

    def send_back(src, dst, key):
        start_unless(here, swap, src, dst, *key)
        sent_unless(here, src, *key)

    for i in range(3):
        u = 3 * seq + i
        group = lax.div(lax.rem(u, 8), 2)
        dst = r.wl.at[lax.rem(u, 2), me.yh, lax.div(u, 8)]
        for dy in range(4):
            y = lax.rem(ypos + dy, 4)
            to = moved(me, z=group, yh=lax.div(y, 2), yl=lax.rem(y, 2))
            if dy:
                copy_to(to, r.units.at[i], dst, "unit").start()
            else:
                start_unless(group == me.z, to, r.units.at[i], dst, "unit", i, recv=("unit",))
        sent_unless(group == me.z, r.units.at[i], "unit", i)
    sent(r.rmf.at[:, 0:3], "unit")

    def seq_peer(k):
        at = shifted(me, "z", k // 2)
        return moved(at, yl=1 - me.yl) if k % 2 else at

    for k in range(1, 8):
        copy_to(seq_peer(k), r.vecs.at[seq], r.vecs.at[seq], "vec").start()
    sent(r.vr, "vec")
    def upper(ref, h):
        return ref.at[pl.ds(64 * h, 64)]

    for h in range(2):
        send_back(upper(r.x_in, h), upper(r.xall.at[me.z], h), ("x", h))

    def x_along(h):
        arrived(upper(r.xall.at[0], 0), "x", h)
        at = upper(r.xall.at[me.z], h)
        for d in (1, 3, 2):
            copy_to(shifted(me, "z", d), at, at, "xall").start()

    @pl.when(here)
    def _():
        x_along(0)
        x_along(1)


    def plane(ref, d):
        return ref.at[(slice(None),) * (len(ref.shape) - 4) + (lax.rem(me.x + 4 - d, 4), me.c)]

    def plane_start(ref, key):
        at = plane(ref, 0)
        for d in (1, 3, 2):
            copy_to(shifted(me, "x", d), at, at, key, recv=(key, d)).start()
        copy_to(sib, at, at, key, "hand").start()
        every = (slice(None),) * (len(ref.shape) - 4)
        sent(ref.at[every + (slice(0, 3), me.c)], key)
        sent(ref.at[every + (slice(0, 4), me.c)], key, "hand")

    def plane_hand(ref, key):
        for d in (1, 3, 2):
            at = plane(ref, d)
            arrived(at, key, d)
            copy_to(sib, at, at, key, "hand").start()

    def plane_finish(ref, key):
        every = (slice(None),) * (len(ref.shape) - 4)
        arrived(ref.at[every + (slice(0, 4), 1 - me.c)], key, "hand")

    def column(d):
        at = shifted(me, "y", -d)
        return r.wz.at[at.yl, at.yh, :, me.c]

    def column_start():
        for d in (1, 3, 2):
            copy_to(shifted(me, "y", d), column(0), column(0), "column", recv=("column", d)).start()
        copy_to(sib, column(0), column(0), "column", "hand").start()
        sent(r.wz.at[0, :, 0:3], "column")
        sent(r.wz.at[:, :, :, me.c], "column", "hand")

    def column_hand():
        for d in (1, 3, 2):
            arrived(column(d), "column", d)
            copy_to(sib, column(d), column(d), "column", "hand").start()

    def column_finish():
        arrived(r.wz.at[:, :, :, 1 - me.c], "column", "hand")

    copy_to(sib, r.segs.at[0], r.segs.at[1], "seg").start()
    sent(r.segs.at[0], "seg")
    own = r.wz.at[me.yl, me.yh, me.x, me.c]
    for d in (1, 3, 2):
        copy_to(shifted(me, "x", d), own, own, "hidden").start()
    sent(r.gy, "hidden")
    around = [(dz, dy) for dz in (1, 3, 0, 2) for dy in (0, 1, 3, 2) if dz or dy]
    at = r.m_w.at[me.z, me.yl, me.yh]
    for dz, dy in around:
        copy_to(shifted(shifted(me, "z", dz), "y", dy), at, at, "merge").start()
    sent(r.m_y, "merge")
    send_back(r.cot_in, r.call.at[me.z], ("cot",))
    arrived(r.wl, "unit")
    for yh in range(2):
        pieces = [r.wl[half, yh, kind, :, 0:96] for kind in (1, 2, 0) for half in range(2)]
        r.wm[yh, me.x, me.c] = lanes(*pieces, jnp.zeros((48, 64), BF))

    plane_start(r.wm, "mixer")
    @pl.when(jnp.logical_not(here))
    def _():
        x_along(0)
        x_along(1)

    arrived(r.gy, "hidden")
    column_start()
    arrived(r.vr, "vec")

    def whole(row):
        return jnp.concatenate([r.vecs[s, row : row + 1, 0:96] for s in range(8)], axis=1)


    gain1, shift1 = whole(FIRST_GAIN), whole(FIRST_SHIFT)
    plane_hand(r.wm, "mixer")
    arrived(r.m_y, "merge")
    for yh in range(2):
        pieces = [r.m_w[s // 2, s % 2, yh, :, 0:96] for s in range(8)]
        r.mc[yh, me.x, me.c] = lanes(*pieces)
    plane_start(r.mc, "merge x")
    take_along("xall")
    arrived(r.call.at[0], "cot")
    send_own("call")
    for b in range(4):
        normed, rstd = norm_parts(r.xall[b].astype(F32))
        r.n1all[b] = normed
        r.rstd1[b] = jnp.broadcast_to(rstd, (TOK, TOK))
        first = normed * gain1 + shift1
        r.fall[b] = first.astype(BF)
        r.fallt[:, :, :, TOK * b : TOK * b + TOK] = turned(first.astype(BF)).reshape(8, 2, 48, TOK)
    plane_finish(r.wm, "mixer")

    at = r.fallt.at[:, 1 - me.c]
    copy_to(sib, at, r.fallt_sib, "first").start()
    sent(r.fallt_sib, "first")
    def mixer(at):
        return r.wm[:, :, :, :, at].reshape(D, -1)

    first = r.fall[...].reshape(4 * TOK, D)

    def mixer_bias(at, half):
        row = MIXER_BIAS + half
        return r.vecs[at, row : row + 1, 0:96]

    kv = nn(first, mixer(slice(0, 384)))
    keys = kv[:, 0:192].astype(BF)
    vbias = lanes(mixer_bias(4 + me.z, 0), mixer_bias(4 + me.z, 1))
    values = (kv[:, 192:384] + vbias).astype(BF)
    packed = lanes(keys, values[:, 128:192], values[:, 0:128])
    for b in range(4):
        r.kv_all[b, me.c] = packed[TOK * b : TOK * b + TOK]
    at = r.kv_all.at[:, me.c]
    copy_to(sib, at, at, "kv").start()
    sent(at, "kv")
    qbias = lanes(mixer_bias(me.z, 0), mixer_bias(me.z, 1))
    q = nn(first, mixer(slice(384, HEADS3)))[:, 0:192]
    q = (q + qbias).astype(BF) * jnp.asarray(0.125, BF)
    q = lanes(q, jnp.zeros((4 * TOK, 64), BF))
    for b in range(4):
        r.q_all[b] = q[TOK * b : TOK * b + TOK]
        r.kvt[:, tile(2 * b + me.c)] = turned(packed[TOK * b : TOK * b + TOK])
    arrived(r.segs.at[1], "seg")
    arrived(r.kv_all.at[:, 1 - me.c], "kv")
    for b in range(4):
        r.kvt[:, tile(2 * b + 1 - me.c)] = turned(r.kv_all[b, 1 - me.c])

    seg = jnp.where(here, r.segs[0], r.segs[1])

    def starts(bound):
        return jnp.sum(jnp.where(seg < bound, 1.0, 0.0), axis=(0, 1), keepdims=True).astype(jnp.int32)

    begin1, begin2 = starts(0.5), starts(1.5)
    lane = lax.broadcasted_iota(jnp.int32, (TOK, TOK), 1)

    def allowed_of(b):
        n = 256 * (b + 1)
        qpos = 256 * b + TOK * me.c + lax.broadcasted_iota(jnp.int32, (1, TOK), 1)
        low = jnp.where(qpos < begin1, 0, jnp.where(qpos < begin2, begin1, begin2))
        kpos = lax.broadcasted_iota(jnp.int32, (n, TOK), 0)
        return (kpos <= qpos) & (kpos >= low)

    def keys_of(b, h):
        at = slice(0, 128) if h < 2 else slice(128, 256)
        return r.kv_all[0 : b + 1, :, :, at].reshape(256 * (b + 1), TOK)

    def values_of(b, h):
        at = slice(256, 384) if h < 2 else slice(128, 256)
        return r.kv_all[0 : b + 1, :, :, at].reshape(256 * (b + 1), TOK)

    K_ROWS = (0, 64, 128)
    V_ROWS = (256, 320, 192)

    def one_head(v, upper):
        keep = lane >= 64 if upper else lane < 64
        return jnp.where(keep, v, jnp.zeros_like(v))

    def query_of(b, h):
        return one_head(r.q_all[b, :, 0:128] if h < 2 else r.q_all[b, :, 128:256], h == 1)

    spare = []
    for b in (3, 2, 1, 0):
        n = 256 * (b + 1)
        allowed = allowed_of(b)
        outs = []
        for h in range(3):
            scores = jnp.where(allowed, nt(keys_of(b, h), query_of(b, h)), NEG)
            top = jnp.max(scores, axis=0, keepdims=True)
            expo = jnp.exp(scores - top)
            total = jnp.sum(expo, axis=0, keepdims=True)
            r.lse[b, h : h + 1, :] = top + jnp.log(total)
            weights = (expo * (1.0 / total)).astype(BF)
            outs.append(nn(r.kvt[V_ROWS[h] : V_ROWS[h] + 64, 0:n], weights))
        r.att_all[me.z, b] = jnp.concatenate(outs[0:2], axis=0).T.astype(BF)
        spare.append(outs[2])
        ready = [b]
        if b % 2 == 0:
            r.att_all[me.z, 4 + b // 2] = jnp.concatenate([spare[-1], spare[-2]], axis=0).T.astype(BF)
            ready.append(4 + b // 2)
        for k in ready:
            for d in (1, 3, 2):
                at = r.att_all.at[me.z, k]
                copy_to(shifted(me, "z", d), at, at, "att", recv=("att", b // 2)).start()
        if b == 1:
            column_hand()
        if b == 0:
            plane_hand(r.mc, "merge x")
    sent(r.att_all.at[0:3], "att")
    take_along("call")
    for b in range(4):
        r.cott[:, TOK * b : TOK * b + TOK] = turned(r.call[b])
    plane_finish(r.mc, "merge x")
    merge = r.mc[...].reshape(D, D)

    column_finish()
    gain2, shift2, b_merge = whole(SECOND_GAIN), whole(SECOND_SHIFT), whole(MERGE_BIAS)

    def hidden(first):
        return lanes(*[r.wz[yl, :, :, :, :, first : first + SHARD].reshape(D, SHARD) for yl in range(2)])

    bias = lanes(*[r.vecs[2 * me.z + yl, EXPAND_BIAS + k : EXPAND_BIAS + k + 1] for yl in range(2) for k in range(3)])
    sums2 = []
    for pair in (1, 0):
        arrived(r.att_all.at[0:3, 0:3], "att", pair)
        rows = slice(2 * pair, 2 * pair + 2)
        for b in (2 * pair, 2 * pair + 1):
            at = slice(64 * (b % 2), 64 * (b % 2) + 64)
            r.att[b] = lanes(*[v for g in range(4) for v in (r.att_all[g, b], r.att_all[g, 4 + pair, :, at])])
        branch = nn(r.att[rows].reshape(2 * TOK, D), merge)
        middle = r.xall[rows].reshape(2 * TOK, D).astype(F32) + branch + b_merge
        r.mid[rows] = middle.reshape(2, TOK, D)
        n2, rstd2 = norm_parts(middle)
        second = (n2 * gain2 + shift2).astype(BF)
        r.second[rows] = second.reshape(2, TOK, D)
        pre = nn(second, hidden(0)) + bias
        square = pre * pre
        tanh = jnp.tanh(0.7978845608028654 * (pre + 0.044715 * square * pre))
        r.active[rows] = (0.5 * pre * (1.0 + tanh)).astype(BF).reshape(2, TOK, WIDE)
        slope = 0.5 * (1.0 + tanh) + 0.5 * pre * (1.0 - tanh * tanh) * (
            0.7978845608028654 * (1.0 + 0.134145 * square)
        )
        cot = r.call[rows]
        d_pre = (nn(cot.reshape(2 * TOK, D), hidden(SHARD)) * slope).astype(BF)
        r.dpre[rows] = d_pre.reshape(2, TOK, WIDE)
        d_second = nt(d_pre, hidden(0))
        sums2.append((col_sums(d_second * n2), col_sums(d_second)))
        d_middle = norm_back(d_second, gain2, n2, rstd2)
        d_branch = []
        for i in range(2):
            own = jnp.where(me.z == 2 * pair + i, cot[i].astype(F32), 0.0) + d_middle[TOK * i : TOK * i + TOK]
            r.dmid[2 * pair + i] = own
            d_branch.append(own.astype(BF))
            r.dbr[2 * pair + i] = d_branch[-1]
        d_att = nt(jnp.concatenate(d_branch, axis=0), merge).astype(BF)
        low, high = d_att[0:TOK], d_att[TOK : 2 * TOK]
        for z in range(4):
            at = 192 * z
            r.do_send[pair, z, 0] = low[:, at : at + 128]
            r.do_send[pair, z, 1] = high[:, at : at + 128]
            r.do_send[pair, z, 2] = lanes(low[:, at + 128 : at + 192], high[:, at + 128 : at + 192])
        for d in (1, 3, 2):
            to = shifted(me, "z", d)
            copy_to(to, r.do_send.at[pair, to.z], r.do_recv.at[pair, me.z], "do", recv=("do", pair)).start()
        r.do_recv[pair, me.z] = r.do_send[pair, me.z]
    sent(r.do_send.at[:, 0:3], "do")

    zeros = jnp.zeros((TOK, 32), BF)

    for b in range(4):
        r.attt[:, TOK * b : TOK * b + TOK] = turned(r.att[b])
    grad = nn(r.attt[...], r.dbr[...].reshape(4 * TOK, D)).astype(BF)
    r.m_g[...] = grad.reshape(2, 4, 2, 48, D)
    copy_to(sib, r.m_g.at[:, :, 1 - me.c], r.m_r0, "merge", "pair").start()
    sent(r.m_r0, "merge", "pair")

    sums = col_sums(r.dpre[...].reshape(4 * TOK, WIDE))
    r.vg[...] = jnp.zeros((8, 16, TOK), F32)
    for yl in range(2):
        for k in range(3):
            at = TOK * (3 * yl + k)
            r.vg[2 * me.z + yl, EXPAND_BIAS + k : EXPAND_BIAS + k + 1, :] = sums[:, at : at + TOK]
    for b in range(4):
        r.secondt[:, TOK * b : TOK * b + TOK] = turned(r.second[b])
    halves = ((r.g_e, r.g_e0), (r.g_s, r.g_s0))

    def hidden_gradient(k, left, right):
        ref, pair0 = halves[k]
        grad = nn(left[...], right[...].reshape(4 * TOK, WIDE)).astype(BF)
        for yl in range(2):
            ref[yl] = grad[:, SHARD * yl : SHARD * yl + SHARD].reshape(2, 4, 2, 48, SHARD)
        copy_to(sib, ref.at[:, :, :, 1 - me.c], pair0, "hidden", k, "pair").start()
        sent(pair0, "hidden", k, "pair")

    hidden_gradient(0, r.secondt, r.dpre)

    hidden_gradient(1, r.cott, r.active)
    result = nt(r.active[...].reshape(4 * TOK, WIDE), hidden(SHARD)).astype(BF)
    for b in range(4):
        r.res_send[b] = result[TOK * b : TOK * b + TOK]
    send_along("res_recv", lambda z: r.res_send.at[z])
    r.res_recv[me.z] = r.res_send[me.z]

    def pair_sum(ref, own, key):
        arrived(ref, *key, "pair")
        every = (slice(None),) * (len(ref.shape) - 2)
        ref[...] = (ref[...].astype(F32) + own[every + (me.c,)].astype(F32)).astype(BF)

    def plane_send(ref, got, key):
        every = (slice(None),) * (len(ref.shape) - 3)
        for d in (1, 3, 2):
            to = shifted(me, "x", d)
            copy_to(to, ref.at[every + (to.x,)], got.at[d - 1], key, "sum").start()
        sent(got, key, "sum")

    def plane_total(ref, got, key):
        arrived(got, key, "sum")
        total = ref[(slice(None),) * (len(ref.shape) - 3) + (me.x,)].astype(F32)
        for d in range(3):
            total += got[d].astype(F32)
        return total.astype(BF)

    def expand_sum():
        pair_sum(r.g_e0, r.g_e, ("hidden", 0))
        for d in (1, 3, 2):
            to = shifted(me, "y", d)
            copy_to(to, r.g_e0.at[to.yl, to.yh], r.g_y.at[d - 1], "expand y").start()
        sent(r.g_y, "expand y")

    def expand_next():
        arrived(r.g_y, "expand y")
        total = r.g_e0[me.yl, me.yh].astype(F32)
        for d in range(3):
            total += r.g_y[d].astype(F32)
        r.g_ex[...] = total.astype(BF)
        for d in (1, 3, 2):
            to = shifted(me, "x", d)
            copy_to(to, r.g_ex.at[to.x], r.g_got.at[0, d - 1], "expand x").start()
        sent(r.g_got.at[0], "expand x")

    def shrink_sum():
        pair_sum(r.g_s0, r.g_s, ("hidden", 1))
        plane_send(r.g_s0, r.g_x, "shrink")

    def shrink_next():
        r.g_sy[...] = plane_total(r.g_s0, r.g_x, "shrink")
        for d in (1, 3, 2):
            to = shifted(me, "y", d)
            copy_to(to, r.g_sy.at[to.yl, to.yh], r.g_got.at[1, d - 1], "shrink y").start()
        sent(r.g_got.at[1], "shrink y")

    def merge_next():
        total = plane_total(r.m_r0, r.m_x, "merge")
        for s in range(8):
            for yh in range(2):
                r.m_t[s // 2, s % 2, yh] = lanes(total[yh, :, 96 * s : 96 * s + 96], zero32)
        for i, (dz, dy) in enumerate(around):
            to = shifted(shifted(me, "z", dz), "y", dy)
            copy_to(to, r.m_t.at[to.z, to.yl, to.yh], r.m_y.at[i], "merge all").start()
        sent(r.m_y, "merge all")

    pair_sum(r.m_r0, r.m_g, ("merge",))
    plane_send(r.m_r0, r.m_x, "merge")
    expand_sum()
    r.dkv[...] = jnp.zeros((8 * TOK, SHARD), F32)
    sent(r.dkv_got, "dkv")

    def take_pair(p):
        arrived(r.do_recv.at[p, 0:3], "do", p)
        total = r.do_recv[p, 0].astype(F32)
        for z in range(1, 4):
            total += r.do_recv[p, z].astype(F32)
        r.do_all[2 * p, :, 0:TOK] = total[0].astype(BF)
        r.do_all[2 * p, :, TOK : 2 * TOK] = lanes(total[2, :, 64:128], total[2, :, 0:64]).astype(BF)
        r.do_all[2 * p + 1, :, 0:TOK] = total[1].astype(BF)
        r.do_all[2 * p + 1, :, TOK : 2 * TOK] = total[2].astype(BF)

    def pair(l0, l1, r0, r1):
        return nn(jnp.concatenate([l0, l1], axis=1), jnp.concatenate([r0, r1], axis=0))

    gain_sum, shift_sum = [], []

    def finish_block(b):
        arrived(r.dkv_got.at[b], "dkv", b)
        own = pl.multiple_of(256 * b + TOK * me.c, TOK)
        dkv = (r.dkv[pl.ds(own, TOK), :] + r.dkv_got[b].astype(F32)).astype(BF)
        dq = r.dq[b]
        r.dpad[b] = lanes(dkv[:, 0:192], dkv[:, 256:384], dkv[:, 192:256], dq[:, 0:192], jnp.zeros((TOK, 64), BF))
        at = r.dpad.at[b]
        copy_to(sib, at, r.dpad_sib.at[b], "dpad").start()

    def first_back(blocks):
        rows = jnp.concatenate([r.dpad[b] for b in blocks], axis=0)
        d_first = nt(rows, mixer(slice(0, HEADS3)))
        for i, b in enumerate(blocks):
            part, normed = d_first[TOK * i : TOK * i + TOK], r.n1all[b]
            gain_sum.append(col_sums(part * normed))
            shift_sum.append(col_sums(part))
            r.df_send[b] = (r.dmid[b] + norm_back(part, gain1, normed, r.rstd1[b][:, 0:1])).astype(BF)

    for b in (3, 2, 1, 0):
        if b % 2:
            take_pair(b // 2)
        n = 256 * (b + 1)
        allowed = allowed_of(b)
        dqs, dss, pbs, dos, qs = [], [], [], [], []
        for h in range(3):
            q = query_of(b, h)
            do = one_head(r.do_all[b, :, 0:128] if h < 2 else r.do_all[b, :, 128:256], h > 0)
            scores = jnp.where(allowed, nt(keys_of(b, h), q), NEG)
            probs = jnp.exp(scores - r.lse[b, h : h + 1, :])
            dw = nt(values_of(b, h), do)
            centre = jnp.sum(probs * dw, axis=0, keepdims=True)
            ds = (probs * (dw - centre)).astype(BF)
            dqs.append(nn(r.kvt[K_ROWS[h] : K_ROWS[h] + 64, 0:n], ds))
            dss.append(ds)
            pbs.append(probs.astype(BF))
            dos.append(do)
            qs.append(q)
        dqs.append(jnp.zeros((64, TOK), F32))
        r.dq[b] = (jnp.concatenate(dqs, axis=0) * 0.125).T.astype(BF)
        r.dkv[0:n, 0:128] += pair(dss[0], dss[1], qs[0], qs[1])
        r.dkv[0:n, 128:256] += pair(dss[2], pbs[2], qs[2], dos[2])
        r.dkv[0:n, 256:384] += pair(pbs[0], pbs[1], dos[0], dos[1])
        other = pl.multiple_of(256 * b + TOK * (1 - me.c), TOK)
        r.dkv_sib[b] = r.dkv[pl.ds(other, TOK), :].astype(BF)
        copy_to(sib, r.dkv_sib.at[b], r.dkv_got.at[b], "dkv", recv=("dkv", b)).start()
        if b == 3:
            shrink_sum()
        if b in (2, 1):
            finish_block(b + 1)
    finish_block(1)
    first_back((3, 1))
    finish_block(0)
    first_back((2, 0))
    g_gain_b, g_shift_b = sums2[0][0] + sums2[1][0], sums2[0][1] + sums2[1][1]
    g_b_shrink = col_sums(r.call[me.z])
    g_b_merge = col_sums(r.dbr[...].reshape(4 * TOK, D))
    rows = [(MERGE_BIAS, g_b_merge), (SECOND_GAIN, g_gain_b), (SECOND_SHIFT, g_shift_b), (SHRINK_BIAS, g_b_shrink)]
    for s in range(8):
        for row, value in rows:
            r.vg[s, row : row + 1, 0:96] = value[:, 96 * s : 96 * s + 96]

    arrived(r.fallt_sib, "first")
    sums = col_sums(r.dpad[...].reshape(4 * TOK, HEADS3))
    for half in range(2):
        row = MIXER_BIAS + half
        r.vg[me.z, row : row + 1, 0:96] = sums[:, 384 + 96 * half : 480 + 96 * half]
        r.vg[4 + me.z, row : row + 1, 0:96] = sums[:, 192 + 96 * half : 288 + 96 * half]
    gain_a, shift_a = sum(gain_sum), sum(shift_sum)
    for s in range(8):
        r.vg[s, FIRST_GAIN : FIRST_GAIN + 1, 0:96] = gain_a[:, 96 * s : 96 * s + 96]
        r.vg[s, FIRST_SHIFT : FIRST_SHIFT + 1, 0:96] = shift_a[:, 96 * s : 96 * s + 96]

    for k in range(1, 8):
        to = seq_peer(k)
        copy_to(to, r.vg.at[to.z * 2 + to.yl], r.vr.at[k - 1], "rows").start()
    sent(r.vr, "rows")
    send_along("df_recv", lambda z: r.df_send.at[z])
    r.df_recv[me.z] = r.df_send[me.z]

    arrived(r.dpad_sib, "dpad")
    sent(r.dpad, "dpad")
    left = jnp.concatenate([r.fallt[:, me.c].reshape(D // 2, 4 * TOK), r.fallt_sib[...].reshape(D // 2, 4 * TOK)], axis=1)
    right = jnp.concatenate([ref[...].reshape(4 * TOK, HEADS3) for ref in (r.dpad, r.dpad_sib)], axis=0)
    r.rm0[...] = nn(left, right).astype(BF).reshape(2, 4, 48, HEADS3)
    plane_send(r.rm0, r.rmx, "mixer")
    take_along("res_recv")
    result = r.mid[me.z] + whole(SHRINK_BIAS)
    for b in range(4):
        result += r.res_recv[b].astype(F32)
    r.hid[...] = result.astype(BF)
    send_back(r.hid, r.hid_recv, ("hid",))
    expand_next()
    merge_next()
    arrived(r.vr, "rows")
    total = r.vg[seq]
    for k in range(7):
        total += r.vr[k]
    ours = me.yh * 8 + me.x * 2 + me.c
    r.vx[ours] = total
    others = [(at, dx, dy) for at in (me, sib) for dx in range(4) for dy in (0, 2) if dx or dy or at is sib]
    for at, dx, dy in others:
        copy_to(shifted(shifted(at, "x", dx), "y", dy), r.vx.at[ours], r.vx.at[ours], "rows all").start()
    sent(r.vx.at[0:15], "rows all")
    shrink_next()
    total = plane_total(r.rm0, r.rmx, "mixer")
    for half in range(2):
        for yh in range(2):
            for kind in range(3):
                at = (384, 0, 192)[kind] + 96 * half
                r.rmy[half, yh, kind] = lanes(total[yh, :, at : at + 96], zero32)
    for dyh in range(2):
        yh = lax.rem(me.yh + dyh, 2)
        for half in range(2):
            for kind in range(3):
                u = 8 * kind + 2 * me.z + half
                owner = lax.div(u, 3)
                to = moved(me, yh=yh, z=lax.div(owner, 2), yl=lax.rem(owner, 2))
                src = r.rmy.at[half, yh, kind]
                dst = r.rmf.at[lax.rem(u, 3), ypos]
                if dyh:
                    copy_to(to, src, dst, "piece").start()
                else:
                    start_unless(owner == seq, to, src, dst, "piece", half, kind, recv=("piece",))
                    sent_unless(owner == seq, r.units.at[0], "piece", half, kind)
    sent(r.rmf.at[:, 0:2], "piece")
    take_along("df_recv")
    r.gin_send[...] = sum(r.df_recv[b].astype(F32) for b in range(4)).astype(BF)
    send_back(r.gin_send, r.gin_recv, ("gin",))

    arrived(r.hid_recv, "hid")
    r.hidden[...] = r.hid_recv[...]
    arrived(r.g_got.at[0], "expand x")
    r.gexp[...] = r.g_ex[me.x].astype(F32) + sum(r.g_got[0, d].astype(F32) for d in range(3))
    arrived(r.g_got.at[1], "shrink y")
    r.gshr[...] = r.g_sy[me.yl, me.yh].astype(F32) + sum(r.g_got[1, d].astype(F32) for d in range(3))
    arrived(r.m_y, "merge all")
    total = r.m_t[me.z, me.yl, me.yh].astype(F32)
    for i in range(15):
        total += r.m_y[i].astype(F32)
    r.gmerge[...] = total[:, 0:96]
    arrived(r.gin_recv, "gin")
    r.gin[...] = r.gin_recv[...].astype(F32)
    arrived(r.vx.at[0:15], "rows all")
    total = r.vx[0]
    for k in range(1, 16):
        total += r.vx[k]
    r.vout[...] = total
    arrived(r.rmf, "piece")
    for i in range(3):
        total = jnp.zeros((48, TOK), F32)
        for y in range(4):
            total += r.rmf[i, y].astype(F32)
        r.gmix[:, 96 * i : 96 * i + 96] = total[:, 0:96]
    for finish in pending:
        finish()
    if (len(sends), len(recvs)) != (SENDS, RECVS):
        raise ValueError((len(sends), len(recvs)))


def scratches():
    v, dma = pltpu.VMEM, pltpu.SemaphoreType.DMA
    blocks = (2, 4, 2, 48)
    s = dict(
        m_w=v((4, 2, 2, 48, TOK), BF),
        m_g=v(blocks + (D,), BF),
        m_r0=v((2, 4, 48, D), BF),
        m_x=v((3, 2, 48, D), BF),
        m_t=v((4, 2, 2, 48, TOK), BF),
        m_y=v((15, 48, TOK), BF),
        mc=v(blocks + (D,), BF),
        wz=v((2,) + blocks + (WIDE,), BF),
        g_e=v((2,) + blocks + (SHARD,), BF),
        g_s=v((2,) + blocks + (SHARD,), BF),
        g_e0=v((2, 2, 4, 48, SHARD), BF),
        g_s0=v((2, 2, 4, 48, SHARD), BF),
        g_y=v((3, 4, 48, SHARD), BF),
        g_x=v((3, 2, 2, 48, SHARD), BF),
        g_ex=v((4, 48, SHARD), BF),
        g_sy=v((2, 2, 48, SHARD), BF),
        g_got=v((2, 3, 48, SHARD), BF),
        gy=v((3, 48, WIDE), BF),
        units=v((3, 48, TOK), BF),
        wl=v((2, 2, 3, 48, TOK), BF),
        wm=v(blocks + (HEADS3,), BF),
        rm0=v((2, 4, 48, HEADS3), BF),
        rmx=v((3, 2, 48, HEADS3), BF),
        rmy=v((2, 2, 3, 48, TOK), BF),
        rmf=v((3, 4, 48, TOK), BF),
        vecs=v((8, 16, TOK), F32),
        segs=v((2, 8, TOK), F32),
        fallt=v((8, 2, 48, 4 * TOK), BF),
        fallt_sib=v((8, 48, 4 * TOK), BF),
        cott=v((D, 4 * TOK), BF),
        secondt=v((D, 4 * TOK), BF),
        attt=v((D, 4 * TOK), BF),
        rstd1=v((4, TOK, TOK), F32),
        dmid=v((4, TOK, D), F32),
        q_all=v((4, TOK, 256), BF),
        kv_all=v((4, 2, TOK, SHARD), BF),
        kvt=v((SHARD, 8 * TOK), BF),
        lse=v((4, 8, TOK), F32),
        att_all=v((4, 6, TOK, TOK), BF),
        dkv=v((8 * TOK, SHARD), F32),
        dkv_sib=v((4, TOK, SHARD), BF),
        dkv_got=v((4, TOK, SHARD), BF),
        dq=v((4, TOK, 256), BF),
        dpad=v((4, TOK, HEADS3), BF),
        dpad_sib=v((4, TOK, HEADS3), BF),
        do_send=v((2, 4, 3, TOK, TOK), BF),
        do_recv=v((2, 4, 3, TOK, TOK), BF),
        do_all=v((4, TOK, 256), BF),
        n1all=v((4, TOK, D), F32),
        mid=v((4, TOK, D), F32),
    )
    for name in ("xall", "call", "fall", "att", "second", "dbr", "res_send", "res_recv", "df_send", "df_recv"):
        s[name] = v((4, TOK, D), BF)
    for name in ("active", "dpre"):
        s[name] = v((4, TOK, WIDE), BF)
    for name in ("hid", "hid_recv", "gin_send", "gin_recv"):
        s[name] = v((TOK, D), BF)
    for name, count in (("vg", 8), ("vr", 7), ("vx", 16)):
        s[name] = v((count, 16, TOK), F32)
    s["send"], s["recv"] = dma((SENDS,)), dma((RECVS,))
    return s


def finish(hidden, gin, gmix, gmerge, gexp, gshr, vout, *outs):
    for ref, out in zip((hidden, gin, gmix, gmerge, gexp, gshr), outs[:6], strict=True):
        out[...] = ref[...]
    v = vout[...]
    rows = (FIRST_GAIN, FIRST_SHIFT, MERGE_BIAS, SECOND_GAIN, SECOND_SHIFT, SHRINK_BIAS)
    for row, out in zip(rows, outs[6:12], strict=True):
        out[...] = v[row : row + 1, 0:96].reshape(96)
    outs[12][...] = lanes(v[MIXER_BIAS : MIXER_BIAS + 1, 0:96], v[MIXER_BIAS + 1 : MIXER_BIAS + 2, 0:96]).reshape(192)
    outs[13][...] = lanes(*[v[EXPAND_BIAS + k : EXPAND_BIAS + k + 1] for k in range(3)]).reshape(SHARD)


def body(
    residual_in, cotangent, segments, first_gain, first_shift, mixer_weight, mixer_bias, merge_weight, merge_bias,
    second_gain, second_shift, expand_weight, expand_bias, shrink_weight, shrink_bias,
):
    vmem = pl.BlockSpec(memory_space=pltpu.VMEM)
    scratch = scratches()
    shapes = [((TOK, D), BF), ((TOK, D), F32), ((48, 288), F32), ((48, 96), F32), ((48, SHARD), F32), ((48, SHARD), F32)]
    held = [jax.ShapeDtypeStruct(*s) for s in shapes]
    parts = pl.pallas_call(
        functools.partial(kernel, IN + OUT + tuple(scratch)),
        out_shape=held + [jax.ShapeDtypeStruct((16, TOK), F32)],
        in_specs=[vmem] * len(IN),
        out_specs=[vmem] * len(OUT),
        scratch_shapes=list(scratch.values()),
        compiler_params=pltpu.CompilerParams(
            collective_id=0, has_side_effects=True, vmem_limit_bytes=62 * 1024 * 1024
        ),
    )(
        residual_in[0], cotangent[0], segments.reshape(8, TOK), mixer_weight, merge_weight, expand_weight,
        shrink_weight.T, first_gain, first_shift, mixer_bias, merge_bias, second_gain, second_shift, expand_bias,
        shrink_bias,
    )
    vectors = [jax.ShapeDtypeStruct((n,), F32) for n in (96, 96, 96, 96, 96, 96, 192, SHARD)]
    hidden, gin, gmix, gmerge, gexp, gshr, fg, fs, mb, sg, ss, sb, xb, eb = pl.pallas_call(
        finish, out_shape=held + vectors, in_specs=[vmem] * 7, out_specs=[vmem] * 14
    )(*parts)
    return hidden[None], gin[None], fg, fs, gmix, xb, gmerge, mb, sg, ss, gexp, eb, gshr.T, sb


def solution(mesh):
    vector, matrix = P("seq"), P("dp", "seq")
    tokens = P("dp", "seq", None)
    return jax.shard_map(
        body,
        mesh=mesh,
        in_specs=(
            tokens, tokens, P("dp", None), vector, vector, matrix, vector, matrix, vector, vector, vector, matrix, vector,
            P("seq", "dp"), vector,
        ),
        out_specs=(
            tokens, tokens, vector, vector, matrix, vector, matrix, vector, vector, vector, matrix, vector,
            P("seq", "dp"), vector,
        ),
        check_vma=False,
    )
```

```python
import functools
import types

import jax
import jax.numpy as jnp
from jax import lax
from jax.experimental import pallas as pl
from jax.experimental.pallas import tpu as pltpu
from jax.sharding import PartitionSpec as P


D = 768
HD = 64
TOK = 128
SHARD = 384
HEADS3 = 640
WIDE = 768
EPS = 1e-05
NEG = -1e30
MESH = pl.DeviceIdType.MESH
BF = jnp.bfloat16
F32 = jnp.float32
SENDS, RECVS = 49, 51
FIRST_GAIN, FIRST_SHIFT, MIXER_BIAS, MERGE_BIAS, SECOND_GAIN, SECOND_SHIFT, SHRINK_BIAS, EXPAND_BIAS = 0, 1, 2, 4, 5, 6, 7, 8


def place_of():
    dp, seq = lax.axis_index("dp"), lax.axis_index("seq")
    return types.SimpleNamespace(
        x=lax.rem(lax.div(dp, 2), 4),
        yh=lax.div(dp, 8),
        yl=lax.rem(seq, 2),
        z=lax.div(seq, 2),
        c=lax.rem(dp, 2),
    )


def moved(at, **to):
    new = types.SimpleNamespace(**vars(at))
    for name, value in to.items():
        setattr(new, name, value)
    return new


def shifted(at, axis, d):
    d = d % 4
    if axis == "x":
        return moved(at, x=lax.rem(at.x + d, 4))
    if axis == "z":
        return moved(at, z=lax.rem(at.z + d, 4))
    y = lax.rem(at.yh * 2 + at.yl + d, 4)
    return moved(at, yh=lax.div(y, 2), yl=lax.rem(y, 2))


def device(at):
    return (at.yh * 8 + at.x * 2 + at.c, at.z * 2 + at.yl)


def nn(a, b):
    return jnp.dot(a, b, preferred_element_type=F32)


def nt(a, b):
    return lax.dot_general(a, b, (((1,), (1,)), ((), ())), preferred_element_type=F32)


def remote(src, dst, send, recv, to):
    return pltpu.make_async_remote_copy(
        src_ref=src, dst_ref=dst, send_sem=send, recv_sem=recv, device_id=device(to), device_id_type=MESH
    )


def norm_parts(v):
    centred = v - jnp.mean(v, axis=-1, keepdims=True)
    rstd = lax.rsqrt(jnp.mean(centred * centred, axis=-1, keepdims=True) + EPS)
    return centred * rstd, rstd


def norm_back(dy, gain, normed, rstd):
    dn = dy * gain
    return rstd * (
        dn
        - jnp.mean(dn, axis=-1, keepdims=True)
        - normed * jnp.mean(dn * normed, axis=-1, keepdims=True)
    )


def col_sums(v):
    return jnp.sum(v.astype(F32), axis=0, keepdims=True)


def turned(v):
    return v.astype(F32).T.astype(BF)


def lanes(*pieces):
    return jnp.concatenate(pieces, axis=1)


def tile(k):
    return pl.ds(pl.multiple_of(k * TOK, TOK), TOK)


IN = (
    "x_in", "cot_in", "seg_in", "mixer_in", "merge_in", "expand_in", "shrink_in", "fgain_in", "fshift_in", "mixb_in",
    "mergeb_in", "sgain_in", "sshift_in", "expandb_in", "shrinkb_in",
)
OUT = ("hidden", "gin", "gmix", "gmerge", "gexp", "gshr", "vout")


def kernel(names, *refs):
    r = types.SimpleNamespace(**dict(zip(names, refs, strict=True)))
    me = place_of()
    sib = moved(me, c=1 - me.c)
    swap = moved(me, yl=me.c, c=me.yl)
    here = me.yl == me.c
    seq = me.z * 2 + me.yl
    ypos = me.yh * 2 + me.yl
    pending = []
    sends, recvs = {}, {}

    def send_of(*key):
        return r.send.at[sends.setdefault(key, len(sends))]

    def recv_of(*key):
        return r.recv.at[recvs.setdefault(key, len(recvs))]

    def copy_to(to, src, dst, *key, recv=None):
        return remote(src, dst, send_of(*key), recv_of(*(recv or key)), to)

    def arrived(size, *key):
        remote(size, size, r.send.at[0], recv_of(*key), sib).wait_recv()

    def wait_sent(size, *key):
        remote(size, size, send_of(*key), r.recv.at[0], sib).wait_send()

    def sent(size, *key):
        pending.append(lambda: wait_sent(size, *key))

    def sent_unless(alone, size, *key):
        def finish():
            @pl.when(jnp.logical_not(alone))
            def _():
                wait_sent(size, *key)

        pending.append(finish)

    def start_unless(alone, to, src, dst, *key, recv=None):
        @pl.when(alone)
        def _():
            pltpu.make_async_copy(src, dst, recv_of(*(recv or key))).start()

        @pl.when(jnp.logical_not(alone))
        def _():
            copy_to(to, src, dst, *key, recv=recv).start()

    zero32 = jnp.zeros((48, 32), BF)
    for i in range(3):
        r.units[i] = lanes(r.mixer_in[:, 96 * i : 96 * i + 96], zero32)
    own = (me.z, me.yl, me.yh, me.x, me.c)
    r.wz[own[1:]] = lanes(r.expand_in[...], r.shrink_in[...])
    r.m_w[own[0:3]] = lanes(r.merge_in[...], zero32)
    mixb = r.mixb_in[...].astype(F32).reshape(1, 192)
    small = [(FIRST_GAIN, r.fgain_in), (FIRST_SHIFT, r.fshift_in), (MERGE_BIAS, r.mergeb_in)]
    small += [(SECOND_GAIN, r.sgain_in), (SECOND_SHIFT, r.sshift_in), (SHRINK_BIAS, r.shrinkb_in)]
    for row, ref in small:
        r.vecs[seq, row : row + 1, 0:96] = ref[...].astype(F32).reshape(1, 96)
    expb = r.expandb_in[...].astype(F32).reshape(1, SHARD)
    for k in range(2):
        r.vecs[seq, MIXER_BIAS + k : MIXER_BIAS + k + 1, 0:96] = mixb[:, 96 * k : 96 * k + 96]
    for k in range(3):
        r.vecs[seq, EXPAND_BIAS + k : EXPAND_BIAS + k + 1, :] = expb[:, TOK * k : TOK * k + TOK]
    r.segs[0] = r.seg_in[...].astype(F32)

    peers = [shifted(shifted(me, "z", dz), "y", dy) for dz in range(4) for dy in range(4) if dz or dy]
    peers += [shifted(me, "x", d) for d in (1, 2, 3)] + [sib, shifted(sib, "y", 2)]
    peers += [moved(shifted(me, "z", d), yl=1 - me.yl, c=1 - me.c) for d in range(4)]
    peers += [shifted(shifted(at, "x", d), "y", dy) for d in (1, 2, 3) for at, dy in ((sib, 0), (me, 2), (sib, 2))]
    barrier = pltpu.get_barrier_semaphore()
    for p in peers:
        pl.semaphore_signal(barrier, inc=1, device_id=device(p), device_id_type=MESH)
    pl.semaphore_wait(barrier, len(peers))

    def send_own(name):
        at = getattr(r, name).at[me.z]
        for d in (1, 3, 2):
            copy_to(shifted(me, "z", d), at, at, name).start()

    def send_along(name, src_of, order=(1, 3, 2)):
        for d in order:
            to = shifted(me, "z", d)
            copy_to(to, src_of(to.z), getattr(r, name).at[me.z], name).start()

    def take_along(name):
        arrived(getattr(r, name).at[0:3], name)
        sent(getattr(r, name).at[0:3], name)

    def send_back(src, dst, key):
        start_unless(here, swap, src, dst, *key)
        sent_unless(here, src, *key)

    for i in range(3):
        u = 3 * seq + i
        group = lax.div(lax.rem(u, 8), 2)
        dst = r.wl.at[lax.rem(u, 2), me.yh, lax.div(u, 8)]
        for dy in range(4):
            y = lax.rem(ypos + dy, 4)
            to = moved(me, z=group, yh=lax.div(y, 2), yl=lax.rem(y, 2))
            if dy:
                copy_to(to, r.units.at[i], dst, "unit").start()
            else:
                start_unless(group == me.z, to, r.units.at[i], dst, "unit", i, recv=("unit",))
        sent_unless(group == me.z, r.units.at[i], "unit", i)
    sent(r.rmf.at[:, 0:3], "unit")

    def seq_peer(k):
        at = shifted(me, "z", k // 2)
        return moved(at, yl=1 - me.yl) if k % 2 else at

    for k in range(1, 8):
        copy_to(seq_peer(k), r.vecs.at[seq], r.vecs.at[seq], "vec").start()
    sent(r.vr, "vec")
    def upper(ref, h):
        return ref.at[pl.ds(64 * h, 64)]

    for h in range(2):
        send_back(upper(r.x_in, h), upper(r.xall.at[me.z], h), ("x", h))

    def x_along(h):
        arrived(upper(r.xall.at[0], 0), "x", h)
        at = upper(r.xall.at[me.z], h)
        for d in (1, 3, 2):
            copy_to(shifted(me, "z", d), at, at, "xall").start()

    @pl.when(here)
    def _():
        x_along(0)
        x_along(1)


    def plane(ref, d):
        return ref.at[(slice(None),) * (len(ref.shape) - 4) + (lax.rem(me.x + 4 - d, 4), me.c)]

    def plane_start(ref, key):
        at = plane(ref, 0)
        for d in (1, 3, 2):
            copy_to(shifted(me, "x", d), at, at, key, recv=(key, d)).start()
        copy_to(sib, at, at, key, "hand").start()
        every = (slice(None),) * (len(ref.shape) - 4)
        sent(ref.at[every + (slice(0, 3), me.c)], key)
        sent(ref.at[every + (slice(0, 4), me.c)], key, "hand")

    def plane_hand(ref, key):
        for d in (1, 3, 2):
            at = plane(ref, d)
            arrived(at, key, d)
            copy_to(sib, at, at, key, "hand").start()

    def plane_finish(ref, key):
        every = (slice(None),) * (len(ref.shape) - 4)
        arrived(ref.at[every + (slice(0, 4), 1 - me.c)], key, "hand")

    def column(d):
        at = shifted(me, "y", -d)
        return r.wz.at[at.yl, at.yh, :, me.c]

    def column_start():
        for d in (1, 3, 2):
            copy_to(shifted(me, "y", d), column(0), column(0), "column", recv=("column", d)).start()
        copy_to(sib, column(0), column(0), "column", "hand").start()
        sent(r.wz.at[0, :, 0:3], "column")
        sent(r.wz.at[:, :, :, me.c], "column", "hand")

    def column_hand():
        for d in (1, 3, 2):
            arrived(column(d), "column", d)
            copy_to(sib, column(d), column(d), "column", "hand").start()

    def column_finish():
        arrived(r.wz.at[:, :, :, 1 - me.c], "column", "hand")

    copy_to(sib, r.segs.at[0], r.segs.at[1], "seg").start()
    sent(r.segs.at[0], "seg")
    own = r.wz.at[me.yl, me.yh, me.x, me.c]
    for d in (1, 3, 2):
        copy_to(shifted(me, "x", d), own, own, "hidden").start()
    sent(r.gy, "hidden")
    around = [(dz, dy) for dz in (1, 3, 0, 2) for dy in (0, 1, 3, 2) if dz or dy]
    at = r.m_w.at[me.z, me.yl, me.yh]
    for dz, dy in around:
        copy_to(shifted(shifted(me, "z", dz), "y", dy), at, at, "merge").start()
    sent(r.m_y, "merge")
    send_back(r.cot_in, r.call.at[me.z], ("cot",))
    arrived(r.wl, "unit")
    for yh in range(2):
        pieces = [r.wl[half, yh, kind, :, 0:96] for kind in (1, 2, 0) for half in range(2)]
        r.wm[yh, me.x, me.c] = lanes(*pieces, jnp.zeros((48, 64), BF))

    plane_start(r.wm, "mixer")
    @pl.when(jnp.logical_not(here))
    def _():
        x_along(0)
        x_along(1)

    arrived(r.gy, "hidden")
    column_start()
    arrived(r.vr, "vec")

    def whole(row):
        return jnp.concatenate([r.vecs[s, row : row + 1, 0:96] for s in range(8)], axis=1)


    gain1, shift1 = whole(FIRST_GAIN), whole(FIRST_SHIFT)
    plane_hand(r.wm, "mixer")
    arrived(r.m_y, "merge")
    for yh in range(2):
        pieces = [r.m_w[s // 2, s % 2, yh, :, 0:96] for s in range(8)]
        r.mc[yh, me.x, me.c] = lanes(*pieces)
    plane_start(r.mc, "merge x")
    take_along("xall")
    arrived(r.call.at[0], "cot")
    send_own("call")
    for b in range(4):
        normed, rstd = norm_parts(r.xall[b].astype(F32))
        r.n1all[b] = normed
        r.rstd1[b] = jnp.broadcast_to(rstd, (TOK, TOK))
        first = normed * gain1 + shift1
        r.fall[b] = first.astype(BF)
        r.fallt[:, :, :, TOK * b : TOK * b + TOK] = turned(first.astype(BF)).reshape(8, 2, 48, TOK)
    plane_finish(r.wm, "mixer")

    at = r.fallt.at[:, 1 - me.c]
    copy_to(sib, at, r.fallt_sib, "first").start()
    sent(r.fallt_sib, "first")
    def mixer(at):
        return r.wm[:, :, :, :, at].reshape(D, -1)

    first = r.fall[...].reshape(4 * TOK, D)

    def mixer_bias(at, half):
        row = MIXER_BIAS + half
        return r.vecs[at, row : row + 1, 0:96]

    kv = nn(first, mixer(slice(0, 384)))
    keys = kv[:, 0:192].astype(BF)
    vbias = lanes(mixer_bias(4 + me.z, 0), mixer_bias(4 + me.z, 1))
    values = (kv[:, 192:384] + vbias).astype(BF)
    packed = lanes(keys, values[:, 128:192], values[:, 0:128])
    for b in range(4):
        r.kv_all[b, me.c] = packed[TOK * b : TOK * b + TOK]
    at = r.kv_all.at[:, me.c]
    copy_to(sib, at, at, "kv").start()
    sent(at, "kv")
    qbias = lanes(mixer_bias(me.z, 0), mixer_bias(me.z, 1))
    q = nn(first, mixer(slice(384, HEADS3)))[:, 0:192]
    q = (q + qbias).astype(BF) * jnp.asarray(0.125, BF)
    q = lanes(q, jnp.zeros((4 * TOK, 64), BF))
    for b in range(4):
        r.q_all[b] = q[TOK * b : TOK * b + TOK]
        r.kvt[:, tile(2 * b + me.c)] = turned(packed[TOK * b : TOK * b + TOK])
    arrived(r.segs.at[1], "seg")
    arrived(r.kv_all.at[:, 1 - me.c], "kv")
    for b in range(4):
        r.kvt[:, tile(2 * b + 1 - me.c)] = turned(r.kv_all[b, 1 - me.c])

    seg = jnp.where(here, r.segs[0], r.segs[1])

    def starts(bound):
        return jnp.sum(jnp.where(seg < bound, 1.0, 0.0), axis=(0, 1), keepdims=True).astype(jnp.int32)

    begin1, begin2 = starts(0.5), starts(1.5)
    lane = lax.broadcasted_iota(jnp.int32, (TOK, TOK), 1)

    def allowed_of(b):
        n = 256 * (b + 1)
        qpos = 256 * b + TOK * me.c + lax.broadcasted_iota(jnp.int32, (1, TOK), 1)
        low = jnp.where(qpos < begin1, 0, jnp.where(qpos < begin2, begin1, begin2))
        kpos = lax.broadcasted_iota(jnp.int32, (n, TOK), 0)
        return (kpos <= qpos) & (kpos >= low)

    def keys_of(b, h):
        at = slice(0, 128) if h < 2 else slice(128, 256)
        return r.kv_all[0 : b + 1, :, :, at].reshape(256 * (b + 1), TOK)

    def values_of(b, h):
        at = slice(256, 384) if h < 2 else slice(128, 256)
        return r.kv_all[0 : b + 1, :, :, at].reshape(256 * (b + 1), TOK)

    K_ROWS = (0, 64, 128)
    V_ROWS = (256, 320, 192)

    def one_head(v, upper):
        keep = lane >= 64 if upper else lane < 64
        return jnp.where(keep, v, jnp.zeros_like(v))

    def query_of(b, h):
        return one_head(r.q_all[b, :, 0:128] if h < 2 else r.q_all[b, :, 128:256], h == 1)

    spare = []
    for b in (3, 2, 1, 0):
        n = 256 * (b + 1)
        allowed = allowed_of(b)
        outs = []
        for h in range(3):
            scores = jnp.where(allowed, nt(keys_of(b, h), query_of(b, h)), NEG)
            top = jnp.max(scores, axis=0, keepdims=True)
            expo = jnp.exp(scores - top)
            total = jnp.sum(expo, axis=0, keepdims=True)
            r.lse[b, h : h + 1, :] = top + jnp.log(total)
            weights = (expo * (1.0 / total)).astype(BF)
            outs.append(nn(r.kvt[V_ROWS[h] : V_ROWS[h] + 64, 0:n], weights))
        r.att_all[me.z, b] = jnp.concatenate(outs[0:2], axis=0).T.astype(BF)
        spare.append(outs[2])
        ready = [b]
        if b % 2 == 0:
            r.att_all[me.z, 4 + b // 2] = jnp.concatenate([spare[-1], spare[-2]], axis=0).T.astype(BF)
            ready.append(4 + b // 2)
        for k in ready:
            for d in (1, 3, 2):
                at = r.att_all.at[me.z, k]
                copy_to(shifted(me, "z", d), at, at, "att", recv=("att", b // 2)).start()
        if b == 1:
            column_hand()
        if b == 0:
            plane_hand(r.mc, "merge x")
    sent(r.att_all.at[0:3], "att")
    take_along("call")
    for b in range(4):
        r.cott[:, TOK * b : TOK * b + TOK] = turned(r.call[b])
    plane_finish(r.mc, "merge x")
    merge = r.mc[...].reshape(D, D)

    column_finish()
    gain2, shift2, b_merge = whole(SECOND_GAIN), whole(SECOND_SHIFT), whole(MERGE_BIAS)

    def hidden(first):
        return lanes(*[r.wz[yl, :, :, :, :, first : first + SHARD].reshape(D, SHARD) for yl in range(2)])

    bias = lanes(*[r.vecs[2 * me.z + yl, EXPAND_BIAS + k : EXPAND_BIAS + k + 1] for yl in range(2) for k in range(3)])
    sums2 = []
    for pair in (1, 0):
        arrived(r.att_all.at[0:3, 0:3], "att", pair)
        rows = slice(2 * pair, 2 * pair + 2)
        for b in (2 * pair, 2 * pair + 1):
            at = slice(64 * (b % 2), 64 * (b % 2) + 64)
            r.att[b] = lanes(*[v for g in range(4) for v in (r.att_all[g, b], r.att_all[g, 4 + pair, :, at])])
        branch = nn(r.att[rows].reshape(2 * TOK, D), merge)
        middle = r.xall[rows].reshape(2 * TOK, D).astype(F32) + branch + b_merge
        r.mid[rows] = middle.reshape(2, TOK, D)
        n2, rstd2 = norm_parts(middle)
        second = (n2 * gain2 + shift2).astype(BF)
        r.second[rows] = second.reshape(2, TOK, D)
        pre = nn(second, hidden(0)) + bias
        square = pre * pre
        tanh = jnp.tanh(0.7978845608028654 * (pre + 0.044715 * square * pre))
        r.active[rows] = (0.5 * pre * (1.0 + tanh)).astype(BF).reshape(2, TOK, WIDE)
        slope = 0.5 * (1.0 + tanh) + 0.5 * pre * (1.0 - tanh * tanh) * (
            0.7978845608028654 * (1.0 + 0.134145 * square)
        )
        cot = r.call[rows]
        d_pre = (nn(cot.reshape(2 * TOK, D), hidden(SHARD)) * slope).astype(BF)
        r.dpre[rows] = d_pre.reshape(2, TOK, WIDE)
        d_second = nt(d_pre, hidden(0))
        sums2.append((col_sums(d_second * n2), col_sums(d_second)))
        d_middle = norm_back(d_second, gain2, n2, rstd2)
        d_branch = []
        for i in range(2):
            own = jnp.where(me.z == 2 * pair + i, cot[i].astype(F32), 0.0) + d_middle[TOK * i : TOK * i + TOK]
            r.dmid[2 * pair + i] = own
            d_branch.append(own.astype(BF))
            r.dbr[2 * pair + i] = d_branch[-1]
        d_att = nt(jnp.concatenate(d_branch, axis=0), merge).astype(BF)
        low, high = d_att[0:TOK], d_att[TOK : 2 * TOK]
        for z in range(4):
            at = 192 * z
            r.do_send[pair, z, 0] = low[:, at : at + 128]
            r.do_send[pair, z, 1] = high[:, at : at + 128]
            r.do_send[pair, z, 2] = lanes(low[:, at + 128 : at + 192], high[:, at + 128 : at + 192])
        for d in (1, 3, 2):
            to = shifted(me, "z", d)
            copy_to(to, r.do_send.at[pair, to.z], r.do_recv.at[pair, me.z], "do", recv=("do", pair)).start()
        r.do_recv[pair, me.z] = r.do_send[pair, me.z]
    sent(r.do_send.at[:, 0:3], "do")

    zeros = jnp.zeros((TOK, 32), BF)

    for b in range(4):
        r.attt[:, TOK * b : TOK * b + TOK] = turned(r.att[b])
    grad = nn(r.attt[...], r.dbr[...].reshape(4 * TOK, D)).astype(BF)
    r.m_g[...] = grad.reshape(2, 4, 2, 48, D)
    copy_to(sib, r.m_g.at[:, :, 1 - me.c], r.m_r0, "merge", "pair").start()
    sent(r.m_r0, "merge", "pair")

    sums = col_sums(r.dpre[...].reshape(4 * TOK, WIDE))
    r.vg[...] = jnp.zeros((8, 16, TOK), F32)
    for yl in range(2):
        for k in range(3):
            at = TOK * (3 * yl + k)
            r.vg[2 * me.z + yl, EXPAND_BIAS + k : EXPAND_BIAS + k + 1, :] = sums[:, at : at + TOK]
    for b in range(4):
        r.secondt[:, TOK * b : TOK * b + TOK] = turned(r.second[b])
    halves = ((r.g_e, r.g_e0), (r.g_s, r.g_s0))

    def hidden_gradient(k, left, right):
        ref, pair0 = halves[k]
        grad = nn(left[...], right[...].reshape(4 * TOK, WIDE)).astype(BF)
        for yl in range(2):
            ref[yl] = grad[:, SHARD * yl : SHARD * yl + SHARD].reshape(2, 4, 2, 48, SHARD)
        copy_to(sib, ref.at[:, :, :, 1 - me.c], pair0, "hidden", k, "pair").start()
        sent(pair0, "hidden", k, "pair")

    hidden_gradient(0, r.secondt, r.dpre)

    hidden_gradient(1, r.cott, r.active)
    result = nt(r.active[...].reshape(4 * TOK, WIDE), hidden(SHARD)).astype(BF)
    for b in range(4):
        r.res_send[b] = result[TOK * b : TOK * b + TOK]
    send_along("res_recv", lambda z: r.res_send.at[z])
    r.res_recv[me.z] = r.res_send[me.z]

    def pair_sum(ref, own, key):
        arrived(ref, *key, "pair")
        every = (slice(None),) * (len(ref.shape) - 2)
        ref[...] = (ref[...].astype(F32) + own[every + (me.c,)].astype(F32)).astype(BF)

    def plane_send(ref, got, key):
        every = (slice(None),) * (len(ref.shape) - 3)
        for d in (1, 3, 2):
            to = shifted(me, "x", d)
            copy_to(to, ref.at[every + (to.x,)], got.at[d - 1], key, "sum").start()
        sent(got, key, "sum")

    def plane_total(ref, got, key):
        arrived(got, key, "sum")
        total = ref[(slice(None),) * (len(ref.shape) - 3) + (me.x,)].astype(F32)
        for d in range(3):
            total += got[d].astype(F32)
        return total.astype(BF)

    def expand_sum():
        pair_sum(r.g_e0, r.g_e, ("hidden", 0))
        for d in (1, 3, 2):
            to = shifted(me, "y", d)
            copy_to(to, r.g_e0.at[to.yl, to.yh], r.g_y.at[d - 1], "expand y").start()
        sent(r.g_y, "expand y")

    def expand_next():
        arrived(r.g_y, "expand y")
        total = r.g_e0[me.yl, me.yh].astype(F32)
        for d in range(3):
            total += r.g_y[d].astype(F32)
        r.g_ex[...] = total.astype(BF)
        for d in (1, 3, 2):
            to = shifted(me, "x", d)
            copy_to(to, r.g_ex.at[to.x], r.g_got.at[0, d - 1], "expand x").start()
        sent(r.g_got.at[0], "expand x")

    def shrink_sum():
        pair_sum(r.g_s0, r.g_s, ("hidden", 1))
        plane_send(r.g_s0, r.g_x, "shrink")

    def shrink_next():
        r.g_sy[...] = plane_total(r.g_s0, r.g_x, "shrink")
        for d in (1, 3, 2):
            to = shifted(me, "y", d)
            copy_to(to, r.g_sy.at[to.yl, to.yh], r.g_got.at[1, d - 1], "shrink y").start()
        sent(r.g_got.at[1], "shrink y")

    def merge_next():
        total = plane_total(r.m_r0, r.m_x, "merge")
        for s in range(8):
            for yh in range(2):
                r.m_t[s // 2, s % 2, yh] = lanes(total[yh, :, 96 * s : 96 * s + 96], zero32)
        for i, (dz, dy) in enumerate(around):
            to = shifted(shifted(me, "z", dz), "y", dy)
            copy_to(to, r.m_t.at[to.z, to.yl, to.yh], r.m_y.at[i], "merge all").start()
        sent(r.m_y, "merge all")

    pair_sum(r.m_r0, r.m_g, ("merge",))
    plane_send(r.m_r0, r.m_x, "merge")
    expand_sum()
    r.dkv[...] = jnp.zeros((8 * TOK, SHARD), F32)
    sent(r.dkv_got, "dkv")

    def take_pair(p):
        arrived(r.do_recv.at[p, 0:3], "do", p)
        total = r.do_recv[p, 0].astype(F32)
        for z in range(1, 4):
            total += r.do_recv[p, z].astype(F32)
        r.do_all[2 * p, :, 0:TOK] = total[0].astype(BF)
        r.do_all[2 * p, :, TOK : 2 * TOK] = lanes(total[2, :, 64:128], total[2, :, 0:64]).astype(BF)
        r.do_all[2 * p + 1, :, 0:TOK] = total[1].astype(BF)
        r.do_all[2 * p + 1, :, TOK : 2 * TOK] = total[2].astype(BF)

    def pair(l0, l1, r0, r1):
        return nn(jnp.concatenate([l0, l1], axis=1), jnp.concatenate([r0, r1], axis=0))

    gain_sum, shift_sum = [], []

    def finish_block(b):
        arrived(r.dkv_got.at[b], "dkv", b)
        own = pl.multiple_of(256 * b + TOK * me.c, TOK)
        dkv = (r.dkv[pl.ds(own, TOK), :] + r.dkv_got[b].astype(F32)).astype(BF)
        dq = r.dq[b]
        r.dpad[b] = lanes(dkv[:, 0:192], dkv[:, 256:384], dkv[:, 192:256], dq[:, 0:192], jnp.zeros((TOK, 64), BF))
        at = r.dpad.at[b]
        copy_to(sib, at, r.dpad_sib.at[b], "dpad").start()

    def first_back(blocks):
        rows = jnp.concatenate([r.dpad[b] for b in blocks], axis=0)
        d_first = nt(rows, mixer(slice(0, HEADS3)))
        for i, b in enumerate(blocks):
            part, normed = d_first[TOK * i : TOK * i + TOK], r.n1all[b]
            gain_sum.append(col_sums(part * normed))
            shift_sum.append(col_sums(part))
            r.df_send[b] = (r.dmid[b] + norm_back(part, gain1, normed, r.rstd1[b][:, 0:1])).astype(BF)

    for b in (3, 2, 1, 0):
        if b % 2:
            take_pair(b // 2)
        n = 256 * (b + 1)
        allowed = allowed_of(b)
        dqs, dss, pbs, dos, qs = [], [], [], [], []
        for h in range(3):
            q = query_of(b, h)
            do = one_head(r.do_all[b, :, 0:128] if h < 2 else r.do_all[b, :, 128:256], h > 0)
            scores = jnp.where(allowed, nt(keys_of(b, h), q), NEG)
            probs = jnp.exp(scores - r.lse[b, h : h + 1, :])
            dw = nt(values_of(b, h), do)
            centre = jnp.sum(probs * dw, axis=0, keepdims=True)
            ds = (probs * (dw - centre)).astype(BF)
            dqs.append(nn(r.kvt[K_ROWS[h] : K_ROWS[h] + 64, 0:n], ds))
            dss.append(ds)
            pbs.append(probs.astype(BF))
            dos.append(do)
            qs.append(q)
        dqs.append(jnp.zeros((64, TOK), F32))
        r.dq[b] = (jnp.concatenate(dqs, axis=0) * 0.125).T.astype(BF)
        r.dkv[0:n, 0:128] += pair(dss[0], dss[1], qs[0], qs[1])
        r.dkv[0:n, 128:256] += pair(dss[2], pbs[2], qs[2], dos[2])
        r.dkv[0:n, 256:384] += pair(pbs[0], pbs[1], dos[0], dos[1])
        other = pl.multiple_of(256 * b + TOK * (1 - me.c), TOK)
        r.dkv_sib[b] = r.dkv[pl.ds(other, TOK), :].astype(BF)
        copy_to(sib, r.dkv_sib.at[b], r.dkv_got.at[b], "dkv", recv=("dkv", b)).start()
        if b == 3:
            shrink_sum()
        if b in (2, 1):
            finish_block(b + 1)
    finish_block(1)
    first_back((3, 1))
    finish_block(0)
    first_back((2, 0))
    g_gain_b, g_shift_b = sums2[0][0] + sums2[1][0], sums2[0][1] + sums2[1][1]
    g_b_shrink = col_sums(r.call[me.z])
    g_b_merge = col_sums(r.dbr[...].reshape(4 * TOK, D))
    rows = [(MERGE_BIAS, g_b_merge), (SECOND_GAIN, g_gain_b), (SECOND_SHIFT, g_shift_b), (SHRINK_BIAS, g_b_shrink)]
    for s in range(8):
        for row, value in rows:
            r.vg[s, row : row + 1, 0:96] = value[:, 96 * s : 96 * s + 96]

    arrived(r.fallt_sib, "first")
    sums = col_sums(r.dpad[...].reshape(4 * TOK, HEADS3))
    for half in range(2):
        row = MIXER_BIAS + half
        r.vg[me.z, row : row + 1, 0:96] = sums[:, 384 + 96 * half : 480 + 96 * half]
        r.vg[4 + me.z, row : row + 1, 0:96] = sums[:, 192 + 96 * half : 288 + 96 * half]
    gain_a, shift_a = sum(gain_sum), sum(shift_sum)
    for s in range(8):
        r.vg[s, FIRST_GAIN : FIRST_GAIN + 1, 0:96] = gain_a[:, 96 * s : 96 * s + 96]
        r.vg[s, FIRST_SHIFT : FIRST_SHIFT + 1, 0:96] = shift_a[:, 96 * s : 96 * s + 96]

    for k in range(1, 8):
        to = seq_peer(k)
        copy_to(to, r.vg.at[to.z * 2 + to.yl], r.vr.at[k - 1], "rows").start()
    sent(r.vr, "rows")
    for d in (1, 3):
        to = shifted(me, "z", d)
        copy_to(to, r.df_send.at[to.z], r.df_recv.at[me.z], "near").start()
    sent(r.df_recv.at[0:2], "near")
    to = shifted(swap, "z", 2)
    copy_to(to, r.df_send.at[to.z], r.gin_far, "far").start()
    sent(r.gin_far, "far")

    arrived(r.dpad_sib, "dpad")
    sent(r.dpad, "dpad")
    left = jnp.concatenate([r.fallt[:, me.c].reshape(D // 2, 4 * TOK), r.fallt_sib[...].reshape(D // 2, 4 * TOK)], axis=1)
    right = jnp.concatenate([ref[...].reshape(4 * TOK, HEADS3) for ref in (r.dpad, r.dpad_sib)], axis=0)
    r.rm0[...] = nn(left, right).astype(BF).reshape(2, 4, 48, HEADS3)
    plane_send(r.rm0, r.rmx, "mixer")
    take_along("res_recv")
    result = r.mid[me.z] + whole(SHRINK_BIAS)
    for b in range(4):
        result += r.res_recv[b].astype(F32)
    r.hid[...] = result.astype(BF)
    send_back(r.hid, r.hid_recv, ("hid",))
    expand_next()
    merge_next()
    arrived(r.vr, "rows")
    total = r.vg[seq]
    for k in range(7):
        total += r.vr[k]
    ours = me.yh * 8 + me.x * 2 + me.c
    r.vx[ours] = total
    others = [(at, dx, dy) for at in (me, sib) for dx in range(4) for dy in (0, 2) if dx or dy or at is sib]
    for at, dx, dy in others:
        copy_to(shifted(shifted(at, "x", dx), "y", dy), r.vx.at[ours], r.vx.at[ours], "rows all").start()
    sent(r.vx.at[0:15], "rows all")
    shrink_next()
    total = plane_total(r.rm0, r.rmx, "mixer")
    for half in range(2):
        for yh in range(2):
            for kind in range(3):
                at = (384, 0, 192)[kind] + 96 * half
                r.rmy[half, yh, kind] = lanes(total[yh, :, at : at + 96], zero32)
    for dyh in range(2):
        yh = lax.rem(me.yh + dyh, 2)
        for half in range(2):
            for kind in range(3):
                u = 8 * kind + 2 * me.z + half
                owner = lax.div(u, 3)
                to = moved(me, yh=yh, z=lax.div(owner, 2), yl=lax.rem(owner, 2))
                src = r.rmy.at[half, yh, kind]
                dst = r.rmf.at[lax.rem(u, 3), ypos]
                if dyh:
                    copy_to(to, src, dst, "piece").start()
                else:
                    start_unless(owner == seq, to, src, dst, "piece", half, kind, recv=("piece",))
                    sent_unless(owner == seq, r.units.at[0], "piece", half, kind)
    sent(r.rmf.at[:, 0:2], "piece")
    arrived(r.df_recv.at[0:2], "near")
    parts = [r.df_send[me.z]] + [r.df_recv[shifted(me, "z", d).z] for d in (1, 3)]
    r.gin_send[...] = sum(part.astype(F32) for part in parts).astype(BF)
    send_back(r.gin_send, r.gin_recv, ("gin",))

    arrived(r.hid_recv, "hid")
    r.hidden[...] = r.hid_recv[...]
    arrived(r.g_got.at[0], "expand x")
    r.gexp[...] = r.g_ex[me.x].astype(F32) + sum(r.g_got[0, d].astype(F32) for d in range(3))
    arrived(r.g_got.at[1], "shrink y")
    r.gshr[...] = r.g_sy[me.yl, me.yh].astype(F32) + sum(r.g_got[1, d].astype(F32) for d in range(3))
    arrived(r.m_y, "merge all")
    total = r.m_t[me.z, me.yl, me.yh].astype(F32)
    for i in range(15):
        total += r.m_y[i].astype(F32)
    r.gmerge[...] = total[:, 0:96]
    arrived(r.gin_recv, "gin")
    arrived(r.gin_far, "far")
    r.gin[...] = r.gin_recv[...].astype(F32) + r.gin_far[...].astype(F32)
    arrived(r.vx.at[0:15], "rows all")
    total = r.vx[0]
    for k in range(1, 16):
        total += r.vx[k]
    r.vout[...] = total
    arrived(r.rmf, "piece")
    for i in range(3):
        total = jnp.zeros((48, TOK), F32)
        for y in range(4):
            total += r.rmf[i, y].astype(F32)
        r.gmix[:, 96 * i : 96 * i + 96] = total[:, 0:96]
    for finish in pending:
        finish()
    if (len(sends), len(recvs)) != (SENDS, RECVS):
        raise ValueError((len(sends), len(recvs)))


def scratches():
    v, dma = pltpu.VMEM, pltpu.SemaphoreType.DMA
    blocks = (2, 4, 2, 48)
    s = dict(
        m_w=v((4, 2, 2, 48, TOK), BF),
        m_g=v(blocks + (D,), BF),
        m_r0=v((2, 4, 48, D), BF),
        m_x=v((3, 2, 48, D), BF),
        m_t=v((4, 2, 2, 48, TOK), BF),
        m_y=v((15, 48, TOK), BF),
        mc=v(blocks + (D,), BF),
        wz=v((2,) + blocks + (WIDE,), BF),
        g_e=v((2,) + blocks + (SHARD,), BF),
        g_s=v((2,) + blocks + (SHARD,), BF),
        g_e0=v((2, 2, 4, 48, SHARD), BF),
        g_s0=v((2, 2, 4, 48, SHARD), BF),
        g_y=v((3, 4, 48, SHARD), BF),
        g_x=v((3, 2, 2, 48, SHARD), BF),
        g_ex=v((4, 48, SHARD), BF),
        g_sy=v((2, 2, 48, SHARD), BF),
        g_got=v((2, 3, 48, SHARD), BF),
        gy=v((3, 48, WIDE), BF),
        units=v((3, 48, TOK), BF),
        wl=v((2, 2, 3, 48, TOK), BF),
        wm=v(blocks + (HEADS3,), BF),
        rm0=v((2, 4, 48, HEADS3), BF),
        rmx=v((3, 2, 48, HEADS3), BF),
        rmy=v((2, 2, 3, 48, TOK), BF),
        rmf=v((3, 4, 48, TOK), BF),
        vecs=v((8, 16, TOK), F32),
        segs=v((2, 8, TOK), F32),
        fallt=v((8, 2, 48, 4 * TOK), BF),
        fallt_sib=v((8, 48, 4 * TOK), BF),
        cott=v((D, 4 * TOK), BF),
        secondt=v((D, 4 * TOK), BF),
        attt=v((D, 4 * TOK), BF),
        rstd1=v((4, TOK, TOK), F32),
        dmid=v((4, TOK, D), F32),
        q_all=v((4, TOK, 256), BF),
        kv_all=v((4, 2, TOK, SHARD), BF),
        kvt=v((SHARD, 8 * TOK), BF),
        lse=v((4, 8, TOK), F32),
        att_all=v((4, 6, TOK, TOK), BF),
        dkv=v((8 * TOK, SHARD), F32),
        dkv_sib=v((4, TOK, SHARD), BF),
        dkv_got=v((4, TOK, SHARD), BF),
        dq=v((4, TOK, 256), BF),
        dpad=v((4, TOK, HEADS3), BF),
        dpad_sib=v((4, TOK, HEADS3), BF),
        do_send=v((2, 4, 3, TOK, TOK), BF),
        do_recv=v((2, 4, 3, TOK, TOK), BF),
        do_all=v((4, TOK, 256), BF),
        n1all=v((4, TOK, D), F32),
        mid=v((4, TOK, D), F32),
    )
    for name in ("xall", "call", "fall", "att", "second", "dbr", "res_send", "res_recv", "df_send", "df_recv"):
        s[name] = v((4, TOK, D), BF)
    for name in ("active", "dpre"):
        s[name] = v((4, TOK, WIDE), BF)
    for name in ("hid", "hid_recv", "gin_send", "gin_recv", "gin_far"):
        s[name] = v((TOK, D), BF)
    for name, count in (("vg", 8), ("vr", 7), ("vx", 16)):
        s[name] = v((count, 16, TOK), F32)
    s["send"], s["recv"] = dma((SENDS,)), dma((RECVS,))
    return s


def finish(hidden, gin, gmix, gmerge, gexp, gshr, vout, *outs):
    for ref, out in zip((hidden, gin, gmix, gmerge, gexp, gshr), outs[:6], strict=True):
        out[...] = ref[...]
    v = vout[...]
    rows = (FIRST_GAIN, FIRST_SHIFT, MERGE_BIAS, SECOND_GAIN, SECOND_SHIFT, SHRINK_BIAS)
    for row, out in zip(rows, outs[6:12], strict=True):
        out[...] = v[row : row + 1, 0:96].reshape(96)
    outs[12][...] = lanes(v[MIXER_BIAS : MIXER_BIAS + 1, 0:96], v[MIXER_BIAS + 1 : MIXER_BIAS + 2, 0:96]).reshape(192)
    outs[13][...] = lanes(*[v[EXPAND_BIAS + k : EXPAND_BIAS + k + 1] for k in range(3)]).reshape(SHARD)


def body(
    residual_in, cotangent, segments, first_gain, first_shift, mixer_weight, mixer_bias, merge_weight, merge_bias,
    second_gain, second_shift, expand_weight, expand_bias, shrink_weight, shrink_bias,
):
    vmem = pl.BlockSpec(memory_space=pltpu.VMEM)
    scratch = scratches()
    shapes = [((TOK, D), BF), ((TOK, D), F32), ((48, 288), F32), ((48, 96), F32), ((48, SHARD), F32), ((48, SHARD), F32)]
    held = [jax.ShapeDtypeStruct(*s) for s in shapes]
    parts = pl.pallas_call(
        functools.partial(kernel, IN + OUT + tuple(scratch)),
        out_shape=held + [jax.ShapeDtypeStruct((16, TOK), F32)],
        in_specs=[vmem] * len(IN),
        out_specs=[vmem] * len(OUT),
        scratch_shapes=list(scratch.values()),
        compiler_params=pltpu.CompilerParams(
            collective_id=0, has_side_effects=True, vmem_limit_bytes=62 * 1024 * 1024
        ),
    )(
        residual_in[0], cotangent[0], segments.reshape(8, TOK), mixer_weight, merge_weight, expand_weight,
        shrink_weight.T, first_gain, first_shift, mixer_bias, merge_bias, second_gain, second_shift, expand_bias,
        shrink_bias,
    )
    vectors = [jax.ShapeDtypeStruct((n,), F32) for n in (96, 96, 96, 96, 96, 96, 192, SHARD)]
    hidden, gin, gmix, gmerge, gexp, gshr, fg, fs, mb, sg, ss, sb, xb, eb = pl.pallas_call(
        finish, out_shape=held + vectors, in_specs=[vmem] * 7, out_specs=[vmem] * 14
    )(*parts)
    return hidden[None], gin[None], fg, fs, gmix, xb, gmerge, mb, sg, ss, gexp, eb, gshr.T, sb


def solution(mesh):
    vector, matrix = P("seq"), P("dp", "seq")
    tokens = P("dp", "seq", None)
    return jax.shard_map(
        body,
        mesh=mesh,
        in_specs=(
            tokens, tokens, P("dp", None), vector, vector, matrix, vector, matrix, vector, vector, vector, matrix, vector,
            P("seq", "dp"), vector,
        ),
        out_specs=(
            tokens, tokens, vector, vector, matrix, vector, matrix, vector, vector, vector, matrix, vector,
            P("seq", "dp"), vector,
        ),
        check_vma=False,
    )
```

```python
import functools
import types

import jax
import jax.numpy as jnp
from jax import lax
from jax.experimental import pallas as pl
from jax.experimental.pallas import tpu as pltpu
from jax.sharding import PartitionSpec as P


D = 768
HD = 64
TOK = 128
SHARD = 384
HEADS3 = 640
WIDE = 768
EPS = 1e-05
NEG = -1e30
MESH = pl.DeviceIdType.MESH
BF = jnp.bfloat16
F32 = jnp.float32
SENDS, RECVS = 49, 51
FIRST_GAIN, FIRST_SHIFT, MIXER_BIAS, MERGE_BIAS, SECOND_GAIN, SECOND_SHIFT, SHRINK_BIAS, EXPAND_BIAS = 0, 1, 2, 4, 5, 6, 7, 8


def place_of():
    dp, seq = lax.axis_index("dp"), lax.axis_index("seq")
    return types.SimpleNamespace(
        x=lax.rem(lax.div(dp, 2), 4),
        yh=lax.div(dp, 8),
        yl=lax.rem(seq, 2),
        z=lax.div(seq, 2),
        c=lax.rem(dp, 2),
    )


def moved(at, **to):
    new = types.SimpleNamespace(**vars(at))
    for name, value in to.items():
        setattr(new, name, value)
    return new


def shifted(at, axis, d):
    d = d % 4
    if axis == "x":
        return moved(at, x=lax.rem(at.x + d, 4))
    if axis == "z":
        return moved(at, z=lax.rem(at.z + d, 4))
    y = lax.rem(at.yh * 2 + at.yl + d, 4)
    return moved(at, yh=lax.div(y, 2), yl=lax.rem(y, 2))


def device(at):
    return (at.yh * 8 + at.x * 2 + at.c, at.z * 2 + at.yl)


def nn(a, b):
    return jnp.dot(a, b, preferred_element_type=F32)


def nt(a, b):
    return lax.dot_general(a, b, (((1,), (1,)), ((), ())), preferred_element_type=F32)


def remote(src, dst, send, recv, to):
    return pltpu.make_async_remote_copy(
        src_ref=src, dst_ref=dst, send_sem=send, recv_sem=recv, device_id=device(to), device_id_type=MESH
    )


def norm_parts(v):
    centred = v - jnp.mean(v, axis=-1, keepdims=True)
    rstd = lax.rsqrt(jnp.mean(centred * centred, axis=-1, keepdims=True) + EPS)
    return centred * rstd, rstd


def norm_back(dy, gain, normed, rstd):
    dn = dy * gain
    return rstd * (
        dn
        - jnp.mean(dn, axis=-1, keepdims=True)
        - normed * jnp.mean(dn * normed, axis=-1, keepdims=True)
    )


def col_sums(v):
    return jnp.sum(v.astype(F32), axis=0, keepdims=True)


def turned(v):
    return v.astype(F32).T.astype(BF)


def lanes(*pieces):
    return jnp.concatenate(pieces, axis=1)


def tile(k):
    return pl.ds(pl.multiple_of(k * TOK, TOK), TOK)


IN = (
    "x_in", "cot_in", "seg_in", "mixer_in", "merge_in", "expand_in", "shrink_in", "fgain_in", "fshift_in", "mixb_in",
    "mergeb_in", "sgain_in", "sshift_in", "expandb_in", "shrinkb_in",
)
OUT = ("hidden", "gin", "gmix", "gmerge", "gexp", "gshr", "vout")


def kernel(names, *refs):
    r = types.SimpleNamespace(**dict(zip(names, refs, strict=True)))
    me = place_of()
    sib = moved(me, c=1 - me.c)
    swap = moved(me, yl=me.c, c=me.yl)
    here = me.yl == me.c
    seq = me.z * 2 + me.yl
    ypos = me.yh * 2 + me.yl
    pending = []
    sends, recvs = {}, {}

    def send_of(*key):
        return r.send.at[sends.setdefault(key, len(sends))]

    def recv_of(*key):
        return r.recv.at[recvs.setdefault(key, len(recvs))]

    def copy_to(to, src, dst, *key, recv=None):
        return remote(src, dst, send_of(*key), recv_of(*(recv or key)), to)

    def arrived(size, *key):
        remote(size, size, r.send.at[0], recv_of(*key), sib).wait_recv()

    def wait_sent(size, *key):
        remote(size, size, send_of(*key), r.recv.at[0], sib).wait_send()

    def sent(size, *key):
        pending.append(lambda: wait_sent(size, *key))

    def sent_unless(alone, size, *key):
        def finish():
            @pl.when(jnp.logical_not(alone))
            def _():
                wait_sent(size, *key)

        pending.append(finish)

    def start_unless(alone, to, src, dst, *key, recv=None):
        @pl.when(alone)
        def _():
            pltpu.make_async_copy(src, dst, recv_of(*(recv or key))).start()

        @pl.when(jnp.logical_not(alone))
        def _():
            copy_to(to, src, dst, *key, recv=recv).start()

    zero32 = jnp.zeros((48, 32), BF)
    for i in range(3):
        r.units[i] = lanes(r.mixer_in[:, 96 * i : 96 * i + 96], zero32)
    own = (me.z, me.yl, me.yh, me.x, me.c)
    r.wz[own[1:]] = lanes(r.expand_in[...], r.shrink_in[...])
    r.m_w[own[0:3]] = lanes(r.merge_in[...], zero32)
    mixb = r.mixb_in[...].astype(F32).reshape(1, 192)
    small = [(FIRST_GAIN, r.fgain_in), (FIRST_SHIFT, r.fshift_in), (MERGE_BIAS, r.mergeb_in)]
    small += [(SECOND_GAIN, r.sgain_in), (SECOND_SHIFT, r.sshift_in), (SHRINK_BIAS, r.shrinkb_in)]
    for row, ref in small:
        r.vecs[seq, row : row + 1, 0:96] = ref[...].astype(F32).reshape(1, 96)
    expb = r.expandb_in[...].astype(F32).reshape(1, SHARD)
    for k in range(2):
        r.vecs[seq, MIXER_BIAS + k : MIXER_BIAS + k + 1, 0:96] = mixb[:, 96 * k : 96 * k + 96]
    for k in range(3):
        r.vecs[seq, EXPAND_BIAS + k : EXPAND_BIAS + k + 1, :] = expb[:, TOK * k : TOK * k + TOK]
    r.segs[0] = r.seg_in[...].astype(F32)

    peers = [shifted(shifted(me, "z", dz), "y", dy) for dz in range(4) for dy in range(4) if dz or dy]
    peers += [shifted(me, "x", d) for d in (1, 2, 3)] + [sib, shifted(sib, "y", 2)]
    peers += [moved(shifted(me, "z", d), yl=1 - me.yl, c=1 - me.c) for d in range(4)]
    peers += [shifted(shifted(at, "x", d), "y", dy) for d in (1, 2, 3) for at, dy in ((sib, 0), (me, 2), (sib, 2))]
    barrier = pltpu.get_barrier_semaphore()
    for p in peers:
        pl.semaphore_signal(barrier, inc=1, device_id=device(p), device_id_type=MESH)
    pl.semaphore_wait(barrier, len(peers))

    def send_own(name):
        at = getattr(r, name).at[me.z]
        for d in (1, 3, 2):
            copy_to(shifted(me, "z", d), at, at, name).start()

    def send_along(name, src_of, order=(1, 3, 2)):
        for d in order:
            to = shifted(me, "z", d)
            copy_to(to, src_of(to.z), getattr(r, name).at[me.z], name).start()

    def take_along(name):
        arrived(getattr(r, name).at[0:3], name)
        sent(getattr(r, name).at[0:3], name)

    def send_back(src, dst, key):
        start_unless(here, swap, src, dst, *key)
        sent_unless(here, src, *key)

    for i in range(3):
        u = 3 * seq + i
        group = lax.div(lax.rem(u, 8), 2)
        dst = r.wl.at[lax.rem(u, 2), me.yh, lax.div(u, 8)]
        for dy in range(4):
            y = lax.rem(ypos + dy, 4)
            to = moved(me, z=group, yh=lax.div(y, 2), yl=lax.rem(y, 2))
            if dy:
                copy_to(to, r.units.at[i], dst, "unit").start()
            else:
                start_unless(group == me.z, to, r.units.at[i], dst, "unit", i, recv=("unit",))
        sent_unless(group == me.z, r.units.at[i], "unit", i)
    sent(r.rmf.at[:, 0:3], "unit")

    def seq_peer(k):
        at = shifted(me, "z", k // 2)
        return moved(at, yl=1 - me.yl) if k % 2 else at

    for k in range(1, 8):
        copy_to(seq_peer(k), r.vecs.at[seq], r.vecs.at[seq], "vec").start()
    sent(r.vr, "vec")
    def upper(ref, h):
        return ref.at[pl.ds(64 * h, 64)]

    for h in range(2):
        send_back(upper(r.x_in, h), upper(r.xall.at[me.z], h), ("x", h))

    def x_along(h):
        arrived(upper(r.xall.at[0], 0), "x", h)
        at = upper(r.xall.at[me.z], h)
        for d in (1, 3, 2):
            copy_to(shifted(me, "z", d), at, at, "xall").start()

    @pl.when(here)
    def _():
        x_along(0)
        x_along(1)


    def plane(ref, d):
        return ref.at[(slice(None),) * (len(ref.shape) - 4) + (lax.rem(me.x + 4 - d, 4), me.c)]

    def plane_start(ref, key):
        at = plane(ref, 0)
        for d in (1, 3, 2):
            copy_to(shifted(me, "x", d), at, at, key, recv=(key, d)).start()
        copy_to(sib, at, at, key, "hand").start()
        every = (slice(None),) * (len(ref.shape) - 4)
        sent(ref.at[every + (slice(0, 3), me.c)], key)
        sent(ref.at[every + (slice(0, 4), me.c)], key, "hand")

    def plane_hand(ref, key):
        for d in (1, 3, 2):
            at = plane(ref, d)
            arrived(at, key, d)
            copy_to(sib, at, at, key, "hand").start()

    def plane_finish(ref, key):
        every = (slice(None),) * (len(ref.shape) - 4)
        arrived(ref.at[every + (slice(0, 4), 1 - me.c)], key, "hand")

    def column(d):
        at = shifted(me, "y", -d)
        return r.wz.at[at.yl, at.yh, :, me.c]

    def column_start():
        for d in (1, 3, 2):
            copy_to(shifted(me, "y", d), column(0), column(0), "column", recv=("column", d)).start()
        copy_to(sib, column(0), column(0), "column", "hand").start()
        sent(r.wz.at[0, :, 0:3], "column")
        sent(r.wz.at[:, :, :, me.c], "column", "hand")

    def column_hand():
        for d in (1, 3, 2):
            arrived(column(d), "column", d)
            copy_to(sib, column(d), column(d), "column", "hand").start()

    def column_finish():
        arrived(r.wz.at[:, :, :, 1 - me.c], "column", "hand")

    copy_to(sib, r.segs.at[0], r.segs.at[1], "seg").start()
    sent(r.segs.at[0], "seg")
    own = r.wz.at[me.yl, me.yh, me.x, me.c]
    for d in (1, 3, 2):
        copy_to(shifted(me, "x", d), own, own, "hidden").start()
    sent(r.gy, "hidden")
    around = [(dz, dy) for dz in (1, 3, 0, 2) for dy in (0, 1, 3, 2) if dz or dy]
    at = r.m_w.at[me.z, me.yl, me.yh]
    for dz, dy in around:
        copy_to(shifted(shifted(me, "z", dz), "y", dy), at, at, "merge").start()
    sent(r.m_y, "merge")
    send_back(r.cot_in, r.call.at[me.z], ("cot",))
    arrived(r.wl, "unit")
    for yh in range(2):
        pieces = [r.wl[half, yh, kind, :, 0:96] for kind in (1, 2, 0) for half in range(2)]
        r.wm[yh, me.x, me.c] = lanes(*pieces, jnp.zeros((48, 64), BF))

    plane_start(r.wm, "mixer")
    @pl.when(jnp.logical_not(here))
    def _():
        x_along(0)
        x_along(1)

    arrived(r.gy, "hidden")
    column_start()
    arrived(r.vr, "vec")

    def whole(row):
        return jnp.concatenate([r.vecs[s, row : row + 1, 0:96] for s in range(8)], axis=1)


    gain1, shift1 = whole(FIRST_GAIN), whole(FIRST_SHIFT)
    plane_hand(r.wm, "mixer")
    arrived(r.m_y, "merge")
    for yh in range(2):
        pieces = [r.m_w[s // 2, s % 2, yh, :, 0:96] for s in range(8)]
        r.mc[yh, me.x, me.c] = lanes(*pieces)
    plane_start(r.mc, "merge x")
    take_along("xall")
    arrived(r.call.at[0], "cot")
    send_own("call")
    for b in range(4):
        normed, rstd = norm_parts(r.xall[b].astype(F32))
        r.n1all[b] = normed
        r.rstd1[b] = jnp.broadcast_to(rstd, (TOK, TOK))
        first = normed * gain1 + shift1
        r.fall[b] = first.astype(BF)
        r.fallt[:, :, :, TOK * b : TOK * b + TOK] = turned(first.astype(BF)).reshape(8, 2, 48, TOK)
    plane_finish(r.wm, "mixer")

    at = r.fallt.at[:, 1 - me.c]
    copy_to(sib, at, r.fallt_sib, "first").start()
    sent(r.fallt_sib, "first")
    def mixer(at):
        return r.wm[:, :, :, :, at].reshape(D, -1)

    first = r.fall[...].reshape(4 * TOK, D)

    def mixer_bias(at, half):
        row = MIXER_BIAS + half
        return r.vecs[at, row : row + 1, 0:96]

    kv = nn(first, mixer(slice(0, 384)))
    keys = kv[:, 0:192].astype(BF)
    vbias = lanes(mixer_bias(4 + me.z, 0), mixer_bias(4 + me.z, 1))
    values = (kv[:, 192:384] + vbias).astype(BF)
    packed = lanes(keys, values[:, 128:192], values[:, 0:128])
    for b in range(4):
        r.kv_all[b, me.c] = packed[TOK * b : TOK * b + TOK]
    at = r.kv_all.at[:, me.c]
    copy_to(sib, at, at, "kv").start()
    sent(at, "kv")
    qbias = lanes(mixer_bias(me.z, 0), mixer_bias(me.z, 1))
    q = nn(first, mixer(slice(384, HEADS3)))[:, 0:192]
    q = (q + qbias).astype(BF) * jnp.asarray(0.125, BF)
    q = lanes(q, jnp.zeros((4 * TOK, 64), BF))
    for b in range(4):
        r.q_all[b] = q[TOK * b : TOK * b + TOK]
        r.kvt[:, tile(2 * b + me.c)] = turned(packed[TOK * b : TOK * b + TOK])
    arrived(r.segs.at[1], "seg")
    arrived(r.kv_all.at[:, 1 - me.c], "kv")
    for b in range(4):
        r.kvt[:, tile(2 * b + 1 - me.c)] = turned(r.kv_all[b, 1 - me.c])

    seg = jnp.where(here, r.segs[0], r.segs[1])

    def starts(bound):
        return jnp.sum(jnp.where(seg < bound, 1.0, 0.0), axis=(0, 1), keepdims=True).astype(jnp.int32)

    begin1, begin2 = starts(0.5), starts(1.5)
    lane = lax.broadcasted_iota(jnp.int32, (TOK, TOK), 1)

    def allowed_of(b):
        n = 256 * (b + 1)
        qpos = 256 * b + TOK * me.c + lax.broadcasted_iota(jnp.int32, (1, TOK), 1)
        low = jnp.where(qpos < begin1, 0, jnp.where(qpos < begin2, begin1, begin2))
        kpos = lax.broadcasted_iota(jnp.int32, (n, TOK), 0)
        return (kpos <= qpos) & (kpos >= low)

    def keys_of(b, h):
        at = slice(0, 128) if h < 2 else slice(128, 256)
        return r.kv_all[0 : b + 1, :, :, at].reshape(256 * (b + 1), TOK)

    def values_of(b, h):
        at = slice(256, 384) if h < 2 else slice(128, 256)
        return r.kv_all[0 : b + 1, :, :, at].reshape(256 * (b + 1), TOK)

    K_ROWS = (0, 64, 128)
    V_ROWS = (256, 320, 192)

    def one_head(v, upper):
        keep = lane >= 64 if upper else lane < 64
        return jnp.where(keep, v, jnp.zeros_like(v))

    def query_of(b, h):
        return one_head(r.q_all[b, :, 0:128] if h < 2 else r.q_all[b, :, 128:256], h == 1)

    spare = []
    for b in (3, 2, 1, 0):
        n = 256 * (b + 1)
        allowed = allowed_of(b)
        outs = []
        for h in range(3):
            scores = jnp.where(allowed, nt(keys_of(b, h), query_of(b, h)), NEG)
            top = jnp.max(scores, axis=0, keepdims=True)
            expo = jnp.exp(scores - top)
            total = jnp.sum(expo, axis=0, keepdims=True)
            r.lse[b, h : h + 1, :] = top + jnp.log(total)
            weights = (expo * (1.0 / total)).astype(BF)
            outs.append(nn(r.kvt[V_ROWS[h] : V_ROWS[h] + 64, 0:n], weights))
        r.att_all[me.z, b] = jnp.concatenate(outs[0:2], axis=0).T.astype(BF)
        spare.append(outs[2])
        ready = [b]
        if b % 2 == 0:
            r.att_all[me.z, 4 + b // 2] = jnp.concatenate([spare[-1], spare[-2]], axis=0).T.astype(BF)
            ready.append(4 + b // 2)
        for k in ready:
            for d in (1, 3, 2):
                at = r.att_all.at[me.z, k]
                copy_to(shifted(me, "z", d), at, at, "att", recv=("att", b // 2)).start()
        if b == 1:
            column_hand()
        if b == 0:
            plane_hand(r.mc, "merge x")
    sent(r.att_all.at[0:3], "att")
    take_along("call")
    for b in range(4):
        r.cott[:, TOK * b : TOK * b + TOK] = turned(r.call[b])
    plane_finish(r.mc, "merge x")
    merge = r.mc[...].reshape(D, D)

    column_finish()
    gain2, shift2, b_merge = whole(SECOND_GAIN), whole(SECOND_SHIFT), whole(MERGE_BIAS)

    def hidden(first):
        return lanes(*[r.wz[yl, :, :, :, :, first : first + SHARD].reshape(D, SHARD) for yl in range(2)])

    bias = lanes(*[r.vecs[2 * me.z + yl, EXPAND_BIAS + k : EXPAND_BIAS + k + 1] for yl in range(2) for k in range(3)])
    sums2 = []
    for pair in (1, 0):
        arrived(r.att_all.at[0:3, 0:3], "att", pair)
        rows = slice(2 * pair, 2 * pair + 2)
        for b in (2 * pair, 2 * pair + 1):
            at = slice(64 * (b % 2), 64 * (b % 2) + 64)
            r.att[b] = lanes(*[v for g in range(4) for v in (r.att_all[g, b], r.att_all[g, 4 + pair, :, at])])
        branch = nn(r.att[rows].reshape(2 * TOK, D), merge)
        middle = r.xall[rows].reshape(2 * TOK, D).astype(F32) + branch + b_merge
        r.mid[rows] = middle.reshape(2, TOK, D)
        n2, rstd2 = norm_parts(middle)
        second = (n2 * gain2 + shift2).astype(BF)
        r.second[rows] = second.reshape(2, TOK, D)
        pre = nn(second, hidden(0)) + bias
        square = pre * pre
        tanh = jnp.tanh(0.7978845608028654 * (pre + 0.044715 * square * pre))
        r.active[rows] = (0.5 * pre * (1.0 + tanh)).astype(BF).reshape(2, TOK, WIDE)
        slope = 0.5 * (1.0 + tanh) + 0.5 * pre * (1.0 - tanh * tanh) * (
            0.7978845608028654 * (1.0 + 0.134145 * square)
        )
        cot = r.call[rows]
        d_pre = (nn(cot.reshape(2 * TOK, D), hidden(SHARD)) * slope).astype(BF)
        r.dpre[rows] = d_pre.reshape(2, TOK, WIDE)
        d_second = nt(d_pre, hidden(0))
        sums2.append((col_sums(d_second * n2), col_sums(d_second)))
        d_middle = norm_back(d_second, gain2, n2, rstd2)
        d_branch = []
        for i in range(2):
            own = jnp.where(me.z == 2 * pair + i, cot[i].astype(F32), 0.0) + d_middle[TOK * i : TOK * i + TOK]
            r.dmid[2 * pair + i] = own
            d_branch.append(own.astype(BF))
            r.dbr[2 * pair + i] = d_branch[-1]
        d_att = nt(jnp.concatenate(d_branch, axis=0), merge).astype(BF)
        low, high = d_att[0:TOK], d_att[TOK : 2 * TOK]
        for z in range(4):
            at = 192 * z
            r.do_send[pair, z, 0] = low[:, at : at + 128]
            r.do_send[pair, z, 1] = high[:, at : at + 128]
            r.do_send[pair, z, 2] = lanes(low[:, at + 128 : at + 192], high[:, at + 128 : at + 192])
        for d in (1, 3, 2):
            to = shifted(me, "z", d)
            copy_to(to, r.do_send.at[pair, to.z], r.do_recv.at[pair, me.z], "do", recv=("do", pair)).start()
        r.do_recv[pair, me.z] = r.do_send[pair, me.z]
    sent(r.do_send.at[:, 0:3], "do")

    zeros = jnp.zeros((TOK, 32), BF)

    for b in range(4):
        r.attt[:, TOK * b : TOK * b + TOK] = turned(r.att[b])
    grad = nn(r.attt[...], r.dbr[...].reshape(4 * TOK, D)).astype(BF)
    r.m_g[...] = grad.reshape(2, 4, 2, 48, D)
    copy_to(sib, r.m_g.at[:, :, 1 - me.c], r.m_r0, "merge", "pair").start()
    sent(r.m_r0, "merge", "pair")

    sums = col_sums(r.dpre[...].reshape(4 * TOK, WIDE))
    r.vg[...] = jnp.zeros((8, 16, TOK), F32)
    for yl in range(2):
        for k in range(3):
            at = TOK * (3 * yl + k)
            r.vg[2 * me.z + yl, EXPAND_BIAS + k : EXPAND_BIAS + k + 1, :] = sums[:, at : at + TOK]
    for b in range(4):
        r.secondt[:, TOK * b : TOK * b + TOK] = turned(r.second[b])
    halves = ((r.g_e, r.g_e0), (r.g_s, r.g_s0))

    def hidden_gradient(k, left, right):
        ref, pair0 = halves[k]
        grad = nn(left[...], right[...].reshape(4 * TOK, WIDE)).astype(BF)
        for yl in range(2):
            ref[yl] = grad[:, SHARD * yl : SHARD * yl + SHARD].reshape(2, 4, 2, 48, SHARD)
        copy_to(sib, ref.at[:, :, :, 1 - me.c], pair0, "hidden", k, "pair").start()
        sent(pair0, "hidden", k, "pair")

    hidden_gradient(0, r.secondt, r.dpre)

    hidden_gradient(1, r.cott, r.active)
    result = nt(r.active[...].reshape(4 * TOK, WIDE), hidden(SHARD)).astype(BF)
    for b in range(4):
        r.res_send[b] = result[TOK * b : TOK * b + TOK]
    send_along("res_recv", lambda z: r.res_send.at[z])
    r.res_recv[me.z] = r.res_send[me.z]

    def pair_sum(ref, own, key):
        arrived(ref, *key, "pair")
        every = (slice(None),) * (len(ref.shape) - 2)
        ref[...] = (ref[...].astype(F32) + own[every + (me.c,)].astype(F32)).astype(BF)

    def plane_send(ref, got, key):
        every = (slice(None),) * (len(ref.shape) - 3)
        for d in (1, 3, 2):
            to = shifted(me, "x", d)
            copy_to(to, ref.at[every + (to.x,)], got.at[d - 1], key, "sum").start()
        sent(got, key, "sum")

    def plane_total(ref, got, key):
        arrived(got, key, "sum")
        total = ref[(slice(None),) * (len(ref.shape) - 3) + (me.x,)].astype(F32)
        for d in range(3):
            total += got[d].astype(F32)
        return total.astype(BF)

    def expand_sum():
        pair_sum(r.g_e0, r.g_e, ("hidden", 0))
        for d in (1, 3, 2):
            to = shifted(me, "y", d)
            copy_to(to, r.g_e0.at[to.yl, to.yh], r.g_y.at[d - 1], "expand y").start()
        sent(r.g_y, "expand y")

    def expand_next():
        arrived(r.g_y, "expand y")
        total = r.g_e0[me.yl, me.yh].astype(F32)
        for d in range(3):
            total += r.g_y[d].astype(F32)
        r.g_ex[...] = total.astype(BF)
        for d in (1, 3, 2):
            to = shifted(me, "x", d)
            copy_to(to, r.g_ex.at[to.x], r.g_got.at[0, d - 1], "expand x").start()
        sent(r.g_got.at[0], "expand x")

    def shrink_sum():
        pair_sum(r.g_s0, r.g_s, ("hidden", 1))
        plane_send(r.g_s0, r.g_x, "shrink")

    def shrink_next():
        r.g_sy[...] = plane_total(r.g_s0, r.g_x, "shrink")
        for d in (1, 3, 2):
            to = shifted(me, "y", d)
            copy_to(to, r.g_sy.at[to.yl, to.yh], r.g_got.at[1, d - 1], "shrink y").start()
        sent(r.g_got.at[1], "shrink y")

    def merge_next():
        total = plane_total(r.m_r0, r.m_x, "merge")
        for s in range(8):
            for yh in range(2):
                r.m_t[s // 2, s % 2, yh] = lanes(total[yh, :, 96 * s : 96 * s + 96], zero32)
        for i, (dz, dy) in enumerate(around):
            to = shifted(shifted(me, "z", dz), "y", dy)
            copy_to(to, r.m_t.at[to.z, to.yl, to.yh], r.m_y.at[i], "merge all").start()
        sent(r.m_y, "merge all")

    pair_sum(r.m_r0, r.m_g, ("merge",))
    plane_send(r.m_r0, r.m_x, "merge")
    expand_sum()
    r.dkv[...] = jnp.zeros((8 * TOK, SHARD), F32)
    sent(r.dkv_got, "dkv")

    def take_pair(p):
        arrived(r.do_recv.at[p, 0:3], "do", p)
        total = r.do_recv[p, 0].astype(F32)
        for z in range(1, 4):
            total += r.do_recv[p, z].astype(F32)
        r.do_all[2 * p, :, 0:TOK] = total[0].astype(BF)
        r.do_all[2 * p, :, TOK : 2 * TOK] = lanes(total[2, :, 64:128], total[2, :, 0:64]).astype(BF)
        r.do_all[2 * p + 1, :, 0:TOK] = total[1].astype(BF)
        r.do_all[2 * p + 1, :, TOK : 2 * TOK] = total[2].astype(BF)

    def pair(l0, l1, r0, r1):
        return nn(jnp.concatenate([l0, l1], axis=1), jnp.concatenate([r0, r1], axis=0))

    gain_sum, shift_sum = [], []

    def finish_block(b):
        arrived(r.dkv_got.at[b], "dkv", b)
        own = pl.multiple_of(256 * b + TOK * me.c, TOK)
        dkv = (r.dkv[pl.ds(own, TOK), :] + r.dkv_got[b].astype(F32)).astype(BF)
        dq = r.dq[b]
        r.dpad[b] = lanes(dkv[:, 0:192], dkv[:, 256:384], dkv[:, 192:256], dq[:, 0:192], jnp.zeros((TOK, 64), BF))
        at = r.dpad.at[b]
        copy_to(sib, at, r.dpad_sib.at[b], "dpad").start()

    def first_back(blocks):
        rows = jnp.concatenate([r.dpad[b] for b in blocks], axis=0)
        d_first = nt(rows, mixer(slice(0, HEADS3)))
        for i, b in enumerate(blocks):
            part, normed = d_first[TOK * i : TOK * i + TOK], r.n1all[b]
            gain_sum.append(col_sums(part * normed))
            shift_sum.append(col_sums(part))
            r.df_send[b] = (r.dmid[b] + norm_back(part, gain1, normed, r.rstd1[b][:, 0:1])).astype(BF)

    for b in (3, 2, 1, 0):
        if b % 2:
            take_pair(b // 2)
        n = 256 * (b + 1)
        allowed = allowed_of(b)
        dqs, dss, pbs, dos, qs = [], [], [], [], []
        for h in range(3):
            q = query_of(b, h)
            do = one_head(r.do_all[b, :, 0:128] if h < 2 else r.do_all[b, :, 128:256], h > 0)
            scores = jnp.where(allowed, nt(keys_of(b, h), q), NEG)
            probs = jnp.exp(scores - r.lse[b, h : h + 1, :])
            dw = nt(values_of(b, h), do)
            centre = jnp.sum(probs * dw, axis=0, keepdims=True)
            ds = (probs * (dw - centre)).astype(BF)
            dqs.append(nn(r.kvt[K_ROWS[h] : K_ROWS[h] + 64, 0:n], ds))
            dss.append(ds)
            pbs.append(probs.astype(BF))
            dos.append(do)
            qs.append(q)
        dqs.append(jnp.zeros((64, TOK), F32))
        r.dq[b] = (jnp.concatenate(dqs, axis=0) * 0.125).T.astype(BF)
        r.dkv[0:n, 0:128] += pair(dss[0], dss[1], qs[0], qs[1])
        r.dkv[0:n, 128:256] += pair(dss[2], pbs[2], qs[2], dos[2])
        r.dkv[0:n, 256:384] += pair(pbs[0], pbs[1], dos[0], dos[1])
        other = pl.multiple_of(256 * b + TOK * (1 - me.c), TOK)
        r.dkv_sib[b] = r.dkv[pl.ds(other, TOK), :].astype(BF)
        copy_to(sib, r.dkv_sib.at[b], r.dkv_got.at[b], "dkv", recv=("dkv", b)).start()
        if b == 3:
            shrink_sum()
        if b in (2, 1):
            finish_block(b + 1)
    finish_block(1)
    first_back((3, 1))
    finish_block(0)
    first_back((2, 0))
    g_gain_b, g_shift_b = sums2[0][0] + sums2[1][0], sums2[0][1] + sums2[1][1]
    g_b_shrink = col_sums(r.call[me.z])
    g_b_merge = col_sums(r.dbr[...].reshape(4 * TOK, D))
    rows = [(MERGE_BIAS, g_b_merge), (SECOND_GAIN, g_gain_b), (SECOND_SHIFT, g_shift_b), (SHRINK_BIAS, g_b_shrink)]
    for s in range(8):
        for row, value in rows:
            r.vg[s, row : row + 1, 0:96] = value[:, 96 * s : 96 * s + 96]

    arrived(r.fallt_sib, "first")
    sums = col_sums(r.dpad[...].reshape(4 * TOK, HEADS3))
    for half in range(2):
        row = MIXER_BIAS + half
        r.vg[me.z, row : row + 1, 0:96] = sums[:, 384 + 96 * half : 480 + 96 * half]
        r.vg[4 + me.z, row : row + 1, 0:96] = sums[:, 192 + 96 * half : 288 + 96 * half]
    gain_a, shift_a = sum(gain_sum), sum(shift_sum)
    for s in range(8):
        r.vg[s, FIRST_GAIN : FIRST_GAIN + 1, 0:96] = gain_a[:, 96 * s : 96 * s + 96]
        r.vg[s, FIRST_SHIFT : FIRST_SHIFT + 1, 0:96] = shift_a[:, 96 * s : 96 * s + 96]

    for k in range(1, 8):
        to = seq_peer(k)
        copy_to(to, r.vg.at[to.z * 2 + to.yl], r.vr.at[k - 1], "rows").start()
    sent(r.vr, "rows")
    for d in (1, 3):
        to = shifted(me, "z", d)
        copy_to(to, r.df_send.at[to.z], r.df_recv.at[me.z], "near").start()
    sent(r.df_recv.at[0:2], "near")
    to = shifted(swap, "z", 2)
    copy_to(to, r.df_send.at[to.z], r.gin_far, "far").start()
    sent(r.gin_far, "far")

    arrived(r.dpad_sib, "dpad")
    sent(r.dpad, "dpad")
    left = jnp.concatenate([r.fallt[:, me.c].reshape(D // 2, 4 * TOK), r.fallt_sib[...].reshape(D // 2, 4 * TOK)], axis=1)
    right = jnp.concatenate([ref[...].reshape(4 * TOK, HEADS3) for ref in (r.dpad, r.dpad_sib)], axis=0)
    r.rm0[...] = nn(left, right).astype(BF).reshape(2, 4, 48, HEADS3)
    plane_send(r.rm0, r.rmx, "mixer")
    take_along("res_recv")
    result = r.mid[me.z] + whole(SHRINK_BIAS)
    for b in range(4):
        result += r.res_recv[b].astype(F32)
    r.hid[...] = result.astype(BF)
    send_back(r.hid, r.hid_recv, ("hid",))
    expand_next()
    arrived(r.vr, "rows")
    total = r.vg[seq]
    for k in range(7):
        total += r.vr[k]
    ours = me.yh * 8 + me.x * 2 + me.c
    r.vx[ours] = total
    others = [(at, dx, dy) for at in (me, sib) for dx in range(4) for dy in (0, 2) if dx or dy or at is sib]
    for at, dx, dy in others:
        copy_to(shifted(shifted(at, "x", dx), "y", dy), r.vx.at[ours], r.vx.at[ours], "rows all").start()
    sent(r.vx.at[0:15], "rows all")
    merge_next()
    shrink_next()
    total = plane_total(r.rm0, r.rmx, "mixer")
    for half in range(2):
        for yh in range(2):
            for kind in range(3):
                at = (384, 0, 192)[kind] + 96 * half
                r.rmy[half, yh, kind] = lanes(total[yh, :, at : at + 96], zero32)
    for dyh in range(2):
        yh = lax.rem(me.yh + dyh, 2)
        for half in range(2):
            for kind in range(3):
                u = 8 * kind + 2 * me.z + half
                owner = lax.div(u, 3)
                to = moved(me, yh=yh, z=lax.div(owner, 2), yl=lax.rem(owner, 2))
                src = r.rmy.at[half, yh, kind]
                dst = r.rmf.at[lax.rem(u, 3), ypos]
                if dyh:
                    copy_to(to, src, dst, "piece").start()
                else:
                    start_unless(owner == seq, to, src, dst, "piece", half, kind, recv=("piece",))
                    sent_unless(owner == seq, r.units.at[0], "piece", half, kind)
    sent(r.rmf.at[:, 0:2], "piece")
    arrived(r.df_recv.at[0:2], "near")
    parts = [r.df_send[me.z]] + [r.df_recv[shifted(me, "z", d).z] for d in (1, 3)]
    r.gin_send[...] = sum(part.astype(F32) for part in parts).astype(BF)
    send_back(r.gin_send, r.gin_recv, ("gin",))

    arrived(r.hid_recv, "hid")
    r.hidden[...] = r.hid_recv[...]
    arrived(r.g_got.at[0], "expand x")
    r.gexp[...] = r.g_ex[me.x].astype(F32) + sum(r.g_got[0, d].astype(F32) for d in range(3))
    arrived(r.g_got.at[1], "shrink y")
    r.gshr[...] = r.g_sy[me.yl, me.yh].astype(F32) + sum(r.g_got[1, d].astype(F32) for d in range(3))
    arrived(r.m_y, "merge all")
    total = r.m_t[me.z, me.yl, me.yh].astype(F32)
    for i in range(15):
        total += r.m_y[i].astype(F32)
    r.gmerge[...] = total[:, 0:96]
    arrived(r.gin_recv, "gin")
    arrived(r.gin_far, "far")
    r.gin[...] = r.gin_recv[...].astype(F32) + r.gin_far[...].astype(F32)
    arrived(r.vx.at[0:15], "rows all")
    total = r.vx[0]
    for k in range(1, 16):
        total += r.vx[k]
    r.vout[...] = total
    arrived(r.rmf, "piece")
    for i in range(3):
        total = jnp.zeros((48, TOK), F32)
        for y in range(4):
            total += r.rmf[i, y].astype(F32)
        r.gmix[:, 96 * i : 96 * i + 96] = total[:, 0:96]
    for finish in pending:
        finish()
    if (len(sends), len(recvs)) != (SENDS, RECVS):
        raise ValueError((len(sends), len(recvs)))


def scratches():
    v, dma = pltpu.VMEM, pltpu.SemaphoreType.DMA
    blocks = (2, 4, 2, 48)
    s = dict(
        m_w=v((4, 2, 2, 48, TOK), BF),
        m_g=v(blocks + (D,), BF),
        m_r0=v((2, 4, 48, D), BF),
        m_x=v((3, 2, 48, D), BF),
        m_t=v((4, 2, 2, 48, TOK), BF),
        m_y=v((15, 48, TOK), BF),
        mc=v(blocks + (D,), BF),
        wz=v((2,) + blocks + (WIDE,), BF),
        g_e=v((2,) + blocks + (SHARD,), BF),
        g_s=v((2,) + blocks + (SHARD,), BF),
        g_e0=v((2, 2, 4, 48, SHARD), BF),
        g_s0=v((2, 2, 4, 48, SHARD), BF),
        g_y=v((3, 4, 48, SHARD), BF),
        g_x=v((3, 2, 2, 48, SHARD), BF),
        g_ex=v((4, 48, SHARD), BF),
        g_sy=v((2, 2, 48, SHARD), BF),
        g_got=v((2, 3, 48, SHARD), BF),
        gy=v((3, 48, WIDE), BF),
        units=v((3, 48, TOK), BF),
        wl=v((2, 2, 3, 48, TOK), BF),
        wm=v(blocks + (HEADS3,), BF),
        rm0=v((2, 4, 48, HEADS3), BF),
        rmx=v((3, 2, 48, HEADS3), BF),
        rmy=v((2, 2, 3, 48, TOK), BF),
        rmf=v((3, 4, 48, TOK), BF),
        vecs=v((8, 16, TOK), F32),
        segs=v((2, 8, TOK), F32),
        fallt=v((8, 2, 48, 4 * TOK), BF),
        fallt_sib=v((8, 48, 4 * TOK), BF),
        cott=v((D, 4 * TOK), BF),
        secondt=v((D, 4 * TOK), BF),
        attt=v((D, 4 * TOK), BF),
        rstd1=v((4, TOK, TOK), F32),
        dmid=v((4, TOK, D), F32),
        q_all=v((4, TOK, 256), BF),
        kv_all=v((4, 2, TOK, SHARD), BF),
        kvt=v((SHARD, 8 * TOK), BF),
        lse=v((4, 8, TOK), F32),
        att_all=v((4, 6, TOK, TOK), BF),
        dkv=v((8 * TOK, SHARD), F32),
        dkv_sib=v((4, TOK, SHARD), BF),
        dkv_got=v((4, TOK, SHARD), BF),
        dq=v((4, TOK, 256), BF),
        dpad=v((4, TOK, HEADS3), BF),
        dpad_sib=v((4, TOK, HEADS3), BF),
        do_send=v((2, 4, 3, TOK, TOK), BF),
        do_recv=v((2, 4, 3, TOK, TOK), BF),
        do_all=v((4, TOK, 256), BF),
        n1all=v((4, TOK, D), F32),
        mid=v((4, TOK, D), F32),
    )
    for name in ("xall", "call", "fall", "att", "second", "dbr", "res_send", "res_recv", "df_send", "df_recv"):
        s[name] = v((4, TOK, D), BF)
    for name in ("active", "dpre"):
        s[name] = v((4, TOK, WIDE), BF)
    for name in ("hid", "hid_recv", "gin_send", "gin_recv", "gin_far"):
        s[name] = v((TOK, D), BF)
    for name, count in (("vg", 8), ("vr", 7), ("vx", 16)):
        s[name] = v((count, 16, TOK), F32)
    s["send"], s["recv"] = dma((SENDS,)), dma((RECVS,))
    return s


def finish(hidden, gin, gmix, gmerge, gexp, gshr, vout, *outs):
    for ref, out in zip((hidden, gin, gmix, gmerge, gexp, gshr), outs[:6], strict=True):
        out[...] = ref[...]
    v = vout[...]
    rows = (FIRST_GAIN, FIRST_SHIFT, MERGE_BIAS, SECOND_GAIN, SECOND_SHIFT, SHRINK_BIAS)
    for row, out in zip(rows, outs[6:12], strict=True):
        out[...] = v[row : row + 1, 0:96].reshape(96)
    outs[12][...] = lanes(v[MIXER_BIAS : MIXER_BIAS + 1, 0:96], v[MIXER_BIAS + 1 : MIXER_BIAS + 2, 0:96]).reshape(192)
    outs[13][...] = lanes(*[v[EXPAND_BIAS + k : EXPAND_BIAS + k + 1] for k in range(3)]).reshape(SHARD)


def body(
    residual_in, cotangent, segments, first_gain, first_shift, mixer_weight, mixer_bias, merge_weight, merge_bias,
    second_gain, second_shift, expand_weight, expand_bias, shrink_weight, shrink_bias,
):
    vmem = pl.BlockSpec(memory_space=pltpu.VMEM)
    scratch = scratches()
    shapes = [((TOK, D), BF), ((TOK, D), F32), ((48, 288), F32), ((48, 96), F32), ((48, SHARD), F32), ((48, SHARD), F32)]
    held = [jax.ShapeDtypeStruct(*s) for s in shapes]
    parts = pl.pallas_call(
        functools.partial(kernel, IN + OUT + tuple(scratch)),
        out_shape=held + [jax.ShapeDtypeStruct((16, TOK), F32)],
        in_specs=[vmem] * len(IN),
        out_specs=[vmem] * len(OUT),
        scratch_shapes=list(scratch.values()),
        compiler_params=pltpu.CompilerParams(
            collective_id=0, has_side_effects=True, vmem_limit_bytes=62 * 1024 * 1024
        ),
    )(
        residual_in[0], cotangent[0], segments.reshape(8, TOK), mixer_weight, merge_weight, expand_weight,
        shrink_weight.T, first_gain, first_shift, mixer_bias, merge_bias, second_gain, second_shift, expand_bias,
        shrink_bias,
    )
    vectors = [jax.ShapeDtypeStruct((n,), F32) for n in (96, 96, 96, 96, 96, 96, 192, SHARD)]
    hidden, gin, gmix, gmerge, gexp, gshr, fg, fs, mb, sg, ss, sb, xb, eb = pl.pallas_call(
        finish, out_shape=held + vectors, in_specs=[vmem] * 7, out_specs=[vmem] * 14
    )(*parts)
    return hidden[None], gin[None], fg, fs, gmix, xb, gmerge, mb, sg, ss, gexp, eb, gshr.T, sb


def solution(mesh):
    vector, matrix = P("seq"), P("dp", "seq")
    tokens = P("dp", "seq", None)
    return jax.shard_map(
        body,
        mesh=mesh,
        in_specs=(
            tokens, tokens, P("dp", None), vector, vector, matrix, vector, matrix, vector, vector, vector, matrix, vector,
            P("seq", "dp"), vector,
        ),
        out_specs=(
            tokens, tokens, vector, vector, matrix, vector, matrix, vector, vector, vector, matrix, vector,
            P("seq", "dp"), vector,
        ),
        check_vma=False,
    )
```

```python
import functools
import types

import jax
import jax.numpy as jnp
from jax import lax
from jax.experimental import pallas as pl
from jax.experimental.pallas import tpu as pltpu
from jax.sharding import PartitionSpec as P


D = 768
HD = 64
TOK = 128
SHARD = 384
HEADS3 = 640
WIDE = 768
EPS = 1e-05
NEG = -1e30
MESH = pl.DeviceIdType.MESH
BF = jnp.bfloat16
F32 = jnp.float32
SENDS, RECVS = 49, 51
FIRST_GAIN, FIRST_SHIFT, MIXER_BIAS, MERGE_BIAS, SECOND_GAIN, SECOND_SHIFT, SHRINK_BIAS, EXPAND_BIAS = 0, 1, 2, 4, 5, 6, 7, 8


def place_of():
    dp, seq = lax.axis_index("dp"), lax.axis_index("seq")
    return types.SimpleNamespace(
        x=lax.rem(lax.div(dp, 2), 4),
        yh=lax.div(dp, 8),
        yl=lax.rem(seq, 2),
        z=lax.div(seq, 2),
        c=lax.rem(dp, 2),
    )


def moved(at, **to):
    new = types.SimpleNamespace(**vars(at))
    for name, value in to.items():
        setattr(new, name, value)
    return new


def shifted(at, axis, d):
    d = d % 4
    if axis == "x":
        return moved(at, x=lax.rem(at.x + d, 4))
    if axis == "z":
        return moved(at, z=lax.rem(at.z + d, 4))
    y = lax.rem(at.yh * 2 + at.yl + d, 4)
    return moved(at, yh=lax.div(y, 2), yl=lax.rem(y, 2))


def device(at):
    return (at.yh * 8 + at.x * 2 + at.c, at.z * 2 + at.yl)


def nn(a, b):
    return jnp.dot(a, b, preferred_element_type=F32)


def nt(a, b):
    return lax.dot_general(a, b, (((1,), (1,)), ((), ())), preferred_element_type=F32)


def remote(src, dst, send, recv, to):
    return pltpu.make_async_remote_copy(
        src_ref=src, dst_ref=dst, send_sem=send, recv_sem=recv, device_id=device(to), device_id_type=MESH
    )


def norm_parts(v):
    centred = v - jnp.mean(v, axis=-1, keepdims=True)
    rstd = lax.rsqrt(jnp.mean(centred * centred, axis=-1, keepdims=True) + EPS)
    return centred * rstd, rstd


def norm_back(dy, gain, normed, rstd):
    dn = dy * gain
    return rstd * (
        dn
        - jnp.mean(dn, axis=-1, keepdims=True)
        - normed * jnp.mean(dn * normed, axis=-1, keepdims=True)
    )


def col_sums(v):
    return jnp.sum(v.astype(F32), axis=0, keepdims=True)


def turned(v):
    return v.astype(F32).T.astype(BF)


def lanes(*pieces):
    return jnp.concatenate(pieces, axis=1)


def tile(k):
    return pl.ds(pl.multiple_of(k * TOK, TOK), TOK)


IN = (
    "x_in", "cot_in", "seg_in", "mixer_in", "merge_in", "expand_in", "shrink_in", "fgain_in", "fshift_in", "mixb_in",
    "mergeb_in", "sgain_in", "sshift_in", "expandb_in", "shrinkb_in",
)
OUT = ("hidden", "gin", "gmix", "gmerge", "gexp", "gshr", "vout")


def kernel(names, *refs):
    r = types.SimpleNamespace(**dict(zip(names, refs, strict=True)))
    me = place_of()
    sib = moved(me, c=1 - me.c)
    swap = moved(me, yl=me.c, c=me.yl)
    here = me.yl == me.c
    seq = me.z * 2 + me.yl
    ypos = me.yh * 2 + me.yl
    pending = []
    sends, recvs = {}, {}

    def send_of(*key):
        return r.send.at[sends.setdefault(key, len(sends))]

    def recv_of(*key):
        return r.recv.at[recvs.setdefault(key, len(recvs))]

    def copy_to(to, src, dst, *key, recv=None):
        return remote(src, dst, send_of(*key), recv_of(*(recv or key)), to)

    def arrived(size, *key):
        remote(size, size, r.send.at[0], recv_of(*key), sib).wait_recv()

    def wait_sent(size, *key):
        remote(size, size, send_of(*key), r.recv.at[0], sib).wait_send()

    def sent(size, *key):
        pending.append(lambda: wait_sent(size, *key))

    def sent_unless(alone, size, *key):
        def finish():
            @pl.when(jnp.logical_not(alone))
            def _():
                wait_sent(size, *key)

        pending.append(finish)

    def start_unless(alone, to, src, dst, *key, recv=None):
        @pl.when(alone)
        def _():
            pltpu.make_async_copy(src, dst, recv_of(*(recv or key))).start()

        @pl.when(jnp.logical_not(alone))
        def _():
            copy_to(to, src, dst, *key, recv=recv).start()

    zero32 = jnp.zeros((48, 32), BF)
    for i in range(3):
        r.units[i] = lanes(r.mixer_in[:, 96 * i : 96 * i + 96], zero32)
    own = (me.z, me.yl, me.yh, me.x, me.c)
    r.wz[own[1:]] = lanes(r.expand_in[...], r.shrink_in[...])
    r.m_w[own[0:3]] = lanes(r.merge_in[...], zero32)
    mixb = r.mixb_in[...].astype(F32).reshape(1, 192)
    small = [(FIRST_GAIN, r.fgain_in), (FIRST_SHIFT, r.fshift_in), (MERGE_BIAS, r.mergeb_in)]
    small += [(SECOND_GAIN, r.sgain_in), (SECOND_SHIFT, r.sshift_in), (SHRINK_BIAS, r.shrinkb_in)]
    for row, ref in small:
        r.vecs[seq, row : row + 1, 0:96] = ref[...].astype(F32).reshape(1, 96)
    expb = r.expandb_in[...].astype(F32).reshape(1, SHARD)
    for k in range(2):
        r.vecs[seq, MIXER_BIAS + k : MIXER_BIAS + k + 1, 0:96] = mixb[:, 96 * k : 96 * k + 96]
    for k in range(3):
        r.vecs[seq, EXPAND_BIAS + k : EXPAND_BIAS + k + 1, :] = expb[:, TOK * k : TOK * k + TOK]
    r.segs[0] = r.seg_in[...].astype(F32)

    peers = [shifted(shifted(me, "z", dz), "y", dy) for dz in range(4) for dy in range(4) if dz or dy]
    peers += [shifted(me, "x", d) for d in (1, 2, 3)] + [sib, shifted(sib, "y", 2)]
    peers += [moved(shifted(me, "z", d), yl=1 - me.yl, c=1 - me.c) for d in range(4)]
    peers += [shifted(shifted(at, "x", d), "y", dy) for d in (1, 2, 3) for at, dy in ((sib, 0), (me, 2), (sib, 2))]
    barrier = pltpu.get_barrier_semaphore()
    for p in peers:
        pl.semaphore_signal(barrier, inc=1, device_id=device(p), device_id_type=MESH)
    pl.semaphore_wait(barrier, len(peers))

    def send_own(name):
        at = getattr(r, name).at[me.z]
        for d in (1, 3, 2):
            copy_to(shifted(me, "z", d), at, at, name).start()

    def send_along(name, src_of, order=(1, 3, 2)):
        for d in order:
            to = shifted(me, "z", d)
            copy_to(to, src_of(to.z), getattr(r, name).at[me.z], name).start()

    def take_along(name):
        arrived(getattr(r, name).at[0:3], name)
        sent(getattr(r, name).at[0:3], name)

    def send_back(src, dst, key):
        start_unless(here, swap, src, dst, *key)
        sent_unless(here, src, *key)

    for i in range(3):
        u = 3 * seq + i
        group = lax.div(lax.rem(u, 8), 2)
        dst = r.wl.at[lax.rem(u, 2), me.yh, lax.div(u, 8)]
        for dy in range(4):
            y = lax.rem(ypos + dy, 4)
            to = moved(me, z=group, yh=lax.div(y, 2), yl=lax.rem(y, 2))
            if dy:
                copy_to(to, r.units.at[i], dst, "unit").start()
            else:
                start_unless(group == me.z, to, r.units.at[i], dst, "unit", i, recv=("unit",))
        sent_unless(group == me.z, r.units.at[i], "unit", i)
    sent(r.rmf.at[:, 0:3], "unit")

    def seq_peer(k):
        at = shifted(me, "z", k // 2)
        return moved(at, yl=1 - me.yl) if k % 2 else at

    for k in range(1, 8):
        copy_to(seq_peer(k), r.vecs.at[seq], r.vecs.at[seq], "vec").start()
    sent(r.vr, "vec")
    def upper(ref, h):
        return ref.at[pl.ds(64 * h, 64)]

    for h in range(2):
        send_back(upper(r.x_in, h), upper(r.xall.at[me.z], h), ("x", h))

    def x_along(h):
        arrived(upper(r.xall.at[0], 0), "x", h)
        at = upper(r.xall.at[me.z], h)
        for d in (1, 3, 2):
            copy_to(shifted(me, "z", d), at, at, "xall").start()

    @pl.when(here)
    def _():
        x_along(0)
        x_along(1)


    def plane(ref, d):
        return ref.at[(slice(None),) * (len(ref.shape) - 4) + (lax.rem(me.x + 4 - d, 4), me.c)]

    def plane_start(ref, key):
        at = plane(ref, 0)
        for d in (1, 3, 2):
            copy_to(shifted(me, "x", d), at, at, key, recv=(key, d)).start()
        copy_to(sib, at, at, key, "hand").start()
        every = (slice(None),) * (len(ref.shape) - 4)
        sent(ref.at[every + (slice(0, 3), me.c)], key)
        sent(ref.at[every + (slice(0, 4), me.c)], key, "hand")

    def plane_hand(ref, key):
        for d in (1, 3, 2):
            at = plane(ref, d)
            arrived(at, key, d)
            copy_to(sib, at, at, key, "hand").start()

    def plane_finish(ref, key):
        every = (slice(None),) * (len(ref.shape) - 4)
        arrived(ref.at[every + (slice(0, 4), 1 - me.c)], key, "hand")

    def column(d):
        at = shifted(me, "y", -d)
        return r.wz.at[at.yl, at.yh, :, me.c]

    def column_start():
        for d in (1, 3, 2):
            copy_to(shifted(me, "y", d), column(0), column(0), "column", recv=("column", d)).start()
        copy_to(sib, column(0), column(0), "column", "hand").start()
        sent(r.wz.at[0, :, 0:3], "column")
        sent(r.wz.at[:, :, :, me.c], "column", "hand")

    def column_hand():
        for d in (1, 3, 2):
            arrived(column(d), "column", d)
            copy_to(sib, column(d), column(d), "column", "hand").start()

    def column_finish():
        arrived(r.wz.at[:, :, :, 1 - me.c], "column", "hand")

    copy_to(sib, r.segs.at[0], r.segs.at[1], "seg").start()
    sent(r.segs.at[0], "seg")
    own = r.wz.at[me.yl, me.yh, me.x, me.c]
    for d in (1, 3, 2):
        copy_to(shifted(me, "x", d), own, own, "hidden").start()
    sent(r.gy, "hidden")
    around = [(dz, dy) for dz in (1, 3, 0, 2) for dy in (0, 1, 3, 2) if dz or dy]
    at = r.m_w.at[me.z, me.yl, me.yh]
    for dz, dy in around:
        copy_to(shifted(shifted(me, "z", dz), "y", dy), at, at, "merge").start()
    sent(r.m_y, "merge")
    send_back(r.cot_in, r.call.at[me.z], ("cot",))
    arrived(r.wl, "unit")
    for yh in range(2):
        pieces = [r.wl[half, yh, kind, :, 0:96] for kind in (1, 2, 0) for half in range(2)]
        r.wm[yh, me.x, me.c] = lanes(*pieces, jnp.zeros((48, 64), BF))

    plane_start(r.wm, "mixer")
    @pl.when(jnp.logical_not(here))
    def _():
        x_along(0)
        x_along(1)

    arrived(r.gy, "hidden")
    column_start()
    arrived(r.vr, "vec")

    def whole(row):
        return jnp.concatenate([r.vecs[s, row : row + 1, 0:96] for s in range(8)], axis=1)


    gain1, shift1 = whole(FIRST_GAIN), whole(FIRST_SHIFT)
    plane_hand(r.wm, "mixer")
    arrived(r.m_y, "merge")
    for yh in range(2):
        pieces = [r.m_w[s // 2, s % 2, yh, :, 0:96] for s in range(8)]
        r.mc[yh, me.x, me.c] = lanes(*pieces)
    plane_start(r.mc, "merge x")
    take_along("xall")
    arrived(r.call.at[0], "cot")
    send_own("call")
    for b in range(4):
        normed, rstd = norm_parts(r.xall[b].astype(F32))
        r.n1all[b] = normed
        r.rstd1[b] = jnp.broadcast_to(rstd, (TOK, TOK))
        first = normed * gain1 + shift1
        r.fall[b] = first.astype(BF)
        r.fallt[:, :, :, TOK * b : TOK * b + TOK] = turned(first.astype(BF)).reshape(8, 2, 48, TOK)
    plane_finish(r.wm, "mixer")

    at = r.fallt.at[:, 1 - me.c]
    copy_to(sib, at, r.fallt_sib, "first").start()
    sent(r.fallt_sib, "first")
    def mixer(at):
        return r.wm[:, :, :, :, at].reshape(D, -1)

    first = r.fall[...].reshape(4 * TOK, D)

    def mixer_bias(at, half):
        row = MIXER_BIAS + half
        return r.vecs[at, row : row + 1, 0:96]

    kv = nn(first, mixer(slice(0, 384)))
    keys = kv[:, 0:192].astype(BF)
    vbias = lanes(mixer_bias(4 + me.z, 0), mixer_bias(4 + me.z, 1))
    values = (kv[:, 192:384] + vbias).astype(BF)
    packed = lanes(keys, values[:, 128:192], values[:, 0:128])
    for b in range(4):
        r.kv_all[b, me.c] = packed[TOK * b : TOK * b + TOK]
    at = r.kv_all.at[:, me.c]
    copy_to(sib, at, at, "kv").start()
    sent(at, "kv")
    qbias = lanes(mixer_bias(me.z, 0), mixer_bias(me.z, 1))
    q = nn(first, mixer(slice(384, HEADS3)))[:, 0:192]
    q = (q + qbias).astype(BF) * jnp.asarray(0.125, BF)
    q = lanes(q, jnp.zeros((4 * TOK, 64), BF))
    for b in range(4):
        r.q_all[b] = q[TOK * b : TOK * b + TOK]
        r.kvt[:, tile(2 * b + me.c)] = turned(packed[TOK * b : TOK * b + TOK])
    arrived(r.segs.at[1], "seg")
    arrived(r.kv_all.at[:, 1 - me.c], "kv")
    for b in range(4):
        r.kvt[:, tile(2 * b + 1 - me.c)] = turned(r.kv_all[b, 1 - me.c])

    seg = jnp.where(here, r.segs[0], r.segs[1])

    def starts(bound):
        return jnp.sum(jnp.where(seg < bound, 1.0, 0.0), axis=(0, 1), keepdims=True).astype(jnp.int32)

    begin1, begin2 = starts(0.5), starts(1.5)
    lane = lax.broadcasted_iota(jnp.int32, (TOK, TOK), 1)

    def allowed_of(b):
        n = 256 * (b + 1)
        qpos = 256 * b + TOK * me.c + lax.broadcasted_iota(jnp.int32, (1, TOK), 1)
        low = jnp.where(qpos < begin1, 0, jnp.where(qpos < begin2, begin1, begin2))
        kpos = lax.broadcasted_iota(jnp.int32, (n, TOK), 0)
        return (kpos <= qpos) & (kpos >= low)

    def keys_of(b, h):
        at = slice(0, 128) if h < 2 else slice(128, 256)
        return r.kv_all[0 : b + 1, :, :, at].reshape(256 * (b + 1), TOK)

    def values_of(b, h):
        at = slice(256, 384) if h < 2 else slice(128, 256)
        return r.kv_all[0 : b + 1, :, :, at].reshape(256 * (b + 1), TOK)

    K_ROWS = (0, 64, 128)
    V_ROWS = (256, 320, 192)

    def one_head(v, upper):
        keep = lane >= 64 if upper else lane < 64
        return jnp.where(keep, v, jnp.zeros_like(v))

    def query_of(b, h):
        return one_head(r.q_all[b, :, 0:128] if h < 2 else r.q_all[b, :, 128:256], h == 1)

    spare = []
    for b in (3, 2, 1, 0):
        n = 256 * (b + 1)
        allowed = allowed_of(b)
        outs = []
        for h in range(3):
            scores = jnp.where(allowed, nt(keys_of(b, h), query_of(b, h)), NEG)
            top = jnp.max(scores, axis=0, keepdims=True)
            expo = jnp.exp(scores - top)
            total = jnp.sum(expo, axis=0, keepdims=True)
            r.lse[b, h : h + 1, :] = top + jnp.log(total)
            weights = (expo * (1.0 / total)).astype(BF)
            outs.append(nn(r.kvt[V_ROWS[h] : V_ROWS[h] + 64, 0:n], weights))
        r.att_all[me.z, b] = jnp.concatenate(outs[0:2], axis=0).T.astype(BF)
        spare.append(outs[2])
        ready = [b]
        if b % 2 == 0:
            r.att_all[me.z, 4 + b // 2] = jnp.concatenate([spare[-1], spare[-2]], axis=0).T.astype(BF)
            ready.append(4 + b // 2)
        for k in ready:
            for d in (1, 3, 2):
                at = r.att_all.at[me.z, k]
                copy_to(shifted(me, "z", d), at, at, "att", recv=("att", b // 2)).start()
        if b == 1:
            column_hand()
        if b == 0:
            plane_hand(r.mc, "merge x")
    sent(r.att_all.at[0:3], "att")
    take_along("call")
    for b in range(4):
        r.cott[:, TOK * b : TOK * b + TOK] = turned(r.call[b])
    plane_finish(r.mc, "merge x")
    merge = r.mc[...].reshape(D, D)

    column_finish()
    gain2, shift2, b_merge = whole(SECOND_GAIN), whole(SECOND_SHIFT), whole(MERGE_BIAS)

    def hidden(first):
        return lanes(*[r.wz[yl, :, :, :, :, first : first + SHARD].reshape(D, SHARD) for yl in range(2)])

    bias = lanes(*[r.vecs[2 * me.z + yl, EXPAND_BIAS + k : EXPAND_BIAS + k + 1] for yl in range(2) for k in range(3)])
    sums2 = []
    for pair in (1, 0):
        arrived(r.att_all.at[0:3, 0:3], "att", pair)
        rows = slice(2 * pair, 2 * pair + 2)
        for b in (2 * pair, 2 * pair + 1):
            at = slice(64 * (b % 2), 64 * (b % 2) + 64)
            r.att[b] = lanes(*[v for g in range(4) for v in (r.att_all[g, b], r.att_all[g, 4 + pair, :, at])])
        branch = nn(r.att[rows].reshape(2 * TOK, D), merge)
        middle = r.xall[rows].reshape(2 * TOK, D).astype(F32) + branch + b_merge
        r.mid[rows] = middle.reshape(2, TOK, D)
        n2, rstd2 = norm_parts(middle)
        second = (n2 * gain2 + shift2).astype(BF)
        r.second[rows] = second.reshape(2, TOK, D)
        pre = nn(second, hidden(0)) + bias
        square = pre * pre
        tanh = jnp.tanh(0.7978845608028654 * (pre + 0.044715 * square * pre))
        r.active[rows] = (0.5 * pre * (1.0 + tanh)).astype(BF).reshape(2, TOK, WIDE)
        slope = 0.5 * (1.0 + tanh) + 0.5 * pre * (1.0 - tanh * tanh) * (
            0.7978845608028654 * (1.0 + 0.134145 * square)
        )
        cot = r.call[rows]
        d_pre = (nn(cot.reshape(2 * TOK, D), hidden(SHARD)) * slope).astype(BF)
        r.dpre[rows] = d_pre.reshape(2, TOK, WIDE)
        d_second = nt(d_pre, hidden(0))
        sums2.append((col_sums(d_second * n2), col_sums(d_second)))
        d_middle = norm_back(d_second, gain2, n2, rstd2)
        d_branch = []
        for i in range(2):
            own = jnp.where(me.z == 2 * pair + i, cot[i].astype(F32), 0.0) + d_middle[TOK * i : TOK * i + TOK]
            r.dmid[2 * pair + i] = own
            d_branch.append(own.astype(BF))
            r.dbr[2 * pair + i] = d_branch[-1]
        d_att = nt(jnp.concatenate(d_branch, axis=0), merge).astype(BF)
        low, high = d_att[0:TOK], d_att[TOK : 2 * TOK]
        for z in range(4):
            at = 192 * z
            r.do_send[pair, z, 0] = low[:, at : at + 128]
            r.do_send[pair, z, 1] = high[:, at : at + 128]
            r.do_send[pair, z, 2] = lanes(low[:, at + 128 : at + 192], high[:, at + 128 : at + 192])
        for d in (1, 3, 2):
            to = shifted(me, "z", d)
            copy_to(to, r.do_send.at[pair, to.z], r.do_recv.at[pair, me.z], "do", recv=("do", pair)).start()
        r.do_recv[pair, me.z] = r.do_send[pair, me.z]
    sent(r.do_send.at[:, 0:3], "do")

    zeros = jnp.zeros((TOK, 32), BF)

    for b in range(4):
        r.attt[:, TOK * b : TOK * b + TOK] = turned(r.att[b])
    grad = nn(r.attt[...], r.dbr[...].reshape(4 * TOK, D)).astype(BF)
    r.m_g[...] = grad.reshape(2, 4, 2, 48, D)
    copy_to(sib, r.m_g.at[:, :, 1 - me.c], r.m_r0, "merge", "pair").start()
    sent(r.m_r0, "merge", "pair")

    sums = col_sums(r.dpre[...].reshape(4 * TOK, WIDE))
    r.vg[...] = jnp.zeros((8, 16, TOK), F32)
    for yl in range(2):
        for k in range(3):
            at = TOK * (3 * yl + k)
            r.vg[2 * me.z + yl, EXPAND_BIAS + k : EXPAND_BIAS + k + 1, :] = sums[:, at : at + TOK]
    for b in range(4):
        r.secondt[:, TOK * b : TOK * b + TOK] = turned(r.second[b])
    halves = ((r.g_e, r.g_e0), (r.g_s, r.g_s0))

    def hidden_gradient(k, left, right):
        ref, pair0 = halves[k]
        grad = nn(left[...], right[...].reshape(4 * TOK, WIDE)).astype(BF)
        for yl in range(2):
            ref[yl] = grad[:, SHARD * yl : SHARD * yl + SHARD].reshape(2, 4, 2, 48, SHARD)
        copy_to(sib, ref.at[:, :, :, 1 - me.c], pair0, "hidden", k, "pair").start()
        sent(pair0, "hidden", k, "pair")

    hidden_gradient(0, r.secondt, r.dpre)

    hidden_gradient(1, r.cott, r.active)
    result = nt(r.active[...].reshape(4 * TOK, WIDE), hidden(SHARD)).astype(BF)
    for b in range(4):
        r.res_send[b] = result[TOK * b : TOK * b + TOK]
    send_along("res_recv", lambda z: r.res_send.at[z])
    r.res_recv[me.z] = r.res_send[me.z]

    def pair_sum(ref, own, key):
        arrived(ref, *key, "pair")
        every = (slice(None),) * (len(ref.shape) - 2)
        ref[...] = (ref[...].astype(F32) + own[every + (me.c,)].astype(F32)).astype(BF)

    def plane_send(ref, got, key):
        every = (slice(None),) * (len(ref.shape) - 3)
        for d in (1, 3, 2):
            to = shifted(me, "x", d)
            copy_to(to, ref.at[every + (to.x,)], got.at[d - 1], key, "sum").start()
        sent(got, key, "sum")

    def plane_total(ref, got, key):
        arrived(got, key, "sum")
        total = ref[(slice(None),) * (len(ref.shape) - 3) + (me.x,)].astype(F32)
        for d in range(3):
            total += got[d].astype(F32)
        return total.astype(BF)

    def expand_sum():
        pair_sum(r.g_e0, r.g_e, ("hidden", 0))
        for d in (1, 3, 2):
            to = shifted(me, "y", d)
            copy_to(to, r.g_e0.at[to.yl, to.yh], r.g_y.at[d - 1], "expand y").start()
        sent(r.g_y, "expand y")

    def expand_next():
        arrived(r.g_y, "expand y")
        total = r.g_e0[me.yl, me.yh].astype(F32)
        for d in range(3):
            total += r.g_y[d].astype(F32)
        r.g_ex[...] = total.astype(BF)
        for d in (1, 3, 2):
            to = shifted(me, "x", d)
            copy_to(to, r.g_ex.at[to.x], r.g_got.at[0, d - 1], "expand x").start()
        sent(r.g_got.at[0], "expand x")

    def shrink_sum():
        pair_sum(r.g_s0, r.g_s, ("hidden", 1))
        plane_send(r.g_s0, r.g_x, "shrink")

    def shrink_next():
        r.g_sy[...] = plane_total(r.g_s0, r.g_x, "shrink")
        for d in (1, 3, 2):
            to = shifted(me, "y", d)
            copy_to(to, r.g_sy.at[to.yl, to.yh], r.g_got.at[1, d - 1], "shrink y").start()
        sent(r.g_got.at[1], "shrink y")

    def merge_next():
        total = plane_total(r.m_r0, r.m_x, "merge")
        for s in range(8):
            for yh in range(2):
                r.m_t[s // 2, s % 2, yh] = lanes(total[yh, :, 96 * s : 96 * s + 96], zero32)
        for i, (dz, dy) in enumerate(around):
            to = shifted(shifted(me, "z", dz), "y", dy)
            copy_to(to, r.m_t.at[to.z, to.yl, to.yh], r.m_y.at[i], "merge all").start()
        sent(r.m_y, "merge all")

    pair_sum(r.m_r0, r.m_g, ("merge",))
    plane_send(r.m_r0, r.m_x, "merge")
    expand_sum()
    r.dkv[...] = jnp.zeros((8 * TOK, SHARD), F32)
    sent(r.dkv_got, "dkv")

    def take_pair(p):
        arrived(r.do_recv.at[p, 0:3], "do", p)
        total = r.do_recv[p, 0].astype(F32)
        for z in range(1, 4):
            total += r.do_recv[p, z].astype(F32)
        r.do_all[2 * p, :, 0:TOK] = total[0].astype(BF)
        r.do_all[2 * p, :, TOK : 2 * TOK] = lanes(total[2, :, 64:128], total[2, :, 0:64]).astype(BF)
        r.do_all[2 * p + 1, :, 0:TOK] = total[1].astype(BF)
        r.do_all[2 * p + 1, :, TOK : 2 * TOK] = total[2].astype(BF)

    def pair(l0, l1, r0, r1):
        return nn(jnp.concatenate([l0, l1], axis=1), jnp.concatenate([r0, r1], axis=0))

    gain_sum, shift_sum = [], []

    def finish_block(b):
        arrived(r.dkv_got.at[b], "dkv", b)
        own = pl.multiple_of(256 * b + TOK * me.c, TOK)
        dkv = (r.dkv[pl.ds(own, TOK), :] + r.dkv_got[b].astype(F32)).astype(BF)
        dq = r.dq[b]
        r.dpad[b] = lanes(dkv[:, 0:192], dkv[:, 256:384], dkv[:, 192:256], dq[:, 0:192], jnp.zeros((TOK, 64), BF))
        at = r.dpad.at[b]
        copy_to(sib, at, r.dpad_sib.at[b], "dpad").start()

    def first_back(blocks):
        rows = jnp.concatenate([r.dpad[b] for b in blocks], axis=0)
        d_first = nt(rows, mixer(slice(0, HEADS3)))
        for i, b in enumerate(blocks):
            part, normed = d_first[TOK * i : TOK * i + TOK], r.n1all[b]
            gain_sum.append(col_sums(part * normed))
            shift_sum.append(col_sums(part))
            r.df_send[b] = (r.dmid[b] + norm_back(part, gain1, normed, r.rstd1[b][:, 0:1])).astype(BF)

    for b in (3, 2, 1, 0):
        if b % 2:
            take_pair(b // 2)
        n = 256 * (b + 1)
        allowed = allowed_of(b)
        dqs, dss, pbs, dos, qs = [], [], [], [], []
        for h in range(3):
            q = query_of(b, h)
            do = one_head(r.do_all[b, :, 0:128] if h < 2 else r.do_all[b, :, 128:256], h > 0)
            scores = jnp.where(allowed, nt(keys_of(b, h), q), NEG)
            probs = jnp.exp(scores - r.lse[b, h : h + 1, :])
            dw = nt(values_of(b, h), do)
            centre = jnp.sum(probs * dw, axis=0, keepdims=True)
            ds = (probs * (dw - centre)).astype(BF)
            dqs.append(nn(r.kvt[K_ROWS[h] : K_ROWS[h] + 64, 0:n], ds))
            dss.append(ds)
            pbs.append(probs.astype(BF))
            dos.append(do)
            qs.append(q)
        dqs.append(jnp.zeros((64, TOK), F32))
        r.dq[b] = (jnp.concatenate(dqs, axis=0) * 0.125).T.astype(BF)
        r.dkv[0:n, 0:128] += pair(dss[0], dss[1], qs[0], qs[1])
        r.dkv[0:n, 128:256] += pair(dss[2], pbs[2], qs[2], dos[2])
        r.dkv[0:n, 256:384] += pair(pbs[0], pbs[1], dos[0], dos[1])
        other = pl.multiple_of(256 * b + TOK * (1 - me.c), TOK)
        r.dkv_sib[b] = r.dkv[pl.ds(other, TOK), :].astype(BF)
        copy_to(sib, r.dkv_sib.at[b], r.dkv_got.at[b], "dkv", recv=("dkv", b)).start()
        if b == 3:
            shrink_sum()
        if b in (2, 1):
            finish_block(b + 1)
    finish_block(1)
    first_back((3, 1))
    finish_block(0)
    first_back((2, 0))
    g_gain_b, g_shift_b = sums2[0][0] + sums2[1][0], sums2[0][1] + sums2[1][1]
    g_b_shrink = col_sums(r.call[me.z])
    g_b_merge = col_sums(r.dbr[...].reshape(4 * TOK, D))
    rows = [(MERGE_BIAS, g_b_merge), (SECOND_GAIN, g_gain_b), (SECOND_SHIFT, g_shift_b), (SHRINK_BIAS, g_b_shrink)]
    for s in range(8):
        for row, value in rows:
            r.vg[s, row : row + 1, 0:96] = value[:, 96 * s : 96 * s + 96]

    arrived(r.fallt_sib, "first")
    sums = col_sums(r.dpad[...].reshape(4 * TOK, HEADS3))
    for half in range(2):
        row = MIXER_BIAS + half
        r.vg[me.z, row : row + 1, 0:96] = sums[:, 384 + 96 * half : 480 + 96 * half]
        r.vg[4 + me.z, row : row + 1, 0:96] = sums[:, 192 + 96 * half : 288 + 96 * half]
    gain_a, shift_a = sum(gain_sum), sum(shift_sum)
    for s in range(8):
        r.vg[s, FIRST_GAIN : FIRST_GAIN + 1, 0:96] = gain_a[:, 96 * s : 96 * s + 96]
        r.vg[s, FIRST_SHIFT : FIRST_SHIFT + 1, 0:96] = shift_a[:, 96 * s : 96 * s + 96]

    for k in range(1, 8):
        to = seq_peer(k)
        copy_to(to, r.vg.at[to.z * 2 + to.yl], r.vr.at[k - 1], "rows").start()
    sent(r.vr, "rows")
    for d in (1, 3):
        to = shifted(me, "z", d)
        copy_to(to, r.df_send.at[to.z], r.df_recv.at[me.z], "near").start()
    sent(r.df_recv.at[0:2], "near")
    to = shifted(swap, "z", 2)
    copy_to(to, r.df_send.at[to.z], r.gin_far, "far").start()
    sent(r.gin_far, "far")

    arrived(r.dpad_sib, "dpad")
    sent(r.dpad, "dpad")
    left = jnp.concatenate([r.fallt[:, me.c].reshape(D // 2, 4 * TOK), r.fallt_sib[...].reshape(D // 2, 4 * TOK)], axis=1)
    right = jnp.concatenate([ref[...].reshape(4 * TOK, HEADS3) for ref in (r.dpad, r.dpad_sib)], axis=0)
    r.rm0[...] = nn(left, right).astype(BF).reshape(2, 4, 48, HEADS3)
    plane_send(r.rm0, r.rmx, "mixer")
    take_along("res_recv")
    result = r.mid[me.z] + whole(SHRINK_BIAS)
    for b in range(4):
        result += r.res_recv[b].astype(F32)
    r.hid[...] = result.astype(BF)
    send_back(r.hid, r.hid_recv, ("hid",))
    arrived(r.vr, "rows")
    total = r.vg[seq]
    for k in range(7):
        total += r.vr[k]
    ours = me.yh * 8 + me.x * 2 + me.c
    r.vx[ours] = total
    others = [(at, dx, dy) for at in (me, sib) for dx in range(4) for dy in (0, 2) if dx or dy or at is sib]
    for at, dx, dy in others:
        copy_to(shifted(shifted(at, "x", dx), "y", dy), r.vx.at[ours], r.vx.at[ours], "rows all").start()
    sent(r.vx.at[0:15], "rows all")
    expand_next()
    merge_next()
    shrink_next()
    total = plane_total(r.rm0, r.rmx, "mixer")
    for half in range(2):
        for yh in range(2):
            for kind in range(3):
                at = (384, 0, 192)[kind] + 96 * half
                r.rmy[half, yh, kind] = lanes(total[yh, :, at : at + 96], zero32)
    for dyh in range(2):
        yh = lax.rem(me.yh + dyh, 2)
        for half in range(2):
            for kind in range(3):
                u = 8 * kind + 2 * me.z + half
                owner = lax.div(u, 3)
                to = moved(me, yh=yh, z=lax.div(owner, 2), yl=lax.rem(owner, 2))
                src = r.rmy.at[half, yh, kind]
                dst = r.rmf.at[lax.rem(u, 3), ypos]
                if dyh:
                    copy_to(to, src, dst, "piece").start()
                else:
                    start_unless(owner == seq, to, src, dst, "piece", half, kind, recv=("piece",))
                    sent_unless(owner == seq, r.units.at[0], "piece", half, kind)
    sent(r.rmf.at[:, 0:2], "piece")
    arrived(r.df_recv.at[0:2], "near")
    parts = [r.df_send[me.z]] + [r.df_recv[shifted(me, "z", d).z] for d in (1, 3)]
    r.gin_send[...] = sum(part.astype(F32) for part in parts).astype(BF)
    send_back(r.gin_send, r.gin_recv, ("gin",))

    arrived(r.hid_recv, "hid")
    r.hidden[...] = r.hid_recv[...]
    arrived(r.g_got.at[0], "expand x")
    r.gexp[...] = r.g_ex[me.x].astype(F32) + sum(r.g_got[0, d].astype(F32) for d in range(3))
    arrived(r.g_got.at[1], "shrink y")
    r.gshr[...] = r.g_sy[me.yl, me.yh].astype(F32) + sum(r.g_got[1, d].astype(F32) for d in range(3))
    arrived(r.m_y, "merge all")
    total = r.m_t[me.z, me.yl, me.yh].astype(F32)
    for i in range(15):
        total += r.m_y[i].astype(F32)
    r.gmerge[...] = total[:, 0:96]
    arrived(r.gin_recv, "gin")
    arrived(r.gin_far, "far")
    r.gin[...] = r.gin_recv[...].astype(F32) + r.gin_far[...].astype(F32)
    arrived(r.vx.at[0:15], "rows all")
    total = r.vx[0]
    for k in range(1, 16):
        total += r.vx[k]
    r.vout[...] = total
    arrived(r.rmf, "piece")
    for i in range(3):
        total = jnp.zeros((48, TOK), F32)
        for y in range(4):
            total += r.rmf[i, y].astype(F32)
        r.gmix[:, 96 * i : 96 * i + 96] = total[:, 0:96]
    for finish in pending:
        finish()
    if (len(sends), len(recvs)) != (SENDS, RECVS):
        raise ValueError((len(sends), len(recvs)))


def scratches():
    v, dma = pltpu.VMEM, pltpu.SemaphoreType.DMA
    blocks = (2, 4, 2, 48)
    s = dict(
        m_w=v((4, 2, 2, 48, TOK), BF),
        m_g=v(blocks + (D,), BF),
        m_r0=v((2, 4, 48, D), BF),
        m_x=v((3, 2, 48, D), BF),
        m_t=v((4, 2, 2, 48, TOK), BF),
        m_y=v((15, 48, TOK), BF),
        mc=v(blocks + (D,), BF),
        wz=v((2,) + blocks + (WIDE,), BF),
        g_e=v((2,) + blocks + (SHARD,), BF),
        g_s=v((2,) + blocks + (SHARD,), BF),
        g_e0=v((2, 2, 4, 48, SHARD), BF),
        g_s0=v((2, 2, 4, 48, SHARD), BF),
        g_y=v((3, 4, 48, SHARD), BF),
        g_x=v((3, 2, 2, 48, SHARD), BF),
        g_ex=v((4, 48, SHARD), BF),
        g_sy=v((2, 2, 48, SHARD), BF),
        g_got=v((2, 3, 48, SHARD), BF),
        gy=v((3, 48, WIDE), BF),
        units=v((3, 48, TOK), BF),
        wl=v((2, 2, 3, 48, TOK), BF),
        wm=v(blocks + (HEADS3,), BF),
        rm0=v((2, 4, 48, HEADS3), BF),
        rmx=v((3, 2, 48, HEADS3), BF),
        rmy=v((2, 2, 3, 48, TOK), BF),
        rmf=v((3, 4, 48, TOK), BF),
        vecs=v((8, 16, TOK), F32),
        segs=v((2, 8, TOK), F32),
        fallt=v((8, 2, 48, 4 * TOK), BF),
        fallt_sib=v((8, 48, 4 * TOK), BF),
        cott=v((D, 4 * TOK), BF),
        secondt=v((D, 4 * TOK), BF),
        attt=v((D, 4 * TOK), BF),
        rstd1=v((4, TOK, TOK), F32),
        dmid=v((4, TOK, D), F32),
        q_all=v((4, TOK, 256), BF),
        kv_all=v((4, 2, TOK, SHARD), BF),
        kvt=v((SHARD, 8 * TOK), BF),
        lse=v((4, 8, TOK), F32),
        att_all=v((4, 6, TOK, TOK), BF),
        dkv=v((8 * TOK, SHARD), F32),
        dkv_sib=v((4, TOK, SHARD), BF),
        dkv_got=v((4, TOK, SHARD), BF),
        dq=v((4, TOK, 256), BF),
        dpad=v((4, TOK, HEADS3), BF),
        dpad_sib=v((4, TOK, HEADS3), BF),
        do_send=v((2, 4, 3, TOK, TOK), BF),
        do_recv=v((2, 4, 3, TOK, TOK), BF),
        do_all=v((4, TOK, 256), BF),
        n1all=v((4, TOK, D), F32),
        mid=v((4, TOK, D), F32),
    )
    for name in ("xall", "call", "fall", "att", "second", "dbr", "res_send", "res_recv", "df_send", "df_recv"):
        s[name] = v((4, TOK, D), BF)
    for name in ("active", "dpre"):
        s[name] = v((4, TOK, WIDE), BF)
    for name in ("hid", "hid_recv", "gin_send", "gin_recv", "gin_far"):
        s[name] = v((TOK, D), BF)
    for name, count in (("vg", 8), ("vr", 7), ("vx", 16)):
        s[name] = v((count, 16, TOK), F32)
    s["send"], s["recv"] = dma((SENDS,)), dma((RECVS,))
    return s


def finish(hidden, gin, gmix, gmerge, gexp, gshr, vout, *outs):
    for ref, out in zip((hidden, gin, gmix, gmerge, gexp, gshr), outs[:6], strict=True):
        out[...] = ref[...]
    v = vout[...]
    rows = (FIRST_GAIN, FIRST_SHIFT, MERGE_BIAS, SECOND_GAIN, SECOND_SHIFT, SHRINK_BIAS)
    for row, out in zip(rows, outs[6:12], strict=True):
        out[...] = v[row : row + 1, 0:96].reshape(96)
    outs[12][...] = lanes(v[MIXER_BIAS : MIXER_BIAS + 1, 0:96], v[MIXER_BIAS + 1 : MIXER_BIAS + 2, 0:96]).reshape(192)
    outs[13][...] = lanes(*[v[EXPAND_BIAS + k : EXPAND_BIAS + k + 1] for k in range(3)]).reshape(SHARD)


def body(
    residual_in, cotangent, segments, first_gain, first_shift, mixer_weight, mixer_bias, merge_weight, merge_bias,
    second_gain, second_shift, expand_weight, expand_bias, shrink_weight, shrink_bias,
):
    vmem = pl.BlockSpec(memory_space=pltpu.VMEM)
    scratch = scratches()
    shapes = [((TOK, D), BF), ((TOK, D), F32), ((48, 288), F32), ((48, 96), F32), ((48, SHARD), F32), ((48, SHARD), F32)]
    held = [jax.ShapeDtypeStruct(*s) for s in shapes]
    parts = pl.pallas_call(
        functools.partial(kernel, IN + OUT + tuple(scratch)),
        out_shape=held + [jax.ShapeDtypeStruct((16, TOK), F32)],
        in_specs=[vmem] * len(IN),
        out_specs=[vmem] * len(OUT),
        scratch_shapes=list(scratch.values()),
        compiler_params=pltpu.CompilerParams(
            collective_id=0, has_side_effects=True, vmem_limit_bytes=62 * 1024 * 1024
        ),
    )(
        residual_in[0], cotangent[0], segments.reshape(8, TOK), mixer_weight, merge_weight, expand_weight,
        shrink_weight.T, first_gain, first_shift, mixer_bias, merge_bias, second_gain, second_shift, expand_bias,
        shrink_bias,
    )
    vectors = [jax.ShapeDtypeStruct((n,), F32) for n in (96, 96, 96, 96, 96, 96, 192, SHARD)]
    hidden, gin, gmix, gmerge, gexp, gshr, fg, fs, mb, sg, ss, sb, xb, eb = pl.pallas_call(
        finish, out_shape=held + vectors, in_specs=[vmem] * 7, out_specs=[vmem] * 14
    )(*parts)
    return hidden[None], gin[None], fg, fs, gmix, xb, gmerge, mb, sg, ss, gexp, eb, gshr.T, sb


def solution(mesh):
    vector, matrix = P("seq"), P("dp", "seq")
    tokens = P("dp", "seq", None)
    return jax.shard_map(
        body,
        mesh=mesh,
        in_specs=(
            tokens, tokens, P("dp", None), vector, vector, matrix, vector, matrix, vector, vector, vector, matrix, vector,
            P("seq", "dp"), vector,
        ),
        out_specs=(
            tokens, tokens, vector, vector, matrix, vector, matrix, vector, vector, vector, matrix, vector,
            P("seq", "dp"), vector,
        ),
        check_vma=False,
    )
```
